32 devices in a mesh: dp: 4 (over x, core), expert: 8 (over z, y).
Axes of the slice: x: 2, y: 2, z: 4, core: 2. Of those that a mesh axis runs over, the one named last changes fastest.
Arguments:
- inputs: bfloat16 [32, 1024, 768], P(('dp', 'expert')), may hold values from -9 to 9
- cotangent: bfloat16 [32, 1024, 768], P(('dp', 'expert')), may hold values from -6 to 6
- attn_gain: bfloat16 [768], P(('dp', 'expert')), may hold values from 0.25 to 1.75
- qkv_weight: bfloat16 [768, 2304], P(('dp', 'expert')), may hold values from -0.21875 to 0.21875
- out_weight: bfloat16 [768, 768], P(('dp', 'expert')), may hold values from -0.875 to 0.875
- ffn_gain: bfloat16 [768], P(('dp', 'expert')), may hold values from 0.25 to 1.75
- router_weight: bfloat16 [768, 8], P(('dp', 'expert')), may hold values from -0.15625 to 0.15625
- rel_bias: float32 [32, 12], replicated, may hold values from -4 to 4
- expert_in: bfloat16 [8, 768, 3072], P('expert'), may hold values from -0.21875 to 0.21875
- expert_out: bfloat16 [8, 3072, 768], P('expert'), may hold values from -1.25 to 1.25
- routes: int32 [32, 1024], P(('dp', 'expert')), may hold values from 0 to 7
- positions: int32 [32, 1024], P(('dp', 'expert')), may hold values from 0 to 160, as said below
- dropped: int32 [32, 1024], P(('dp', 'expert')), may hold values from 0 to 1, as said below
- segment_ids: int32 [32, 1024], P(('dp', 'expert')), may hold values from 0 to 7, never falling along the last dimension, each value on 1 to 512 neighbouring positions
- valid_mask: int32 [32, 1024], P(('dp', 'expert')), may hold values from 0 to 1, as said below
- buckets: int32 [2047], replicated, may hold values from 0 to 31
Outputs:
- output: bfloat16 [32, 1024, 768], P(('dp', 'expert'))
- input_grad: float32 [32, 1024, 768], P(('dp', 'expert'))
- grad_attn_gain: float32 [768], P(('dp', 'expert'))
- grad_qkv_weight: float32 [768, 2304], P(('dp', 'expert'))
- grad_out_weight: float32 [768, 768], P(('dp', 'expert'))
- grad_ffn_gain: float32 [768], P(('dp', 'expert'))
- grad_router_weight: float32 [768, 8], P(('dp', 'expert'))
- grad_rel_bias: float32 [32, 12], replicated
- grad_expert_in: float32 [8, 768, 3072], P('expert', None, 'dp')
- grad_expert_out: float32 [8, 3072, 768], P('expert', 'dp')
- stats: float32 [3], replicated
The draws below stay inside these ranges and needn't reach their ends.
Inputs may be any that keep to these rules, and one draw needn't show every extreme that they name: `positions`: A kept token's position is its rank among the tokens of its aligned group of 1024 tokens that name the same expert, so no two kept tokens of a group share expert and position; a token beyond the capacity has position 160. dropped is 1 exactly where positions is 160. `valid_mask`: the first token of every sequence is real.
All inputs are finite; a program needn't handle non-finite values.
Results may differ from the reference program's by a relative error of at most 0.015.
Values may be sent and summed in bfloat16 or wider, within the bound.
No kernel may reach another device: no remote copies, remote signals or barrier semaphores. Data moves between devices by JAX's collectives and lax.ppermute only.
A program may use at most 320 MiB of HBM per device.

```python
import math
import jax
import jax.numpy as jnp
import numpy as np
from jax import lax

D = 768
HEADS = 12
HEAD_DIM = 64
FF = 3072
NB = 32
LEN = 1024
SEGS = 8
SEQS_DEV = 1
SEQS = 32
EXPERTS = 8
CAP = 160


def draw_inputs(key, part):
    ladder = jnp.arange(SEQS, dtype=jnp.float32) / max(SEQS - 1, 1)
    sample = jnp.clip(jax.random.normal(jax.random.fold_in(key, 6), (SEQS, LEN, D), jnp.float32), -4.5, 4.5)
    spread = 0.5 + 1.5 * ladder
    return (sample * spread[:, None, None]).astype(jnp.bfloat16)


def draw_buckets(key, part):
    anchors = jnp.array([11, 16, 23, 32, 45, 64, 91], jnp.int32)
    jitter = jax.random.randint(jax.random.fold_in(key, 3), (7,), 0, 1 + anchors // 4)
    bounds = anchors + jitter
    offset = jnp.arange(2 * LEN - 1, dtype=jnp.int32) - (LEN - 1)
    distance = jnp.abs(offset)
    distant = 8 + jnp.sum((distance[:, None] >= bounds[None, :]).astype(jnp.int32), axis=1)
    magnitude = jnp.where(distance < 8, distance, distant)
    return (magnitude + jnp.where(offset > 0, NB // 2, 0)).astype(jnp.int32)


def draw_valid_mask(key, part):
    dice_roll = jax.random.randint(jax.random.fold_in(key, 4), (SEQS, LEN), 0, 8)
    seq_at = jnp.arange(SEQS, dtype=jnp.int32)
    keep_len = LEN - 2 * LEN // 3 * seq_at // max(SEQS - 1, 1)
    places = jnp.arange(LEN, dtype=jnp.int32)[None, :]
    leading = places == 0
    inside = places < keep_len[:, None]
    return jnp.where((dice_roll != 0) & inside | leading, 1, 0).astype(jnp.int32)


def routing_tables(key):
    group_rows = SEQS_DEV * LEN
    group_count = SEQS // SEQS_DEV
    popularity = np.floor(1000.0 * (np.arange(EXPERTS) + 1.0) ** (-0.6)).astype(np.int64)
    boundary = jnp.asarray(np.cumsum(popularity), dtype=jnp.int32)
    seeded = jax.random.fold_in(key, 77)
    ticket = jax.random.randint(jax.random.fold_in(seeded, 1), (group_count, group_rows), 0, int(np.sum(popularity)))
    ranking = jnp.searchsorted(boundary, ticket, side='right').astype(jnp.int32)
    relabel = jax.random.permutation(jax.random.fold_in(seeded, 2), EXPERTS).astype(jnp.int32)
    route_ids = relabel[ranking]
    priority = jax.random.permutation(jax.random.fold_in(seeded, 3), group_count * group_rows).astype(jnp.int32).reshape(group_count, group_rows)
    sort_score = route_ids * (group_count * group_rows) + priority
    sorted_at = jnp.argsort(sort_score, axis=1, stable=True).astype(jnp.int32)
    sorted_routes = jnp.take_along_axis(route_ids, sorted_at, axis=1)
    expert_ids = jnp.arange(EXPERTS, dtype=jnp.int32)
    loads = jnp.sum((route_ids[:, :, None] == expert_ids[None, None, :]).astype(jnp.int32), axis=1)
    first_at = jnp.cumsum(loads, axis=1) - loads
    sorted_rank = jnp.arange(group_rows, dtype=jnp.int32)[None, :] - jnp.take_along_axis(first_at, sorted_routes, axis=1)
    inverse = jnp.argsort(sorted_at, axis=1, stable=True)
    slot_rank = jnp.minimum(jnp.take_along_axis(sorted_rank, inverse, axis=1), CAP).astype(jnp.int32)
    return (route_ids.reshape(SEQS, LEN), slot_rank.reshape(SEQS, LEN), (slot_rank >= CAP).astype(jnp.int32).reshape(SEQS, LEN))


def draw_routes(key, part):
    return routing_tables(key)[0]


def draw_positions(key, part):
    return routing_tables(key)[1]


def draw_dropped(key, part):
    return routing_tables(key)[2]


def block_levels(stream_key, dims, shards, least, top_value):
    level = 1.0
    for axis_at, shards_of in shards:
        heights = jax.random.uniform(jax.random.fold_in(jax.random.fold_in(stream_key, 6), axis_at), (shards_of,), jnp.float32, least / len(shards), top_value / len(shards))
        level = level * jnp.repeat(jnp.exp(heights), dims[axis_at] // shards_of).reshape((-1,) + (1,) * (len(dims) - 1 - axis_at))
    return level


def split_up(number_of, total, reach, skew):
    weights = [(1 << 20) // math.isqrt(grade ** skew) + 1 for grade in range(2, number_of + 1)]
    spare, counts = total - reach - (number_of - 1), [1] * (number_of - 1)
    while spare > 0:
        candidates = [i for i in range(number_of - 1) if counts[i] < reach]
        pool, left = sum([weights[i] for i in candidates]), spare
        for i in candidates:
            extra = min(reach - counts[i], max(1, left * weights[i] // pool), spare)
            counts[i] = counts[i] + extra
            spare = spare - extra
    return np.array([reach] + counts)


def uneven_parts(rng, number_of, total, limit, slope):
    if number_of == 2:
        one = jax.random.randint(rng, (), max(1, total - limit), min(limit, total - 1) + 1)
        return jnp.stack([one, total - one])
    tallies = jnp.asarray(split_up(number_of, total, limit, slope), jnp.int32)
    twos = (number_of - 1) // 2
    donor, taker = tallies[1:1 + 2 * twos:2], tallies[2:2 + 2 * twos:2]
    margin = jnp.minimum(donor - 1, limit - taker)
    moved = jax.random.randint(jax.random.fold_in(rng, 1), (twos,), 0, 1 << 20) % (margin + 1)
    tallies = tallies.at[1:1 + 2 * twos:2].set(donor - moved).at[2:2 + 2 * twos:2].set(taker + moved)
    return tallies[jax.random.permutation(jax.random.fold_in(rng, 2), number_of)]


def noise(own_key, dims, deviation, bound, shards=(), kind=jnp.bfloat16):
    values = deviation * jax.random.normal(own_key, dims, jnp.float32)
    if shards:
        values = values * block_levels(own_key, dims, shards, -0.22, 0.18)
    return jnp.clip(values, -bound, bound).astype(kind)


def setup_inputs(seed: int = 0) -> dict:
    seeds = jax.random.split(jax.random.key(seed), 17)
    inputs = draw_inputs(jax.random.fold_in(seeds[16], 71), 0)
    cotangent = noise(seeds[1], (SEQS, LEN, D), 1.0, 6.0, ((0, 32),))
    attn_gain = jnp.clip(1.0 + 0.15 * jax.random.normal(seeds[2], (D,), jnp.float32), 0.25, 1.75).astype(jnp.bfloat16)
    qkv_weight = noise(seeds[3], (D, 3 * D), D ** -0.5, 0.21875, ((0, 32),))
    out_weight = noise(seeds[4], (D, D), (D // 16) ** -0.5, 0.875, ((0, 32),))
    ffn_gain = jnp.clip(1.0 + 0.15 * jax.random.normal(seeds[5], (D,), jnp.float32), 0.25, 1.75).astype(jnp.bfloat16)
    router_weight = noise(seeds[6], (D, EXPERTS), (2 * D) ** -0.5, 0.15625, ((0, 32),))
    rel_bias = noise(seeds[7], (NB, HEADS), 1.0, 4.0, (), jnp.float32)
    expert_in = noise(seeds[8], (EXPERTS, D, FF), D ** -0.5, 0.21875, ((0, 8),))
    expert_out = noise(seeds[9], (EXPERTS, FF, D), (max(1, FF // (2 * EXPERTS * EXPERTS))) ** -0.5, 1.25, ((0, 8),))
    routes = draw_routes(jax.random.fold_in(seeds[16], 71), 0)
    positions = draw_positions(jax.random.fold_in(seeds[16], 71), 0)
    dropped = draw_dropped(jax.random.fold_in(seeds[16], 71), 0)
    segment_ids = jax.vmap(lambda own: jnp.searchsorted(jnp.cumsum(uneven_parts(own, SEGS, LEN, LEN // 2, 2)), jnp.arange(LEN), side="right"))(jax.random.split(seeds[13], SEQS)).reshape((SEQS, LEN)).astype(jnp.int32)
    valid_mask = draw_valid_mask(jax.random.fold_in(seeds[16], 71), 0)
    buckets = draw_buckets(jax.random.fold_in(seeds[16], 71), 0)
    return {"inputs": inputs, "cotangent": cotangent, "attn_gain": attn_gain, "qkv_weight": qkv_weight, "out_weight": out_weight, "ffn_gain": ffn_gain, "router_weight": router_weight, "rel_bias": rel_bias, "expert_in": expert_in, "expert_out": expert_out, "routes": routes, "positions": positions, "dropped": dropped, "segment_ids": segment_ids, "valid_mask": valid_mask, "buckets": buckets}


@jax.custom_vjp
def low(v):
    return lax.optimization_barrier(v.astype(jnp.bfloat16)).astype(jnp.float32)

@jax.custom_vjp
def low_back(v):
    return v

def low_keep(v):
    return (low(v), None)

def low_pass(kept, grad):
    return (grad,)

def back_keep(v):
    return (v, None)

def back_low(kept, grad):
    return (low(grad),)
low.defvjp(low_keep, low_pass)
low_back.defvjp(back_keep, back_low)
HIGHEST = lax.Precision.HIGHEST
EPSILON = 1e-06
MASKED = -1e+30

def matmul(left, right):
    return jnp.dot(left, right, precision=HIGHEST, preferred_element_type=jnp.float32)

def rms_norm(values, norm_gain):
    factor = lax.rsqrt(lax.optimization_barrier(jnp.mean(values * values, axis=-1, keepdims=True)) + EPSILON)
    return values * factor * norm_gain

def smooth_unit(values):
    return jax.nn.gelu(values, approximate=True)

def attention_block(layer_seq, segments, validity, bias_heads, norm_gain, w_qkv, w_out):
    normed = low(rms_norm(layer_seq, norm_gain))
    packed = low_back(low(matmul(normed, w_qkv)))
    queries = packed[:, :D].reshape(LEN, HEADS, HEAD_DIM)
    keys_all = packed[:, D:2 * D].reshape(LEN, HEADS, HEAD_DIM)
    values_all = packed[:, 2 * D:].reshape(LEN, HEADS, HEAD_DIM)
    raw_scores = jnp.einsum('qhd,khd->hqk', queries, keys_all, precision=HIGHEST) * HEAD_DIM ** (-0.5) + bias_heads
    places = jnp.arange(LEN, dtype=jnp.int32)
    allowed = (segments[:, None] == segments[None, :]) & (validity[None, :] == 1) | (places[:, None] == places[None, :])
    scores = low_back(jnp.where(allowed[None], raw_scores, MASKED))
    weights = low(jax.nn.softmax(scores, axis=-1))
    mixed = jnp.einsum('hqk,khd->qhd', weights, values_all, precision=HIGHEST).reshape(LEN, D)
    mixed = low_back(low(mixed))
    return low_back(matmul(mixed, w_out))

def reference(inputs, cotangent, attn_gain, qkv_weight, out_weight, ffn_gain, router_weight, rel_bias, expert_in, expert_out, routes, positions, dropped, segment_ids, valid_mask, buckets):
    tokens = SEQS * LEN
    group_rows = SEQS_DEV * LEN
    slot_count = SEQS // SEQS_DEV * CAP
    places = jnp.arange(LEN, dtype=jnp.int32)
    bucket_grid = buckets[(places[None, :] - places[:, None] + (LEN - 1)).astype(jnp.int32)]
    route_flat = routes.reshape(tokens).astype(jnp.int32)
    owner_group = (jnp.arange(tokens, dtype=jnp.int32) // group_rows).astype(jnp.int32)
    slot_index = jnp.where(dropped.reshape(tokens) == 1, EXPERTS * slot_count, route_flat * slot_count + owner_group * CAP + positions.reshape(tokens)).astype(jnp.int32)
    live_rows = valid_mask.reshape(tokens).astype(jnp.float32)

    def forward(layer_in, gain_one, w_qkv, w_out, gain_two, w_router, bias_table, w_in, w_back):
        bias_heads = jnp.transpose(bias_table[bucket_grid], (2, 0, 1))

        def per_sequence(element):
            return attention_block(element[0], element[1], element[2], bias_heads, gain_one, w_qkv, w_out)
        attn = lax.map(jax.checkpoint(per_sequence), (layer_in, segment_ids, valid_mask))
        middle = (layer_in + attn).reshape(tokens, D)
        normed = low(rms_norm(middle, gain_two))
        logits = low_back(matmul(normed, w_router))
        router_probs = jax.nn.softmax(logits, axis=-1)
        gate_value = jnp.take_along_axis(router_probs, route_flat[:, None], axis=1)[:, 0]
        filled = jnp.zeros((EXPERTS * slot_count, D), normed.dtype).at[slot_index].set(normed, mode='drop')
        filled = low_back(filled).reshape(EXPERTS, slot_count, D)

        def per_expert(element):
            before = low_back(matmul(element[0], element[1]))
            hidden = low(smooth_unit(before))
            return low_back(low(matmul(hidden, element[2])))
        results = lax.map(per_expert, (filled, w_in, w_back)).reshape(EXPERTS * slot_count, D)
        picked = jnp.take(results, slot_index, axis=0, mode='fill', fill_value=0.0)
        final = middle + gate_value[:, None] * picked
        flat_in = layer_in.reshape(tokens, D)
        square_sums = jnp.stack([jnp.sum(live_rows[:, None] * flat_in * flat_in), jnp.sum(live_rows[:, None] * middle * middle), jnp.sum(live_rows[:, None] * final * final)])
        return (final.reshape(SEQS, LEN, D), square_sums)
    final, pullback, square_sums = jax.vjp(forward, inputs.astype(jnp.float32), attn_gain.astype(jnp.float32), qkv_weight.astype(jnp.float32), out_weight.astype(jnp.float32), ffn_gain.astype(jnp.float32), router_weight.astype(jnp.float32), rel_bias.astype(jnp.float32), expert_in.astype(jnp.float32), expert_out.astype(jnp.float32), has_aux=True)
    grads = pullback(cotangent.astype(jnp.float32))
    live_count = jnp.sum(live_rows)
    stats = jnp.sqrt(square_sums / (live_count * D))
    return (final.astype(jnp.bfloat16), grads[0], grads[1], grads[2], grads[3], grads[4], grads[5], grads[6], grads[7], grads[8], stats)
```

```python
import functools

import jax
import jax.numpy as jnp
from jax import lax
from jax.experimental import pallas as pl
from jax.experimental.pallas import tpu as pltpu
from jax.sharding import PartitionSpec as P

EPSILON = 1e-06
HIGHEST = lax.Precision.HIGHEST


def smooth_unit(values):
    return jax.nn.gelu(values, approximate=True)


def smooth_slope(values):
    unused_value, pullback = jax.vjp(smooth_unit, values)
    return pullback(jnp.ones_like(values))[0]


def norm_factor(values):
    return lax.rsqrt(jnp.mean(values * values, axis=-1, keepdims=True) + EPSILON)


def norm_backward(grad_rows, values, factor, norm_gain):
    normed = values * factor
    weighted = grad_rows * norm_gain
    gain_grad = jnp.sum(grad_rows * normed, axis=0)
    values_grad = factor * (weighted - normed * jnp.mean(weighted * normed, axis=-1, keepdims=True))
    return (values_grad, gain_grad)


def bucket_table(buckets, rel_bias):
    indices = jnp.arange(rel_bias.shape[0], dtype=jnp.int32)
    return (buckets[:, None] == indices[None, :]).astype(jnp.float32)


def scatter_rows(rows, slot_index, experts, capacity):
    empty = jnp.zeros((experts * capacity, rows.shape[1]), rows.dtype)
    return empty.at[slot_index].set(rows, mode="drop").reshape(experts, 1, capacity, rows.shape[1])


MASK_STEP = 1e30
ROWS = 256
LANES = 128
REACH = 5
bf16, f32 = jnp.bfloat16, jnp.float32
NT = (((1,), (1,)), ((), ()))
NN = (((1,), (0,)), ((), ()))


def dot(left, right, dims):
    return lax.dot_general(left, right, dims, preferred_element_type=f32)


def bias_windows(values, reach):
    heads, offsets = values.shape
    chunks = (offsets + 1) // LANES
    turned = jnp.pad(values[:, ::-1], ((0, 0), (1, 0))).reshape(heads, chunks, LANES)
    middle = chunks // 2
    groups = list(range(-reach, reach + 1))
    first = [middle - g for g in groups]
    here = turned[:, first[-1] : first[0] + 1][:, ::-1]
    before = turned[:, first[-1] - 1 : first[0]][:, ::-1]
    return jnp.concatenate([here, before], axis=2)


def toeplitz_kernel(reach, window_ref, tile_ref):
    for g in range(2 * reach + 1):
        row = window_ref[0, g : g + 1, :]
        full = jnp.broadcast_to(row, (LANES, 2 * LANES))
        turned = pltpu.roll(full, 0, 1, stride=1, stride_axis=0)
        tile_ref[0, g * LANES : (g + 1) * LANES, :] = turned[:, :LANES]


def toeplitz_tiles(windows):
    heads, groups, width = windows.shape
    return pl.pallas_call(
        functools.partial(toeplitz_kernel, groups // 2),
        grid=(heads,),
        in_specs=[pl.BlockSpec((1, groups, width), lambda n: (n, 0, 0))],
        out_specs=pl.BlockSpec((1, groups * LANES, LANES), lambda n: (n, 0, 0)),
        out_shape=jax.ShapeDtypeStruct((heads, groups * LANES, LANES), f32),
        name="toeplitz_tiles",
    )(windows)


def head_lanes(rows, head, head_dim):
    lane = lax.broadcasted_iota(jnp.int32, rows.shape, 1)
    return jnp.where((lane >= head * head_dim) & (lane < (head + 1) * head_dim), rows, jnp.zeros_like(rows))


def bias_tile(bias_ref, head, offset):
    parts = [
        bias_ref[head, pl.ds(pl.multiple_of(offset - LANES * part, LANES), ROWS), :]
        for part in range(ROWS // LANES)
    ]
    return jnp.concatenate(parts, axis=1)


def forward_kernel(head_dim, reach, low_ref, high_ref, q_ref, k_ref, v_ref, qx_ref, kx_ref, bias_ref, mix_ref, lse_ref, vt_ref):
    length, width = q_ref.shape
    heads = width // head_dim
    scale = head_dim ** (-0.5)
    for c in range(width // LANES):
        vt_ref[c * LANES : (c + 1) * LANES, :] = v_ref[:, c * LANES : (c + 1) * LANES].T
    per = LANES // head_dim

    def one_block(qb, unused):
        first = pl.multiple_of(qb * ROWS, ROWS)
        qx = qx_ref[pl.ds(first, ROWS), :]
        queries = []
        for h in range(heads):
            c = h // per
            pair = q_ref[pl.ds(first, ROWS), c * LANES : (c + 1) * LANES] * jnp.asarray(scale, bf16)
            queries.append(jnp.concatenate([head_lanes(pair, h % per, head_dim), qx], axis=1))

        def one_tile(kb, carry):
            keys_at = pl.multiple_of(kb * ROWS, ROWS)
            offset = pl.multiple_of(keys_at - first + LANES * reach, LANES)
            kx = kx_ref[pl.ds(keys_at, ROWS), :]
            out = []
            for h in range(heads):
                c = h // per
                peak, total, mixed = carry[h]
                keys = jnp.concatenate([k_ref[pl.ds(keys_at, ROWS), c * LANES : (c + 1) * LANES], kx], axis=1)
                scores = dot(keys, queries[h], NT) + bias_tile(bias_ref, h, offset)
                new_peak = jnp.maximum(peak, jnp.max(scores, axis=0, keepdims=True))
                weights = jnp.exp(scores - new_peak)
                shrink = jnp.exp(peak - new_peak)
                total = total * shrink + jnp.sum(weights, axis=0, keepdims=True)
                values = vt_ref[h * head_dim : (h + 1) * head_dim, pl.ds(keys_at, ROWS)]
                mixed = mixed * shrink + dot(values, weights.astype(bf16), NN)
                out.append((new_peak, total, mixed))
            return tuple(out)

        start = tuple(
            (jnp.full((1, ROWS), -3e38, f32), jnp.zeros((1, ROWS), f32), jnp.zeros((head_dim, ROWS), f32))
            for h in range(heads)
        )
        done = lax.fori_loop(low_ref[qb], high_ref[qb], one_tile, start)
        for c in range(width // LANES):
            rows = jnp.concatenate([done[h][2] / done[h][1] for h in range(c * per, (c + 1) * per)], axis=0)
            mix_ref[pl.ds(first, ROWS), c * LANES : (c + 1) * LANES] = rows.T.astype(bf16)
        for h in range(heads):
            lse_ref[0, h : h + 1, pl.ds(first, ROWS)] = done[h][0] + jnp.log(done[h][1])
        return unused

    lax.fori_loop(0, length // ROWS, one_block, 0)


def backward_kernel(head_dim, reach, low_ref, high_ref, q_ref, k_ref, v_ref, dmix_ref, mix_ref, qx_ref, kx_ref, bias_ref, lse_ref,
                    grad_ref, diag_ref, kt_ref, dk_ref, dv_ref, along_ref):
    length, width = q_ref.shape
    heads = width // head_dim
    scale = head_dim ** (-0.5)
    per = LANES // head_dim
    for c in range(width // LANES):
        kt_ref[c * LANES : (c + 1) * LANES, :] = k_ref[:, c * LANES : (c + 1) * LANES].T
    dk_ref[...] = jnp.zeros_like(dk_ref)
    dv_ref[...] = jnp.zeros_like(dv_ref)
    along_ref[...] = jnp.zeros_like(along_ref)

    def one_block(qb, unused):
        first = pl.multiple_of(qb * ROWS, ROWS)
        qx = qx_ref[pl.ds(first, ROWS), :]
        queries, d_mixes, deltas = [], [], []
        for h in range(heads):
            c = h // per
            lanes = slice(c * LANES, (c + 1) * LANES)
            queries.append(head_lanes(q_ref[pl.ds(first, ROWS), lanes] * jnp.asarray(scale, bf16), h % per, head_dim))
            d_mix = dmix_ref[pl.ds(first, ROWS), lanes]
            d_mixes.append(head_lanes(d_mix, h % per, head_dim))
            if h % per == 0:
                product = (d_mix.astype(f32) * mix_ref[pl.ds(first, ROWS), lanes].astype(f32)).T
            deltas.append(jnp.sum(product[(h % per) * head_dim : (h % per + 1) * head_dim], axis=0, keepdims=True))
        wide = [jnp.concatenate([queries[h], qx], axis=1) for h in range(heads)]
        lses = [lse_ref[0, h : h + 1, pl.ds(first, ROWS)] for h in range(heads)]

        def one_tile(kb, carry):
            keys_at = pl.multiple_of(kb * ROWS, ROWS)
            offset = pl.multiple_of(keys_at - first + LANES * reach, LANES)
            kx = kx_ref[pl.ds(keys_at, ROWS), :]
            out = []
            low_weights, low_scores = [], []
            for h in range(heads):
                c = h // per
                lanes = slice(c * LANES, (c + 1) * LANES)
                keys = jnp.concatenate([k_ref[pl.ds(keys_at, ROWS), lanes], kx], axis=1)
                scores = dot(keys, wide[h], NT) + bias_tile(bias_ref, h, offset)
                weights = jnp.exp(scores - lses[h])
                d_weights = dot(v_ref[pl.ds(keys_at, ROWS), lanes], d_mixes[h], NT)
                d_scores = weights * (d_weights - deltas[h])
                for part in range(ROWS // LANES):
                    at = pl.ds(pl.multiple_of(offset - LANES * part, LANES), ROWS)
                    along_ref[h, at, :] += d_scores[:, part * LANES : (part + 1) * LANES]
                low_weights.append(weights.astype(bf16))
                low_scores.append(d_scores.astype(bf16))
                out.append(carry[h] + dot(kt_ref[h * head_dim : (h + 1) * head_dim, pl.ds(keys_at, ROWS)], low_scores[h], NN))
            for c in range(width // LANES):
                mine = range(c * per, (c + 1) * per)
                lanes = slice(c * LANES, (c + 1) * LANES)
                dv_ref[pl.ds(keys_at, ROWS), lanes] += dot(
                    jnp.concatenate([low_weights[h] for h in mine], axis=1), jnp.concatenate([d_mixes[h] for h in mine], axis=0), NN)
                dk_ref[pl.ds(keys_at, ROWS), lanes] += dot(
                    jnp.concatenate([low_scores[h] for h in mine], axis=1), jnp.concatenate([queries[h] for h in mine], axis=0), NN)
            return tuple(out)

        start = tuple(jnp.zeros((head_dim, ROWS), f32) for h in range(heads))
        done = lax.fori_loop(low_ref[qb], high_ref[qb], one_tile, start)
        for c in range(width // LANES):
            rows = jnp.concatenate([done[h] for h in range(c * per, (c + 1) * per)], axis=0) * scale
            grad_ref[0, pl.ds(first, ROWS), c * LANES : (c + 1) * LANES] = rows.T.astype(bf16)
        return unused

    lax.fori_loop(0, length // ROWS, one_block, 0)
    grad_ref[1] = dk_ref[...].astype(bf16)
    grad_ref[2] = dv_ref[...].astype(bf16)
    for h in range(heads):
        for g in range(2 * reach + 1):
            tile = along_ref[h, g * LANES : (g + 1) * LANES, :]
            turned = jnp.concatenate([tile, jnp.zeros_like(tile)], axis=1)
            step = LANES // 2
            while step >= 8:
                turned = turned[:step] + pltpu.roll(turned[step:], 2 * LANES - step, 1)
                step //= 2
            while step:
                turned = turned + pltpu.roll(pltpu.roll(turned, 2 * LANES - step, 1), 8 - step, 0)
                step //= 2
            diag_ref[h, g : g + 1, :] = turned[:1]


def tile_bounds(segments):
    length = segments.shape[0]
    blocks = segments.reshape(length // ROWS, ROWS)
    starts = jnp.sum((segments[None, :] < blocks[:, :1]).astype(jnp.int32), axis=1)
    ends = jnp.sum((segments[None, :] <= blocks[:, -1:]).astype(jnp.int32), axis=1)
    return starts // ROWS, (ends + ROWS - 1) // ROWS


def mask_columns(segments, validity, segment_count=8):
    length = segments.shape[0]
    short = 1
    while short * (short + 1) < length:
        short += 1
    at = jnp.arange(length, dtype=jnp.int32)
    lane = jnp.arange(LANES, dtype=jnp.int32)[None, :]
    in_first = (lane >= segment_count) & (lane < segment_count + short)
    in_second = (lane >= segment_count + short) & (lane < segment_count + 2 * short + 1)
    mine = (
        (lane == segments[:, None])
        | (in_first & (lane - segment_count == (at % short)[:, None]))
        | (in_second & (lane - segment_count - short == (at % (short + 1))[:, None]))
    )
    used = lane < segment_count + 2 * short + 1
    query_side = jnp.where(used & ~mine, -MASK_STEP, 0.0).astype(bf16)
    real = (validity == 1)[:, None]
    key_side = jnp.where(mine & jnp.where(real, lane < segment_count, lane >= segment_count), 1.0, 0.0).astype(bf16)
    return query_side, key_side


def attend_forward(packed, query_side, key_side, bounds, tiles, head_dim, heads_step):
    length = packed.shape[0]
    width = packed.shape[1] // 3
    heads = tiles.shape[0]
    reach = tiles.shape[1] // LANES // 2
    block = heads_step * head_dim
    steps = width // block
    grid_spec = pltpu.PrefetchScalarGridSpec(
        num_scalar_prefetch=2,
        grid=(steps,),
        in_specs=[
            pl.BlockSpec((length, block), lambda p, *_: (0, p)),
            pl.BlockSpec((length, block), lambda p, *_: (0, p + steps)),
            pl.BlockSpec((length, block), lambda p, *_: (0, p + 2 * steps)),
            pl.BlockSpec((length, LANES), lambda p, *_: (0, 0)),
            pl.BlockSpec((length, LANES), lambda p, *_: (0, 0)),
            pl.BlockSpec((heads_step, tiles.shape[1], LANES), lambda p, *_: (p, 0, 0)),
        ],
        out_specs=[
            pl.BlockSpec((length, block), lambda p, *_: (0, p)),
            pl.BlockSpec((1, heads_step, length), lambda p, *_: (p, 0, 0)),
        ],
        scratch_shapes=[pltpu.VMEM((block, length), bf16)],
    )
    return pl.pallas_call(
        functools.partial(forward_kernel, head_dim, reach),
        grid_spec=grid_spec,
        out_shape=[
            jax.ShapeDtypeStruct((length, width), bf16),
            jax.ShapeDtypeStruct((steps, heads_step, length), f32),
        ],
        compiler_params=pltpu.CompilerParams(vmem_limit_bytes=48 * 2**20),
        name="attend_forward",
    )(*bounds, packed, packed, packed, query_side, key_side, tiles)


def attend_backward(packed, d_mix, mix, lse, query_side, key_side, bounds, tiles, head_dim, heads_step):
    length = packed.shape[0]
    width = packed.shape[1] // 3
    heads = tiles.shape[0]
    reach = tiles.shape[1] // LANES // 2
    groups = 2 * reach + 1
    block = heads_step * head_dim
    steps = width // block
    grid_spec = pltpu.PrefetchScalarGridSpec(
        num_scalar_prefetch=2,
        grid=(steps,),
        in_specs=[
            pl.BlockSpec((length, block), lambda p, *_: (0, p)),
            pl.BlockSpec((length, block), lambda p, *_: (0, p + steps)),
            pl.BlockSpec((length, block), lambda p, *_: (0, p + 2 * steps)),
            pl.BlockSpec((length, block), lambda p, *_: (0, p)),
            pl.BlockSpec((length, block), lambda p, *_: (0, p)),
            pl.BlockSpec((length, LANES), lambda p, *_: (0, 0)),
            pl.BlockSpec((length, LANES), lambda p, *_: (0, 0)),
            pl.BlockSpec((heads_step, tiles.shape[1], LANES), lambda p, *_: (p, 0, 0)),
            pl.BlockSpec((1, heads_step, length), lambda p, *_: (p, 0, 0)),
        ],
        out_specs=[
            pl.BlockSpec((3, length, block), lambda p, *_: (0, 0, p)),
            pl.BlockSpec((heads_step, groups, 2 * LANES), lambda p, *_: (p, 0, 0)),
        ],
        scratch_shapes=[
            pltpu.VMEM((block, length), bf16),
            pltpu.VMEM((length, block), f32),
            pltpu.VMEM((length, block), f32),
            pltpu.VMEM((heads_step, groups * LANES, LANES), f32),
        ],
    )
    return pl.pallas_call(
        functools.partial(backward_kernel, head_dim, reach),
        grid_spec=grid_spec,
        out_shape=[
            jax.ShapeDtypeStruct((3, length, width), bf16),
            jax.ShapeDtypeStruct((heads, groups, 2 * LANES), f32),
        ],
        compiler_params=pltpu.CompilerParams(vmem_limit_bytes=56 * 2**20),
        name="attend_backward",
    )(*bounds, packed, packed, packed, d_mix, mix, query_side, key_side, tiles, lse)


def body(
    inputs,
    cotangent,
    attn_gain,
    qkv_weight,
    out_weight,
    ffn_gain,
    router_weight,
    rel_bias,
    expert_in,
    expert_out,
    routes,
    positions,
    dropped,
    segment_ids,
    valid_mask,
    buckets,
):
    seq_count, seq_length, model_width = inputs.shape
    tokens = seq_count * seq_length
    dense_full = (
        lax.all_gather(attn_gain, ("dp", "expert"), axis=0, tiled=True),
        lax.all_gather(qkv_weight, ("dp", "expert"), axis=0, tiled=True),
        lax.all_gather(out_weight, ("dp", "expert"), axis=0, tiled=True),
        lax.all_gather(ffn_gain, ("dp", "expert"), axis=0, tiled=True),
        lax.all_gather(router_weight, ("dp", "expert"), axis=0, tiled=True),
    )
    gain_one = dense_full[0].astype(jnp.float32)
    gain_two = dense_full[3].astype(jnp.float32)
    one_hot_buckets = bucket_table(buckets, rel_bias)
    head_bias = jnp.dot(
        one_hot_buckets, rel_bias, precision=HIGHEST, preferred_element_type=jnp.float32
    ).T
    head_count = rel_bias.shape[1]
    head_dim = model_width // head_count
    windows = bias_windows(head_bias, REACH)
    tiles = toeplitz_tiles(windows)
    layer_in = inputs.astype(jnp.float32)
    saved = []
    for seq in range(seq_count):
        factor = norm_factor(layer_in[seq])
        normed = (layer_in[seq] * factor * gain_one).astype(jnp.bfloat16)
        packed = jnp.dot(normed, dense_full[1], preferred_element_type=jnp.float32).astype(jnp.bfloat16)
        masks = mask_columns(segment_ids[seq], valid_mask[seq])
        bounds = tile_bounds(segment_ids[seq])
        mixed, log_totals = attend_forward(packed, *masks, bounds, tiles, head_dim, 2)
        attn_out = jnp.dot(mixed, dense_full[2], preferred_element_type=jnp.float32)
        saved.append((factor, normed, packed, masks, bounds, mixed, log_totals, attn_out))
    mid_rows = (layer_in + jnp.stack([state[-1] for state in saved])).reshape(tokens, model_width)
    experts = dense_full[4].shape[1]
    capacity = 5 * tokens // (4 * experts)
    route_ids = routes.reshape(tokens)
    slot_index = jnp.where(
        dropped.reshape(tokens) == 1,
        experts * capacity,
        route_ids * capacity + positions.reshape(tokens),
    )
    mid_factor = norm_factor(mid_rows)
    ffn_normed = (mid_rows * mid_factor * gain_two).astype(jnp.bfloat16)
    logits = jnp.dot(ffn_normed, dense_full[4], preferred_element_type=jnp.float32)
    router_probs = jax.nn.softmax(logits, axis=-1)
    chosen = (route_ids[:, None] == jnp.arange(experts, dtype=jnp.int32)[None, :]).astype(
        jnp.float32
    )
    gate_value = jnp.sum(router_probs * chosen, axis=-1)
    send_rows = scatter_rows(ffn_normed, slot_index, experts, capacity)
    received = lax.all_to_all(send_rows, "expert", split_axis=0, concat_axis=1, tiled=True)
    pre_act = jnp.einsum("escd,edf->escf", received, expert_in, preferred_element_type=jnp.float32)
    hidden = smooth_unit(pre_act).astype(jnp.bfloat16)
    rows_out = jnp.einsum(
        "escf,efd->escd", hidden, expert_out, preferred_element_type=jnp.float32
    ).astype(jnp.bfloat16)
    returned = lax.all_to_all(rows_out, "expert", split_axis=1, concat_axis=0, tiled=True)
    picked = jnp.take(
        returned.reshape(experts * capacity, model_width),
        slot_index,
        axis=0,
        mode="fill",
        fill_value=0,
    ).astype(jnp.float32)
    final_rows = mid_rows + gate_value[:, None] * picked
    output = final_rows.astype(jnp.bfloat16).reshape(inputs.shape)
    live_rows = valid_mask.reshape(tokens).astype(jnp.float32)
    flat_in = layer_in.reshape(tokens, model_width)
    square_sums = jnp.stack(
        [
            jnp.sum(live_rows[:, None] * flat_in * flat_in),
            jnp.sum(live_rows[:, None] * mid_rows * mid_rows),
            jnp.sum(live_rows[:, None] * final_rows * final_rows),
        ]
    )
    live_count = jnp.sum(live_rows)
    dense_back = (
        lax.all_gather(attn_gain, ("dp", "expert"), axis=0, tiled=True),
        lax.all_gather(qkv_weight, ("dp", "expert"), axis=0, tiled=True),
        lax.all_gather(out_weight, ("dp", "expert"), axis=0, tiled=True),
        lax.all_gather(ffn_gain, ("dp", "expert"), axis=0, tiled=True),
        lax.all_gather(router_weight, ("dp", "expert"), axis=0, tiled=True),
    )
    back_gain_one = dense_back[0].astype(jnp.float32)
    back_gain_two = dense_back[3].astype(jnp.float32)
    grad_final = cotangent.astype(jnp.float32).reshape(tokens, model_width)
    grad_gate = jnp.sum(grad_final * picked, axis=-1)
    grad_rows = (gate_value[:, None] * grad_final).astype(jnp.bfloat16)
    grad_send = scatter_rows(grad_rows, slot_index, experts, capacity)
    grad_rows_out = lax.all_to_all(grad_send, "expert", split_axis=0, concat_axis=1, tiled=True)
    grad_hidden = jnp.einsum(
        "escd,efd->escf", grad_rows_out, expert_out, preferred_element_type=jnp.float32
    )
    grad_pre = (grad_hidden * smooth_slope(pre_act)).astype(jnp.bfloat16)
    grad_rows_in = jnp.einsum(
        "escf,edf->escd", grad_pre, expert_in, preferred_element_type=jnp.float32
    ).astype(jnp.bfloat16)
    grad_back = lax.all_to_all(grad_rows_in, "expert", split_axis=1, concat_axis=0, tiled=True)
    grad_expert_rows = jnp.take(
        grad_back.reshape(experts * capacity, model_width),
        slot_index,
        axis=0,
        mode="fill",
        fill_value=0,
    ).astype(jnp.float32)
    part_in = jnp.einsum("escd,escf->edf", received, grad_pre, preferred_element_type=jnp.float32)
    part_out = jnp.einsum(
        "escf,escd->efd", hidden, grad_rows_out, preferred_element_type=jnp.float32
    )
    grad_expert_in, grad_expert_out = (
        lax.psum_scatter(
            part_in.astype(jnp.bfloat16), "dp", scatter_dimension=2, tiled=True
        ).astype(jnp.float32),
        lax.psum_scatter(
            part_out.astype(jnp.bfloat16), "dp", scatter_dimension=1, tiled=True
        ).astype(jnp.float32),
    )
    grad_logits = (router_probs * (chosen - gate_value[:, None]) * grad_gate[:, None]).astype(
        jnp.bfloat16
    )
    grad_router = jnp.einsum(
        "td,te->de", ffn_normed, grad_logits, preferred_element_type=jnp.float32
    )
    grad_ffn_normed = (
        jnp.einsum("te,de->td", grad_logits, dense_back[4], preferred_element_type=jnp.float32)
        + grad_expert_rows
    )
    grad_mid_norm, grad_gain_two = norm_backward(
        grad_ffn_normed, mid_rows, mid_factor, back_gain_two
    )
    grad_mid = grad_final + grad_mid_norm
    grad_mid_seq = grad_mid.reshape(seq_count, seq_length, model_width)

    one_hot_windows = bias_windows(one_hot_buckets.T, REACH)
    attn_totals, grad_attn_in = None, []
    for seq in range(seq_count):
        factor, normed, packed, masks, bounds, mixed, log_totals, unused = saved[seq]
        grad_attn_low = grad_mid_seq[seq].astype(jnp.bfloat16)
        grad_out_w = jnp.einsum("td,te->de", mixed, grad_attn_low, preferred_element_type=jnp.float32)
        grad_mixed = jnp.einsum("te,de->td", grad_attn_low, dense_back[2], preferred_element_type=jnp.float32)
        grad_parts, grad_diagonals = attend_backward(
            packed, grad_mixed.astype(jnp.bfloat16), mixed, log_totals, *masks, bounds, tiles, head_dim, 2
        )
        grad_buckets = jnp.einsum("hgp,bgp->bh", grad_diagonals, one_hot_windows, precision=HIGHEST)
        grad_qkv_w = jnp.concatenate(
            [jnp.einsum("td,te->de", normed, grad_parts[i], preferred_element_type=jnp.float32) for i in range(3)], axis=1
        )
        w_parts = dense_back[1].reshape(model_width, 3, model_width)
        grad_normed = jnp.einsum("pte,dpe->td", grad_parts, w_parts, preferred_element_type=jnp.float32)
        grad_layer, grad_gain = norm_backward(grad_normed, layer_in[seq], factor, back_gain_one)
        grad_attn_in.append(grad_layer)
        grads_local = (grad_qkv_w, grad_out_w, grad_gain, grad_buckets)
        attn_totals = grads_local if attn_totals is None else jax.tree.map(jnp.add, attn_totals, grads_local)
    input_grad = grad_mid_seq + jnp.stack(grad_attn_in)
    grad_rel_local = attn_totals[3]
    grad_shards = (
        lax.psum_scatter(attn_totals[2], ("dp", "expert"), scatter_dimension=0, tiled=True),
        lax.psum_scatter(attn_totals[0], ("dp", "expert"), scatter_dimension=0, tiled=True),
        lax.psum_scatter(attn_totals[1], ("dp", "expert"), scatter_dimension=0, tiled=True),
        lax.psum_scatter(grad_gain_two, ("dp", "expert"), scatter_dimension=0, tiled=True),
        lax.psum_scatter(grad_router, ("dp", "expert"), scatter_dimension=0, tiled=True),
    )
    totals, count_all, grad_rel = lax.psum(
        (square_sums, live_count, grad_rel_local), ("dp", "expert")
    )
    stats = jnp.sqrt(totals / (count_all * model_width))
    return (
        output,
        input_grad,
        grad_shards[0],
        grad_shards[1],
        grad_shards[2],
        grad_shards[3],
        grad_shards[4],
        grad_rel,
        grad_expert_in,
        grad_expert_out,
        stats,
    )


def solution(mesh):
    in_specs = (
        P(("dp", "expert"), None, None),
        P(("dp", "expert"), None, None),
        P(("dp", "expert")),
        P(("dp", "expert"), None),
        P(("dp", "expert"), None),
        P(("dp", "expert")),
        P(("dp", "expert"), None),
        P(),
        P("expert", None, None),
        P("expert", None, None),
        P(("dp", "expert"), None),
        P(("dp", "expert"), None),
        P(("dp", "expert"), None),
        P(("dp", "expert"), None),
        P(("dp", "expert"), None),
        P(),
    )
    out_specs = (
        P(("dp", "expert"), None, None),
        P(("dp", "expert"), None, None),
        P(("dp", "expert")),
        P(("dp", "expert"), None),
        P(("dp", "expert"), None),
        P(("dp", "expert")),
        P(("dp", "expert"), None),
        P(),
        P("expert", None, "dp"),
        P("expert", "dp", None),
        P(),
    )
    return jax.shard_map(body, mesh=mesh, in_specs=in_specs, out_specs=out_specs, check_vma=False)
```

```python
import functools

import jax
import jax.numpy as jnp
from jax import lax
from jax.experimental import pallas as pl
from jax.experimental.pallas import tpu as pltpu
from jax.sharding import PartitionSpec as P

MASK_STEP = 1e30
ROWS = 256
LANES = 128
STEP_HEADS = 4
SMALL_GAINS = 2
bf16, f32 = jnp.bfloat16, jnp.float32
NT = (((1,), (1,)), ((), ()))
NN = (((1,), (0,)), ((), ()))
TN = (((0,), (0,)), ((), ()))


def dot(left, right, dims):
    return lax.dot_general(left, right, dims, preferred_element_type=f32)


def bias_windows(values, reach):
    heads, offsets = values.shape
    chunks = (offsets + 1) // LANES
    turned = jnp.pad(values[:, ::-1], ((0, 0), (1, 0))).reshape(heads, chunks, LANES)
    middle = chunks // 2
    groups = list(range(-reach, reach + 1))
    first = [middle - g for g in groups]
    here = turned[:, first[-1] : first[0] + 1][:, ::-1]
    before = turned[:, first[-1] - 1 : first[0]][:, ::-1]
    return jnp.concatenate([here, before], axis=2)


def toeplitz_kernel(reach, window_ref, tile_ref):
    for g in range(2 * reach + 1):
        row = window_ref[0, g : g + 1, :]
        full = jnp.broadcast_to(row, (LANES, 2 * LANES))
        turned = pltpu.roll(full, 0, 1, stride=1, stride_axis=0)
        tile_ref[0, g * LANES : (g + 1) * LANES, :] = turned[:, :LANES]


def toeplitz_tiles(windows):
    heads, groups, width = windows.shape
    return pl.pallas_call(
        functools.partial(toeplitz_kernel, groups // 2),
        grid=(heads,),
        in_specs=[pl.BlockSpec((1, groups, width), lambda n: (n, 0, 0))],
        out_specs=pl.BlockSpec((1, groups * LANES, LANES), lambda n: (n, 0, 0)),
        out_shape=jax.ShapeDtypeStruct((heads, groups * LANES, LANES), f32),
        name="toeplitz_tiles",
    )(windows)


def head_lanes(rows, head, head_dim):
    lane = lax.broadcasted_iota(jnp.int32, rows.shape, 1)
    return jnp.where((lane >= head * head_dim) & (lane < (head + 1) * head_dim), rows, jnp.zeros_like(rows))


def head_rows(columns, head, head_dim):
    row = lax.broadcasted_iota(jnp.int32, columns.shape, 0)
    return jnp.where((row >= head * head_dim) & (row < (head + 1) * head_dim), columns, jnp.zeros_like(columns))


def bias_tile(bias_ref, head, offset):
    parts = [
        bias_ref[head, pl.ds(pl.multiple_of(offset - LANES * part, LANES), ROWS), :]
        for part in range(ROWS // LANES)
    ]
    return jnp.concatenate(parts, axis=1)


def forward_kernel(head_dim, reach, low_ref, high_ref, q_ref, k_ref, v_ref, qx_ref, kx_ref, bias_ref, unused_ref, mix_ref, lse_ref, vt_ref):
    length, width = q_ref.shape
    heads = width // head_dim
    scale = head_dim ** (-0.5)
    for c in range(width // LANES):
        vt_ref[c * LANES : (c + 1) * LANES, :] = v_ref[:, c * LANES : (c + 1) * LANES].T
    per = LANES // head_dim

    def one_block(qb, unused):
        first = pl.multiple_of(qb * ROWS, ROWS)
        qx = qx_ref[:, pl.ds(first, ROWS)]
        queries = []
        for c in range(width // LANES):
            pair = (q_ref[pl.ds(first, ROWS), c * LANES : (c + 1) * LANES] * jnp.asarray(scale, bf16)).T
            queries += [jnp.concatenate([head_rows(pair, h, head_dim), qx], axis=0) for h in range(per)]

        def one_tile(kb, carry):
            keys_at = pl.multiple_of(kb * ROWS, ROWS)
            offset = pl.multiple_of(keys_at - first + LANES * reach, LANES)
            kx = kx_ref[pl.ds(keys_at, ROWS), :]
            out = []
            all_scores = []
            for h in range(heads):
                c = h // per
                keys = jnp.concatenate([k_ref[pl.ds(keys_at, ROWS), c * LANES : (c + 1) * LANES], kx], axis=1)
                all_scores.append(dot(keys, queries[h], NN))
            soft = []
            for h in range(heads):
                peak, total, mixed = carry[h]
                scores = all_scores[h] + bias_tile(bias_ref, h, offset)
                new_peak = jnp.maximum(peak, jnp.max(scores, axis=0, keepdims=True))
                weights = jnp.exp(scores - new_peak)
                shrink = jnp.exp(peak - new_peak)
                total = total * shrink + jnp.sum(weights, axis=0, keepdims=True)
                soft.append((new_peak, total, shrink, weights.astype(bf16)))
            for h in range(heads):
                new_peak, total, shrink, weights = soft[h]
                values = vt_ref[h * head_dim : (h + 1) * head_dim, pl.ds(keys_at, ROWS)]
                mixed = carry[h][2] * shrink + dot(values, weights, NN)
                out.append((new_peak, total, mixed))
            return tuple(out)

        start = tuple(
            (jnp.full((1, ROWS), -3e38, f32), jnp.zeros((1, ROWS), f32), jnp.zeros((head_dim, ROWS), f32))
            for h in range(heads)
        )
        done = lax.fori_loop(low_ref[qb], high_ref[qb], one_tile, start)
        for c in range(width // LANES):
            rows = jnp.concatenate([done[h][2] / done[h][1] for h in range(c * per, (c + 1) * per)], axis=0)
            mix_ref[pl.ds(first, ROWS), c * LANES : (c + 1) * LANES] = rows.T.astype(bf16)
        for h in range(heads):
            lse_ref[0, h : h + 1, pl.ds(first, ROWS)] = done[h][0] + jnp.log(done[h][1])
        return unused

    lax.fori_loop(0, length // ROWS, one_block, 0)


def diagonal_sums(tiles):
    groups = tiles.shape[0]
    step = LANES // 2
    zero = jnp.zeros((groups, step, LANES), f32)
    turned = jnp.concatenate([tiles[:, :step], zero], axis=2) + pltpu.roll(
        jnp.concatenate([tiles[:, step:], zero], axis=2), 2 * LANES - step, 2
    )
    while step > 8:
        step //= 2
        turned = turned[:, :step] + pltpu.roll(turned[:, step:], 2 * LANES - step, 2)
    while step > 1:
        step //= 2
        turned = turned + pltpu.roll(pltpu.roll(turned, 2 * LANES - step, 2), 8 - step, 1)
    return turned[:, 0]


def backward_kernel(head_dim, reach, low_ref, high_ref, q_ref, k_ref, v_ref, dmix_ref, mix_ref, qx_ref, kx_ref, bias_ref, lse_ref,
                    grad_ref, diag_ref, kt_ref, dk_ref, dv_ref, along_ref):
    length, width = q_ref.shape
    heads = width // head_dim
    scale = head_dim ** (-0.5)
    per = LANES // head_dim
    for c in range(width // LANES):
        kt_ref[c * LANES : (c + 1) * LANES, :] = k_ref[:, c * LANES : (c + 1) * LANES].T
    dk_ref[...] = jnp.zeros_like(dk_ref)
    dv_ref[...] = jnp.zeros_like(dv_ref)
    along_ref[...] = jnp.zeros_like(along_ref)

    def one_block(qb, unused):
        first = pl.multiple_of(qb * ROWS, ROWS)
        qx = qx_ref[:, pl.ds(first, ROWS)]
        queries, d_mixes, deltas, wide, d_turned = [], [], [], [], []
        for c in range(width // LANES):
            lanes = slice(c * LANES, (c + 1) * LANES)
            query = q_ref[pl.ds(first, ROWS), lanes] * jnp.asarray(scale, bf16)
            d_mix = dmix_ref[pl.ds(first, ROWS), lanes]
            product = (d_mix.astype(f32) * mix_ref[pl.ds(first, ROWS), lanes].astype(f32)).T
            query_turned, d_mix_turned = query.T, d_mix.T
            for h in range(per):
                queries.append(head_lanes(query, h, head_dim))
                d_mixes.append(head_lanes(d_mix, h, head_dim))
                wide.append(jnp.concatenate([head_rows(query_turned, h, head_dim), qx], axis=0))
                d_turned.append(head_rows(d_mix_turned, h, head_dim))
                deltas.append(jnp.sum(product[h * head_dim : (h + 1) * head_dim], axis=0, keepdims=True))
        lses = [lse_ref[0, h : h + 1, pl.ds(first, ROWS)] for h in range(heads)]

        def one_tile(kb, carry):
            keys_at = pl.multiple_of(kb * ROWS, ROWS)
            offset = pl.multiple_of(keys_at - first + LANES * reach, LANES)
            kx = kx_ref[pl.ds(keys_at, ROWS), :]
            out = []
            low_weights, low_scores, all_scores, all_weights = [], [], [], []
            for h in range(heads):
                lanes = slice(h // per * LANES, (h // per + 1) * LANES)
                keys = jnp.concatenate([k_ref[pl.ds(keys_at, ROWS), lanes], kx], axis=1)
                all_scores.append(dot(keys, wide[h], NN))
            for h in range(heads):
                lanes = slice(h // per * LANES, (h // per + 1) * LANES)
                all_weights.append(dot(v_ref[pl.ds(keys_at, ROWS), lanes], d_turned[h], NN))
            for h in range(heads):
                weights = jnp.exp(all_scores[h] + bias_tile(bias_ref, h, offset) - lses[h])
                d_scores = weights * (all_weights[h] - deltas[h])
                for part in range(ROWS // LANES):
                    at = pl.ds(pl.multiple_of(offset - LANES * part, LANES), ROWS)
                    along_ref[h, at, :] += d_scores[:, part * LANES : (part + 1) * LANES]
                low_weights.append(weights.astype(bf16))
                low_scores.append(d_scores.astype(bf16))
            for h in range(heads):
                keys_turned = kt_ref[h * head_dim : (h + 1) * head_dim, pl.ds(keys_at, ROWS)]
                out.append(carry[h] + dot(keys_turned, low_scores[h], NN))
            for c in range(width // LANES):
                mine = range(c * per, (c + 1) * per)
                lanes = slice(c * LANES, (c + 1) * LANES)
                dv_ref[pl.ds(keys_at, ROWS), lanes] += dot(
                    jnp.concatenate([low_weights[h] for h in mine], axis=1), jnp.concatenate([d_mixes[h] for h in mine], axis=0), NN)
                dk_ref[pl.ds(keys_at, ROWS), lanes] += dot(
                    jnp.concatenate([low_scores[h] for h in mine], axis=1), jnp.concatenate([queries[h] for h in mine], axis=0), NN)
            return tuple(out)

        start = tuple(jnp.zeros((head_dim, ROWS), f32) for h in range(heads))
        done = lax.fori_loop(low_ref[qb], high_ref[qb], one_tile, start)
        for c in range(width // LANES):
            rows = jnp.concatenate([done[h] for h in range(c * per, (c + 1) * per)], axis=0) * scale
            grad_ref[pl.ds(first, ROWS), c * LANES : (c + 1) * LANES] = rows.T.astype(bf16)
        return unused

    lax.fori_loop(0, length // ROWS, one_block, 0)
    grad_ref[:, width : 2 * width] = dk_ref[...].astype(bf16)
    grad_ref[:, 2 * width :] = dv_ref[...].astype(bf16)
    for h in range(heads):
        diag_ref[h] = diagonal_sums(along_ref[h].reshape(2 * reach + 1, LANES, LANES))


def tile_bounds(segments):
    length = segments.shape[0]
    blocks = segments.reshape(length // ROWS, ROWS)
    starts = jnp.sum((segments[None, :] < blocks[:, :1]).astype(jnp.int32), axis=1)
    ends = jnp.sum((segments[None, :] <= blocks[:, -1:]).astype(jnp.int32), axis=1)
    return starts // ROWS, (ends + ROWS - 1) // ROWS


def mask_columns(segments, validity, segment_count=8):
    length = segments.shape[0]
    short = 1
    while short * (short + 1) < length:
        short += 1
    at = jnp.arange(length, dtype=jnp.int32)
    lane = jnp.arange(LANES, dtype=jnp.int32)[None, :]
    in_first = (lane >= segment_count) & (lane < segment_count + short)
    in_second = (lane >= segment_count + short) & (lane < segment_count + 2 * short + 1)
    mine = (
        (lane == segments[:, None])
        | (in_first & (lane - segment_count == (at % short)[:, None]))
        | (in_second & (lane - segment_count - short == (at % (short + 1))[:, None]))
    )
    used = lane < segment_count + 2 * short + 1
    query_side = jnp.where(used & ~mine, -MASK_STEP, 0.0).astype(bf16).T
    real = (validity == 1)[:, None]
    key_side = jnp.where(mine & jnp.where(real, lane < segment_count, lane >= segment_count), 1.0, 0.0).astype(bf16)
    return query_side, key_side


def attend_forward(packed, query_side, key_side, bounds, tiles, mixed, first, head_dim):
    length = packed.shape[0]
    width = STEP_HEADS * head_dim
    steps = packed.shape[1] // 3 // width
    reach = tiles.shape[1] // LANES // 2
    whole = lambda *_: (0, 0)
    grid_spec = pltpu.PrefetchScalarGridSpec(
        num_scalar_prefetch=2,
        grid=(steps,),
        in_specs=[
            pl.BlockSpec((length, width), lambda p, *_: (0, 3 * p)),
            pl.BlockSpec((length, width), lambda p, *_: (0, 3 * p + 1)),
            pl.BlockSpec((length, width), lambda p, *_: (0, 3 * p + 2)),
            pl.BlockSpec((LANES, length), whole),
            pl.BlockSpec((length, LANES), whole),
            pl.BlockSpec((STEP_HEADS, tiles.shape[1], LANES), lambda p, *_: (first + p, 0, 0)),
            pl.BlockSpec(memory_space=pl.ANY),
        ],
        out_specs=[
            pl.BlockSpec((length, width), lambda p, *_: (0, first + p)),
            pl.BlockSpec((1, STEP_HEADS, length), lambda p, *_: (p, 0, 0)),
        ],
        scratch_shapes=[pltpu.VMEM((width, length), bf16)],
    )
    work = steps * STEP_HEADS * length * length
    return pl.pallas_call(
        functools.partial(forward_kernel, head_dim, reach),
        grid_spec=grid_spec,
        out_shape=[
            jax.ShapeDtypeStruct(mixed.shape, bf16),
            jax.ShapeDtypeStruct((steps, STEP_HEADS, length), f32),
        ],
        input_output_aliases={8: 0},
        compiler_params=pltpu.CompilerParams(vmem_limit_bytes=40 * 2**20),
        cost_estimate=pl.CostEstimate(flops=32 * work * head_dim, bytes_accessed=steps * 36 * 2**20, transcendentals=work),
        name="attend_forward",
    )(*bounds, packed, packed, packed, query_side, key_side, tiles, mixed)


def attend_backward(packed, d_mix, mix, lse, query_side, key_side, bounds, tiles, first, head_dim):
    length = packed.shape[0]
    width = STEP_HEADS * head_dim
    steps = packed.shape[1] // 3 // width
    reach = tiles.shape[1] // LANES // 2
    groups = 2 * reach + 1
    whole = lambda *_: (0, 0)
    grid_spec = pltpu.PrefetchScalarGridSpec(
        num_scalar_prefetch=2,
        grid=(steps,),
        in_specs=[
            pl.BlockSpec((length, width), lambda p, *_: (0, 3 * p)),
            pl.BlockSpec((length, width), lambda p, *_: (0, 3 * p + 1)),
            pl.BlockSpec((length, width), lambda p, *_: (0, 3 * p + 2)),
            pl.BlockSpec((length, width), lambda p, *_: (0, first + p)),
            pl.BlockSpec((length, width), lambda p, *_: (0, first + p)),
            pl.BlockSpec((LANES, length), whole),
            pl.BlockSpec((length, LANES), whole),
            pl.BlockSpec((STEP_HEADS, tiles.shape[1], LANES), lambda p, *_: (first + p, 0, 0)),
            pl.BlockSpec((1, STEP_HEADS, length), lambda p, *_: (p, 0, 0)),
        ],
        out_specs=[
            pl.BlockSpec((length, 3 * width), lambda p, *_: (0, p)),
            pl.BlockSpec((STEP_HEADS, groups, 2 * LANES), lambda p, *_: (p, 0, 0)),
        ],
        scratch_shapes=[
            pltpu.VMEM((width, length), bf16),
            pltpu.VMEM((length, width), f32),
            pltpu.VMEM((length, width), f32),
            pltpu.VMEM((STEP_HEADS, groups * LANES, LANES), f32),
        ],
    )
    work = steps * STEP_HEADS * length * length
    return pl.pallas_call(
        functools.partial(backward_kernel, head_dim, reach),
        grid_spec=grid_spec,
        out_shape=[
            jax.ShapeDtypeStruct((length, 3 * width * steps), bf16),
            jax.ShapeDtypeStruct((steps * STEP_HEADS, groups, 2 * LANES), f32),
        ],
        compiler_params=pltpu.CompilerParams(vmem_limit_bytes=52 * 2**20),
        cost_estimate=pl.CostEstimate(flops=80 * work * head_dim, bytes_accessed=steps * 72 * 2**20, transcendentals=work),
        name="attend_backward",
    )(*bounds, packed, packed, packed, d_mix, mix, query_side, key_side, tiles, lse)


def spread_kernel(groups, width, weight_ref, first_ref, second_ref, router_ref, *outs):
    receivers, count = outs[0].shape[:2]
    steps = weight_ref.shape[1] // (3 * width)
    for (first, many), out_ref in zip(groups, outs):
        for p in range(many):
            for part in range(3):
                at = (part * steps + first + p) * width
                rows = weight_ref[:, at : at + width]
                to = (3 * p + part) * width
                out_ref[:, :, to : to + width] = jnp.broadcast_to(rows[None], (receivers, *rows.shape))
    row = lax.broadcasted_iota(jnp.int32, (count, count), 0)
    same = row == lax.broadcasted_iota(jnp.int32, (count, count), 1)
    columns = [
        jnp.sum(jnp.where(same, jnp.broadcast_to(ref[...].astype(f32), same.shape), 0.0), axis=1, keepdims=True)
        for ref in (first_ref, second_ref)
    ]
    columns.append(router_ref[...].astype(f32))
    used = SMALL_GAINS + router_ref.shape[1]
    columns.append(jnp.zeros((count, -used % LANES), f32))
    rows = jnp.concatenate(columns, axis=1).astype(bf16)
    outs[0][:, :, 3 * groups[0][1] * width :] = jnp.broadcast_to(rows[None], (receivers, *rows.shape))


def spread_shard(weight, first_gain, second_gain, router, groups, width, receivers):
    rows = weight.shape[0]
    small = SMALL_GAINS + router.shape[1]
    small += -small % LANES
    widths = [3 * many * width + (0 if first else small) for first, many in groups]
    return pl.pallas_call(
        functools.partial(spread_kernel, groups, width),
        out_shape=[jax.ShapeDtypeStruct((receivers, rows, columns), bf16) for columns in widths],
        name="spread_shard",
    )(weight, first_gain.reshape(1, rows), second_gain.reshape(1, rows), router)


def expert_kernel(experts, me_ref, rows_ref, in_ref, small_ref, d_hidden_ref, hidden_ref, d_pre_ref, d_rows_ref, d_logits_ref, gate_ref,
                  probs_ref, total_ref, d_gate_ref):
    step = pl.program_id(0)
    lane = lax.broadcasted_iota(jnp.int32, probs_ref.shape, 1)
    chosen = lane == me_ref[0] + SMALL_GAINS

    @pl.when(step == 0)
    def _():
        logits = dot(rows_ref[...], small_ref[...], NN)
        logits = jnp.where((lane >= SMALL_GAINS) & (lane < SMALL_GAINS + experts), logits, -MASK_STEP)
        raised = jnp.exp(logits - jnp.max(logits, axis=1, keepdims=True))
        probs = raised / jnp.sum(raised, axis=1, keepdims=True)
        probs_ref[...] = probs
        gate_ref[...] = jnp.sum(jnp.where(chosen, probs, 0.0), axis=1, keepdims=True)
        total_ref[...] = jnp.zeros_like(total_ref)
        d_gate_ref[...] = jnp.zeros_like(d_gate_ref)

    count = rows_ref.shape[0]
    chunk = 256 if count % 256 == 0 else count
    weights = in_ref[...]
    pres = [dot(rows_ref[at : at + chunk], weights, NN) for at in range(0, count, chunk)]
    lows = []
    for i, at in enumerate(range(0, count, chunk)):
        here = slice(at, at + chunk)
        unit, slope = gelu_and_slope(pres[i])
        hidden = unit.astype(bf16)
        d_hidden = d_hidden_ref[here].astype(f32)
        hidden_ref[here] = hidden
        d_gate_ref[here] += jnp.sum(unit * d_hidden, axis=1, keepdims=True)
        low = (gate_ref[here] * d_hidden * slope).astype(bf16)
        d_pre_ref[here] = low
        lows.append(low)
    for i, at in enumerate(range(0, count, chunk)):
        total_ref[at : at + chunk] += dot(lows[i], weights, NT)

    @pl.when(step == pl.num_programs(0) - 1)
    def _():
        d_logits = (probs_ref[...] * (chosen.astype(f32) - gate_ref[...]) * d_gate_ref[...]).astype(bf16)
        d_logits_ref[...] = d_logits
        d_rows_ref[...] = (total_ref[...] + dot(d_logits, small_ref[...], NT)).astype(bf16)


def run_expert(me, rows, w_in, small, d_hidden, experts):
    count, width = rows.shape
    hidden_width = w_in.shape[1]
    block = 512
    row_blocks = pl.BlockSpec((count, block), lambda f, *_: (0, f))
    whole = lambda f, *_: (0, 0)
    grid_spec = pltpu.PrefetchScalarGridSpec(
        num_scalar_prefetch=1,
        grid=(hidden_width // block,),
        in_specs=[
            pl.BlockSpec((count, width), whole),
            pl.BlockSpec((width, block), lambda f, *_: (0, f)),
            pl.BlockSpec(small.shape, whole),
            row_blocks,
        ],
        out_specs=[
            row_blocks,
            row_blocks,
            pl.BlockSpec((count, width), whole),
            pl.BlockSpec((count, LANES), whole),
            pl.BlockSpec((count, 1), whole),
        ],
        scratch_shapes=[pltpu.VMEM((count, LANES), f32), pltpu.VMEM((count, width), f32), pltpu.VMEM((count, 1), f32)],
    )
    return pl.pallas_call(
        functools.partial(expert_kernel, experts),
        grid_spec=grid_spec,
        out_shape=[
            jax.ShapeDtypeStruct((count, hidden_width), bf16),
            jax.ShapeDtypeStruct((count, hidden_width), bf16),
            jax.ShapeDtypeStruct((count, width), bf16),
            jax.ShapeDtypeStruct((count, LANES), bf16),
            jax.ShapeDtypeStruct((count, 1), f32),
        ],
        compiler_params=pltpu.CompilerParams(vmem_limit_bytes=48 * 2**20),
        cost_estimate=pl.CostEstimate(
            flops=4 * count * width * hidden_width, bytes_accessed=30 * 2**20, transcendentals=count * hidden_width
        ),
        name="run_expert",
    )(me.reshape(1), rows, w_in, small, d_hidden)


EPSILON = 1e-06
HIGHEST = lax.Precision.HIGHEST
SEGMENT_LIMIT = 512
REACH = (SEGMENT_LIMIT + ROWS - LANES) // LANES


def norm_factor(values):
    return lax.rsqrt(jnp.mean(values * values, axis=-1, keepdims=True) + EPSILON)


def distances(axis):
    return [1 << i for i in reversed(range(lax.axis_size(axis).bit_length() - 1))]


def exchange(rows, axis, distance):
    return lax.ppermute(rows, axis, [(i, i ^ distance) for i in range(lax.axis_size(axis))])


def is_high(axis, distance):
    return (lax.axis_index(axis) & distance) != 0


def swap_blocks(blocks):
    return lax.all_to_all(blocks, "expert", split_axis=0, concat_axis=0, tiled=True)


def after(value, *earlier):
    return lax.optimization_barrier((value, *earlier))[0]


def gather_rows(near):
    block = near[None]
    for distance in distances("dp"):
        other = exchange(block, "dp", distance)
        high = is_high("dp", distance)
        block = jnp.stack([jnp.where(high, other, block), jnp.where(high, block, other)], axis=1)
        block = block.reshape(-1, *near.shape)
    return block.reshape(-1, near.shape[-1])


def near_shards(shard):
    count = lax.axis_size("expert")
    return swap_blocks(jnp.broadcast_to(shard[None], (count, *shard.shape)))


def scatter_dp(rows):
    width = rows.shape[1]
    block = rows.reshape(lax.axis_size("dp"), -1, width)
    for distance in distances("dp")[::-1]:
        halves = block.reshape(block.shape[0] // 2, 2, -1, width)
        high = is_high("dp", distance).astype(jnp.int32)
        keep = lax.dynamic_index_in_dim(halves, high, 1, keepdims=False)
        send = lax.dynamic_index_in_dim(halves, 1 - high, 1, keepdims=False)
        block = keep + exchange(send.astype(bf16), "dp", distance).astype(f32)
    return block[0].astype(bf16)


def scatter_near(rows):
    parts = swap_blocks(rows.reshape(lax.axis_size("expert"), -1, rows.shape[1]))
    return jnp.sum(parts.astype(f32), axis=0)


def sum_all(rows):
    for axis in ("dp", "expert"):
        for distance in distances(axis)[::-1]:
            rows = rows + exchange(rows, axis, distance)
    return rows


def gelu_and_slope(values):
    root = 0.7978845608028654
    square = values * values
    share = 0.5 + 0.5 * jnp.tanh(values * (root + root * 0.044715 * square))
    unit = values * share
    slope = share + 2.0 * unit * (1.0 - share) * (root + 3.0 * root * 0.044715 * square)
    return unit, slope


def body(
    inputs,
    cotangent,
    attn_gain,
    qkv_weight,
    out_weight,
    ffn_gain,
    router_weight,
    rel_bias,
    expert_in,
    expert_out,
    routes,
    positions,
    dropped,
    segment_ids,
    valid_mask,
    buckets,
):
    seq_count, seq_length, model_width = inputs.shape
    tokens = seq_count * seq_length
    bucket_count, head_count = rel_bias.shape
    head_dim = model_width // head_count
    experts = router_weight.shape[1]
    capacity = 5 * tokens // (4 * experts)
    slots = experts * capacity
    me = lax.axis_index("expert")

    width = STEP_HEADS * head_dim
    steps = head_count // STEP_HEADS
    groups = [(0, steps - 1), (steps - 1, 1)]
    one_hot_buckets = (buckets[:, None] == jnp.arange(bucket_count, dtype=jnp.int32)[None, :]).astype(f32)
    head_bias = jnp.dot(one_hot_buckets, rel_bias, precision=HIGHEST, preferred_element_type=f32).T
    tiles = toeplitz_tiles(bias_windows(head_bias, REACH))
    one_hot_windows = bias_windows(one_hot_buckets.T, REACH)
    all_masks = [mask_columns(segment_ids[seq], valid_mask[seq]) for seq in range(seq_count)]
    near = []
    for blocks in spread_shard(
        qkv_weight, attn_gain, ffn_gain, router_weight, groups, width, lax.axis_size("expert")
    ):
        near.append(swap_blocks(after(blocks, *near[-1:])))
    near[0], tiles, all_masks = lax.optimization_barrier((near[0], tiles, all_masks))
    gathered = [gather_rows(block) for block in near]
    w_out = lax.all_gather(out_weight, ("dp", "expert"), axis=0, tiled=True)
    w_groups = [gathered[g][:, : 3 * many * width] for g, (first, many) in enumerate(groups)]
    small_all = gathered[0][:, w_groups[0].shape[1] :]
    gain_one = small_all[:, 0].astype(f32)
    gain_two = small_all[:, 1].astype(f32)

    slot_index = jnp.where(
        dropped.reshape(tokens) == 1, slots, routes.reshape(tokens) * capacity + positions.reshape(tokens)
    )
    place = (jnp.arange(slots, dtype=jnp.int32)[:, None] == slot_index[None, :]).astype(bf16)

    def fill_slots(rows):
        return jnp.dot(place, rows, preferred_element_type=f32).astype(bf16)

    def send_slots(rows):
        return swap_blocks(rows.reshape(experts, capacity, model_width)).reshape(slots, model_width)

    def read_slots(rows):
        return lax.dot_general(place, rows, (((0,), (0,)), ((), ())), preferred_element_type=f32)

    layer_in = inputs.astype(f32)

    saved = []
    for seq in range(seq_count):
        factor = norm_factor(layer_in[seq])
        normed = (layer_in[seq] * factor * gain_one).astype(bf16)
        masks = all_masks[seq]
        bounds = tile_bounds(segment_ids[seq])
        packs, lses = [], []
        mixed = jnp.zeros((seq_length, model_width), bf16)
        for g, (first, many) in enumerate(groups):
            packed = jnp.dot(normed, w_groups[g], preferred_element_type=f32).astype(bf16)
            mixed, lse = attend_forward(packed, *masks, bounds, tiles, mixed, first, head_dim)
            packs.append(packed)
            lses.append(lse)
        attn_out = jnp.dot(mixed, w_out, preferred_element_type=f32)
        saved.append((factor, normed, masks, bounds, packs, lses, mixed, attn_out))
    d_final_rows = send_slots(fill_slots(after(cotangent.reshape(tokens, model_width), saved[0][5][0], near[-1])))
    mid_rows = (layer_in + jnp.stack([state[-1] for state in saved])).reshape(tokens, model_width)
    mid_factor = norm_factor(mid_rows)
    mid_normed = mid_rows * mid_factor
    ffn_normed = (mid_normed * gain_two).astype(bf16)
    filled = fill_slots(ffn_normed)
    slot_rows = send_slots(filled)

    w_in, w_back = expert_in[0], expert_out[0]
    d_hidden = dot(after(d_final_rows, filled), w_back, NT).astype(bf16)
    slot_rows, d_hidden = lax.optimization_barrier((slot_rows, d_hidden))
    hidden, d_pre, d_rows, d_logits, gate = run_expert(me, slot_rows, w_in, small_all, d_hidden, experts)
    d_returned = send_slots(d_rows)

    moe_rows = (gate * dot(hidden, w_back, NN)).astype(bf16)
    d_slot_out = (gate * d_final_rows.astype(f32)).astype(bf16)
    grad_router = dot(slot_rows, d_logits, TN)[:, SMALL_GAINS : SMALL_GAINS + experts]
    part_in = dot(slot_rows, d_pre, TN).astype(bf16)
    part_out = dot(hidden, d_slot_out, TN).astype(bf16)
    grad_expert_in = lax.psum_scatter(part_in, "dp", scatter_dimension=1, tiled=True).astype(f32)[None]
    grad_expert_out = lax.psum_scatter(part_out, "dp", scatter_dimension=0, tiled=True).astype(f32)[None]
    d_returned, moe_rows, part_in, part_out = lax.optimization_barrier((d_returned, moe_rows, part_in, part_out))
    d_normed = read_slots(d_returned)
    moe_returned = send_slots(moe_rows)
    moe = read_slots(moe_returned)

    final_rows = mid_rows + moe
    output = final_rows.astype(bf16).reshape(inputs.shape)
    live_rows = valid_mask.reshape(tokens, 1).astype(f32)
    flat_in = layer_in.reshape(tokens, model_width)
    sums = jnp.stack(
        [jnp.sum(live_rows * rows * rows) for rows in (flat_in, mid_rows, final_rows)] + [jnp.sum(live_rows)]
    )

    weighted = d_normed * gain_two
    grad_gain_two = jnp.sum(d_normed * mid_normed, axis=0)
    d_mid = cotangent.astype(f32).reshape(tokens, model_width) + mid_factor * (
        weighted - mid_normed * jnp.mean(weighted * mid_normed, axis=-1, keepdims=True)
    )
    d_attn = d_mid.astype(bf16)
    d_mixed = dot(d_attn, w_out, NT).astype(bf16)
    mixed_all = jnp.concatenate([state[6] for state in saved], axis=0)
    grad_out = dot(mixed_all, d_attn, TN)
    out_half = scatter_dp(grad_out)

    diagonals, grad_groups, halves, dense_qkv = [], [], [], []
    d_normed_one = [jnp.zeros((seq_length, model_width), f32)] * seq_count
    for g, (first, many) in enumerate(groups):
        if g:
            d_mixed, out_half, moe_returned = lax.optimization_barrier((d_mixed, out_half, moe_returned))
            dense_out = scatter_near(out_half)
        grad_group, diagonal = None, None
        for seq in range(seq_count):
            factor, normed, masks, bounds, packs, lses, mixed, unused = saved[seq]
            parts, diagonal_seq = attend_backward(
                packs[g],
                d_mixed[seq * seq_length : (seq + 1) * seq_length],
                mixed,
                lses[g],
                *masks,
                bounds,
                tiles,
                first,
                head_dim,
            )
            if g:
                parts, dense_out, halves[0] = lax.optimization_barrier((parts, dense_out, halves[0]))
            here = dot(normed, parts, TN)
            grad_group = here if grad_group is None else grad_group + here
            diagonal = diagonal_seq if diagonal is None else diagonal + diagonal_seq
            d_normed_one[seq] = d_normed_one[seq] + dot(parts, w_groups[g], NT)
        diagonals.append(diagonal)
        halves.append(scatter_dp(grad_group))
    grad_parts = []
    for g, (first, many) in enumerate(groups):
        total = scatter_near(halves[g])
        grad_parts.append(total.reshape(-1, many, 3, width))
    grad_qkv = jnp.concatenate(grad_parts, axis=1).transpose(0, 2, 1, 3).reshape(-1, 3 * model_width)
    grad_gain_one = jnp.sum(grad_qkv * qkv_weight.astype(f32), axis=1) / attn_gain.astype(f32)

    input_grads = []
    for seq in range(seq_count):
        factor = saved[seq][0]
        normed_in = layer_in[seq] * factor
        weighted = d_normed_one[seq] * gain_one
        input_grads.append(
            d_mid[seq * seq_length : (seq + 1) * seq_length]
            + factor * (weighted - normed_in * jnp.mean(weighted * normed_in, axis=-1, keepdims=True))
        )
    input_grad = jnp.stack(input_grads)

    grad_rel = jnp.einsum("hgp,bgp->bh", jnp.concatenate(diagonals, axis=0), one_hot_windows, precision=HIGHEST)
    shares = [grad_rel, grad_gain_two, grad_router, sums]
    tail = jnp.concatenate([share.reshape(-1) for share in shares])
    tail = jnp.pad(tail, (0, -tail.shape[0] % (8 * LANES))).reshape(-1, LANES)
    tail = sum_all(tail).reshape(-1)
    ends = [0]
    for share in shares:
        ends.append(ends[-1] + share.size)
    grad_rel, grad_gain_two, grad_router, totals = [
        tail[ends[i] : ends[i + 1]].reshape(share.shape) for i, share in enumerate(shares)
    ]
    stats = jnp.sqrt(totals[:3] / (totals[3] * model_width))
    own_rows = attn_gain.shape[0]
    own_first = (lax.axis_index("dp") * lax.axis_size("expert") + me) * own_rows
    return (
        output,
        input_grad,
        grad_gain_one,
        grad_qkv,
        dense_out,
        lax.dynamic_slice_in_dim(grad_gain_two, own_first, own_rows),
        lax.dynamic_slice_in_dim(grad_router, own_first, own_rows),
        grad_rel,
        grad_expert_in,
        grad_expert_out,
        stats,
    )


def solution(mesh):
    in_specs = (
        P(("dp", "expert"), None, None),
        P(("dp", "expert"), None, None),
        P(("dp", "expert")),
        P(("dp", "expert"), None),
        P(("dp", "expert"), None),
        P(("dp", "expert")),
        P(("dp", "expert"), None),
        P(),
        P("expert", None, None),
        P("expert", None, None),
        P(("dp", "expert"), None),
        P(("dp", "expert"), None),
        P(("dp", "expert"), None),
        P(("dp", "expert"), None),
        P(("dp", "expert"), None),
        P(),
    )
    out_specs = (
        P(("dp", "expert"), None, None),
        P(("dp", "expert"), None, None),
        P(("dp", "expert")),
        P(("dp", "expert"), None),
        P(("dp", "expert"), None),
        P(("dp", "expert")),
        P(("dp", "expert"), None),
        P(),
        P("expert", None, "dp"),
        P("expert", "dp", None),
        P(),
    )
    return jax.shard_map(body, mesh=mesh, in_specs=in_specs, out_specs=out_specs, check_vma=False)
```

```python
import functools

import jax
import jax.numpy as jnp
from jax import lax
from jax.experimental import pallas as pl
from jax.experimental.pallas import tpu as pltpu
from jax.sharding import PartitionSpec as P

EPSILON = 1e-06
MASK_STEP = 1e30
ROWS = 256
LANES = 128
STEP_HEADS = 4
VMEM_BYTES = 60 * 2**20
SMALL_GAINS = 2
bf16, f32 = jnp.bfloat16, jnp.float32
NT = (((1,), (1,)), ((), ()))
NN = (((1,), (0,)), ((), ()))
TN = (((0,), (0,)), ((), ()))


def cost(microseconds):
    return pl.CostEstimate(flops=int(microseconds * 1.1e9), bytes_accessed=0, transcendentals=0)


def dot(left, right, dims):
    return lax.dot_general(left, right, dims, preferred_element_type=f32)


def offset_windows(values, reach):
    chunks = (values.shape[0] + 1) // LANES
    turned = jnp.pad(values[::-1], (1, 0)).reshape(chunks, LANES)
    middle = chunks // 2
    return jnp.stack(
        [jnp.concatenate([turned[middle - g], turned[middle - g - 1]]) for g in range(-reach, reach + 1)]
    )


def toeplitz_kernel(reach, window_ref, tile_ref):
    for g in range(2 * reach + 1):
        row = window_ref[0, g : g + 1, :]
        full = jnp.broadcast_to(row, (LANES, 2 * LANES))
        turned = pltpu.roll(full, 0, 1, stride=1, stride_axis=0)
        tile_ref[0, g * LANES : (g + 1) * LANES, :] = turned[:, :LANES]


def toeplitz_tiles(windows):
    heads, groups, width = windows.shape
    return pl.pallas_call(
        functools.partial(toeplitz_kernel, groups // 2),
        grid=(heads,),
        in_specs=[pl.BlockSpec((1, groups, width), lambda n: (n, 0, 0))],
        out_specs=pl.BlockSpec((1, groups * LANES, LANES), lambda n: (n, 0, 0)),
        out_shape=jax.ShapeDtypeStruct((heads, groups * LANES, LANES), f32),
        compiler_params=pltpu.CompilerParams(vmem_limit_bytes=VMEM_BYTES),
        cost_estimate=cost(9),
        name="toeplitz_tiles",
    )(windows)


def head_lanes(rows, head, head_dim):
    lane = lax.broadcasted_iota(jnp.int32, rows.shape, 1)
    return jnp.where((lane >= head * head_dim) & (lane < (head + 1) * head_dim), rows, jnp.zeros_like(rows))


def head_rows(columns, head, head_dim):
    row = lax.broadcasted_iota(jnp.int32, columns.shape, 0)
    return jnp.where((row >= head * head_dim) & (row < (head + 1) * head_dim), columns, jnp.zeros_like(columns))


def bias_tile(bias_ref, head, offset):
    parts = [
        bias_ref[head, pl.ds(pl.multiple_of(offset - LANES * part, LANES), ROWS), :]
        for part in range(ROWS // LANES)
    ]
    return jnp.concatenate(parts, axis=1)


def forward_kernel(head_dim, reach, low_ref, high_ref, q_ref, k_ref, v_ref, qx_ref, kx_ref, bias_ref, *refs):
    mix_ref, lse_ref, vt_ref = refs[-3:]
    length, width = q_ref.shape
    heads = width // head_dim
    scale = head_dim ** (-0.5)
    for c in range(width // LANES):
        vt_ref[c * LANES : (c + 1) * LANES, :] = v_ref[:, c * LANES : (c + 1) * LANES].T
    per = LANES // head_dim

    def one_block(qb, unused):
        first = pl.multiple_of(qb * ROWS, ROWS)
        qx = qx_ref[:, pl.ds(first, ROWS)]
        queries = []
        for c in range(width // LANES):
            pair = (q_ref[pl.ds(first, ROWS), c * LANES : (c + 1) * LANES] * jnp.asarray(scale, bf16)).T
            queries += [jnp.concatenate([head_rows(pair, h, head_dim), qx], axis=0) for h in range(per)]

        def one_tile(kb, carry):
            keys_at = pl.multiple_of(kb * ROWS, ROWS)
            offset = pl.multiple_of(keys_at - first + LANES * reach, LANES)
            kx = kx_ref[pl.ds(keys_at, ROWS), :]
            out = []
            all_scores = []
            for h in range(heads):
                c = h // per
                keys = jnp.concatenate([k_ref[pl.ds(keys_at, ROWS), c * LANES : (c + 1) * LANES], kx], axis=1)
                all_scores.append(dot(keys, queries[h], NN))
            soft = []
            for h in range(heads):
                peak, total, mixed = carry[h]
                scores = all_scores[h] + bias_tile(bias_ref, h, offset)
                new_peak = jnp.maximum(peak, jnp.max(scores, axis=0, keepdims=True))
                weights = jnp.exp(scores - new_peak)
                shrink = jnp.exp(peak - new_peak)
                total = total * shrink + jnp.sum(weights, axis=0, keepdims=True)
                soft.append((new_peak, total, shrink, weights.astype(bf16)))
            for h in range(heads):
                new_peak, total, shrink, weights = soft[h]
                values = vt_ref[h * head_dim : (h + 1) * head_dim, pl.ds(keys_at, ROWS)]
                mixed = carry[h][2] * shrink + dot(values, weights, NN)
                out.append((new_peak, total, mixed))
            return tuple(out)

        start = tuple(
            (jnp.full((1, ROWS), -3e38, f32), jnp.zeros((1, ROWS), f32), jnp.zeros((head_dim, ROWS), f32))
            for h in range(heads)
        )
        done = lax.fori_loop(low_ref[qb], high_ref[qb], one_tile, start)
        for c in range(width // LANES):
            rows = jnp.concatenate([done[h][2] / done[h][1] for h in range(c * per, (c + 1) * per)], axis=0)
            mix_ref[pl.ds(first, ROWS), c * LANES : (c + 1) * LANES] = rows.T.astype(bf16)
        for h in range(heads):
            lse_ref[0, h : h + 1, pl.ds(first, ROWS)] = done[h][0] + jnp.log(done[h][1])
        return unused

    lax.fori_loop(0, length // ROWS, one_block, 0)


def diagonal_sums(tiles):
    groups = tiles.shape[0]
    step = LANES // 2
    zero = jnp.zeros((groups, step, LANES), f32)
    turned = jnp.concatenate([tiles[:, :step], zero], axis=2) + pltpu.roll(
        jnp.concatenate([tiles[:, step:], zero], axis=2), 2 * LANES - step, 2
    )
    while step > 8:
        step //= 2
        turned = turned[:, :step] + pltpu.roll(turned[:, step:], 2 * LANES - step, 2)
    while step > 1:
        step //= 2
        turned = turned + pltpu.roll(pltpu.roll(turned, 2 * LANES - step, 2), 8 - step, 1)
    return turned[:, 0]


def backward_kernel(head_dim, reach, low_ref, high_ref, q_ref, k_ref, v_ref, dmix_ref, mix_ref, qx_ref, kx_ref, bias_ref, lse_ref,
                    grad_ref, diag_ref, kt_ref, dk_ref, dv_ref, along_ref):
    length, width = q_ref.shape
    heads = width // head_dim
    scale = head_dim ** (-0.5)
    per = LANES // head_dim
    for c in range(width // LANES):
        kt_ref[c * LANES : (c + 1) * LANES, :] = k_ref[:, c * LANES : (c + 1) * LANES].T
    dk_ref[...] = jnp.zeros_like(dk_ref)
    dv_ref[...] = jnp.zeros_like(dv_ref)
    along_ref[...] = jnp.zeros_like(along_ref)

    def one_block(qb, unused):
        first = pl.multiple_of(qb * ROWS, ROWS)
        qx = qx_ref[:, pl.ds(first, ROWS)]
        queries, d_mixes, deltas, wide, d_turned = [], [], [], [], []
        for c in range(width // LANES):
            lanes = slice(c * LANES, (c + 1) * LANES)
            query = q_ref[pl.ds(first, ROWS), lanes] * jnp.asarray(scale, bf16)
            d_mix = dmix_ref[pl.ds(first, ROWS), lanes]
            product = (d_mix.astype(f32) * mix_ref[pl.ds(first, ROWS), lanes].astype(f32)).T
            query_turned, d_mix_turned = query.T, d_mix.T
            for h in range(per):
                queries.append(head_lanes(query, h, head_dim))
                d_mixes.append(head_lanes(d_mix, h, head_dim))
                wide.append(jnp.concatenate([head_rows(query_turned, h, head_dim), qx], axis=0))
                d_turned.append(head_rows(d_mix_turned, h, head_dim))
                deltas.append(jnp.sum(product[h * head_dim : (h + 1) * head_dim], axis=0, keepdims=True))
        lses = [lse_ref[0, h : h + 1, pl.ds(first, ROWS)] for h in range(heads)]

        def one_tile(kb, carry):
            keys_at = pl.multiple_of(kb * ROWS, ROWS)
            offset = pl.multiple_of(keys_at - first + LANES * reach, LANES)
            kx = kx_ref[pl.ds(keys_at, ROWS), :]
            out = []
            low_weights, low_scores, all_scores, all_weights = [], [], [], []
            for h in range(heads):
                lanes = slice(h // per * LANES, (h // per + 1) * LANES)
                keys = jnp.concatenate([k_ref[pl.ds(keys_at, ROWS), lanes], kx], axis=1)
                all_scores.append(dot(keys, wide[h], NN))
            for h in range(heads):
                lanes = slice(h // per * LANES, (h // per + 1) * LANES)
                all_weights.append(dot(v_ref[pl.ds(keys_at, ROWS), lanes], d_turned[h], NN))
            for h in range(heads):
                weights = jnp.exp(all_scores[h] + bias_tile(bias_ref, h, offset) - lses[h])
                d_scores = weights * (all_weights[h] - deltas[h])
                for part in range(ROWS // LANES):
                    at = pl.ds(pl.multiple_of(offset - LANES * part, LANES), ROWS)
                    along_ref[h, at, :] += d_scores[:, part * LANES : (part + 1) * LANES]
                low_weights.append(weights.astype(bf16))
                low_scores.append(d_scores.astype(bf16))
            for h in range(heads):
                keys_turned = kt_ref[h * head_dim : (h + 1) * head_dim, pl.ds(keys_at, ROWS)]
                out.append(carry[h] + dot(keys_turned, low_scores[h], NN))
            for c in range(width // LANES):
                mine = range(c * per, (c + 1) * per)
                lanes = slice(c * LANES, (c + 1) * LANES)
                dv_ref[pl.ds(keys_at, ROWS), lanes] += dot(
                    jnp.concatenate([low_weights[h] for h in mine], axis=1), jnp.concatenate([d_mixes[h] for h in mine], axis=0), NN)
                dk_ref[pl.ds(keys_at, ROWS), lanes] += dot(
                    jnp.concatenate([low_scores[h] for h in mine], axis=1), jnp.concatenate([queries[h] for h in mine], axis=0), NN)
            return tuple(out)

        start = tuple(jnp.zeros((head_dim, ROWS), f32) for h in range(heads))
        done = lax.fori_loop(low_ref[qb], high_ref[qb], one_tile, start)
        for c in range(width // LANES):
            rows = jnp.concatenate([done[h] for h in range(c * per, (c + 1) * per)], axis=0) * scale
            grad_ref[pl.ds(first, ROWS), c * LANES : (c + 1) * LANES] = rows.T.astype(bf16)
        return unused

    lax.fori_loop(0, length // ROWS, one_block, 0)
    grad_ref[:, width : 2 * width] = dk_ref[...].astype(bf16)
    grad_ref[:, 2 * width :] = dv_ref[...].astype(bf16)
    for h in range(heads):
        diag_ref[h] = diagonal_sums(along_ref[h].reshape(2 * reach + 1, LANES, LANES))


def tile_bounds(segments):
    length = segments.shape[0]
    blocks = segments.reshape(length // ROWS, ROWS)
    starts = jnp.sum((segments[None, :] < blocks[:, :1]).astype(jnp.int32), axis=1)
    ends = jnp.sum((segments[None, :] <= blocks[:, -1:]).astype(jnp.int32), axis=1)
    return starts // ROWS, (ends + ROWS - 1) // ROWS


def mask_columns(segments, validity, segment_count=8):
    length = segments.shape[0]
    short = 1
    while short * (short + 1) < length:
        short += 1
    at = jnp.arange(length, dtype=jnp.int32)
    lane = jnp.arange(LANES, dtype=jnp.int32)[None, :]
    in_first = (lane >= segment_count) & (lane < segment_count + short)
    in_second = (lane >= segment_count + short) & (lane < segment_count + 2 * short + 1)
    mine = (
        (lane == segments[:, None])
        | (in_first & (lane - segment_count == (at % short)[:, None]))
        | (in_second & (lane - segment_count - short == (at % (short + 1))[:, None]))
    )
    used = lane < segment_count + 2 * short + 1
    query_side = jnp.where(used & ~mine, -MASK_STEP, 0.0).astype(bf16).T
    real = (validity == 1)[:, None]
    key_side = jnp.where(mine & jnp.where(real, lane < segment_count, lane >= segment_count), 1.0, 0.0).astype(bf16)
    return query_side, key_side


def attend_forward(packed, query_side, key_side, bounds, tiles, mixed, first, head_dim):
    length = packed.shape[0]
    width = STEP_HEADS * head_dim
    steps = packed.shape[1] // 3 // width
    reach = tiles.shape[1] // LANES // 2
    shared = [] if mixed is None else [mixed]
    whole = lambda *_: (0, 0)
    grid_spec = pltpu.PrefetchScalarGridSpec(
        num_scalar_prefetch=2,
        grid=(steps,),
        in_specs=[
            pl.BlockSpec((length, width), lambda p, *_: (0, 3 * p)),
            pl.BlockSpec((length, width), lambda p, *_: (0, 3 * p + 1)),
            pl.BlockSpec((length, width), lambda p, *_: (0, 3 * p + 2)),
            pl.BlockSpec((LANES, length), whole),
            pl.BlockSpec((length, LANES), whole),
            pl.BlockSpec((STEP_HEADS, tiles.shape[1], LANES), lambda p, *_: (first + p, 0, 0)),
        ]
        + [pl.BlockSpec(memory_space=pl.ANY)] * len(shared),
        out_specs=[
            pl.BlockSpec((length, width), lambda p, *_: (0, first + p)),
            pl.BlockSpec((1, STEP_HEADS, length), lambda p, *_: (p, 0, 0)),
        ],
        scratch_shapes=[pltpu.VMEM((width, length), bf16)],
    )
    return pl.pallas_call(
        functools.partial(forward_kernel, head_dim, reach),
        grid_spec=grid_spec,
        out_shape=[
            jax.ShapeDtypeStruct((length, tiles.shape[0] * head_dim), bf16),
            jax.ShapeDtypeStruct((steps, STEP_HEADS, length), f32),
        ],
        input_output_aliases={8: 0} if shared else {},
        compiler_params=pltpu.CompilerParams(vmem_limit_bytes=56 * 2**20),
        cost_estimate=cost(1),
        name="attend_forward",
    )(*bounds, packed, packed, packed, query_side, key_side, tiles, *shared)


def attend_backward(packed, d_mix, mix, lse, query_side, key_side, bounds, tiles, first, head_dim):
    length = packed.shape[0]
    width = STEP_HEADS * head_dim
    steps = packed.shape[1] // 3 // width
    reach = tiles.shape[1] // LANES // 2
    groups = 2 * reach + 1
    whole = lambda *_: (0, 0)
    grid_spec = pltpu.PrefetchScalarGridSpec(
        num_scalar_prefetch=2,
        grid=(steps,),
        in_specs=[
            pl.BlockSpec((length, width), lambda p, *_: (0, 3 * p)),
            pl.BlockSpec((length, width), lambda p, *_: (0, 3 * p + 1)),
            pl.BlockSpec((length, width), lambda p, *_: (0, 3 * p + 2)),
            pl.BlockSpec((length, width), lambda p, *_: (0, first + p)),
            pl.BlockSpec((length, width), lambda p, *_: (0, first + p)),
            pl.BlockSpec((LANES, length), whole),
            pl.BlockSpec((length, LANES), whole),
            pl.BlockSpec((STEP_HEADS, tiles.shape[1], LANES), lambda p, *_: (first + p, 0, 0)),
            pl.BlockSpec((1, STEP_HEADS, length), lambda p, *_: (p, 0, 0)),
        ],
        out_specs=[
            pl.BlockSpec((length, 3 * width), lambda p, *_: (0, p)),
            pl.BlockSpec((STEP_HEADS, groups, 2 * LANES), lambda p, *_: (p, 0, 0)),
        ],
        scratch_shapes=[
            pltpu.VMEM((width, length), bf16),
            pltpu.VMEM((length, width), f32),
            pltpu.VMEM((length, width), f32),
            pltpu.VMEM((STEP_HEADS, groups * LANES, LANES), f32),
        ],
    )
    work = steps * STEP_HEADS * length * length
    return pl.pallas_call(
        functools.partial(backward_kernel, head_dim, reach),
        grid_spec=grid_spec,
        out_shape=[
            jax.ShapeDtypeStruct((length, 3 * width * steps), bf16),
            jax.ShapeDtypeStruct((steps * STEP_HEADS, groups, 2 * LANES), f32),
        ],
        compiler_params=pltpu.CompilerParams(vmem_limit_bytes=56 * 2**20),
        cost_estimate=cost(20 * steps),
        name="attend_backward",
    )(*bounds, packed, packed, packed, d_mix, mix, query_side, key_side, tiles, lse)


def spread_kernel(width, near_steps, weight_ref, out_weight_ref, first_ref, second_ref, router_ref, *outs):
    receivers, count = outs[0].shape[:2]
    steps = weight_ref.shape[1] // (3 * width)
    row = lax.broadcasted_iota(jnp.int32, (count, count), 0)
    same = row == lax.broadcasted_iota(jnp.int32, (count, count), 1)
    columns = [
        jnp.sum(jnp.where(same, jnp.broadcast_to(ref[...].astype(f32), same.shape), 0.0), axis=1, keepdims=True)
        for ref in (first_ref, second_ref)
    ]
    columns.append(router_ref[...].astype(f32))
    used = SMALL_GAINS + router_ref.shape[1]
    columns.append(jnp.zeros((count, -used % LANES), f32))
    pieces = [
        weight_ref[:, (part * steps + p) * width : (part * steps + p + 1) * width] for p in range(steps) for part in range(3)
    ]
    groups = [
        pieces[: 3 * near_steps] + [jnp.concatenate(columns, axis=1).astype(bf16)],
        pieces[3 * near_steps :] + [out_weight_ref[...]],
    ]
    for group, out_ref in zip(groups, outs):
        at = 0
        for piece in group:
            out_ref[:, :, at : at + piece.shape[1]] = jnp.broadcast_to(piece[None], (receivers, *piece.shape))
            at += piece.shape[1]


def spread_shard(weight, out_weight, first_gain, second_gain, router, width, near_steps, receivers):
    rows, columns = weight.shape
    small = SMALL_GAINS + router.shape[1]
    small += -small % LANES
    near = 3 * width * near_steps
    return pl.pallas_call(
        functools.partial(spread_kernel, width, near_steps),
        out_shape=[
            jax.ShapeDtypeStruct((receivers, rows, near + small), bf16),
            jax.ShapeDtypeStruct((receivers, rows, columns - near + out_weight.shape[1]), bf16),
        ],
        compiler_params=pltpu.CompilerParams(vmem_limit_bytes=VMEM_BYTES),
        cost_estimate=cost(2),
        name="spread_shard",
    )(weight, out_weight, first_gain.reshape(1, rows), second_gain.reshape(1, rows), router)


def expert_kernel(experts, me_ref, rows_ref, in_ref, small_ref, d_hidden_ref, hidden_ref, d_pre_ref, d_rows_ref, d_logits_ref, gate_ref,
                  probs_ref, total_ref, d_gate_ref):
    step = pl.program_id(0)
    lane = lax.broadcasted_iota(jnp.int32, probs_ref.shape, 1)
    chosen = lane == me_ref[0] + SMALL_GAINS

    @pl.when(step == 0)
    def _():
        logits = dot(rows_ref[...], small_ref[...], NN)
        logits = jnp.where((lane >= SMALL_GAINS) & (lane < SMALL_GAINS + experts), logits, -MASK_STEP)
        raised = jnp.exp(logits - jnp.max(logits, axis=1, keepdims=True))
        probs = raised / jnp.sum(raised, axis=1, keepdims=True)
        probs_ref[...] = probs
        gate_ref[...] = jnp.sum(jnp.where(chosen, probs, 0.0), axis=1, keepdims=True)
        total_ref[...] = jnp.zeros_like(total_ref)
        d_gate_ref[...] = jnp.zeros_like(d_gate_ref)

    count = rows_ref.shape[0]
    chunk = 256 if count % 256 == 0 else count
    weights = in_ref[...]
    pres = [dot(rows_ref[at : at + chunk], weights, NN) for at in range(0, count, chunk)]
    lows = []
    for i, at in enumerate(range(0, count, chunk)):
        here = slice(at, at + chunk)
        unit, slope = gelu_and_slope(pres[i])
        hidden = unit.astype(bf16)
        d_hidden = d_hidden_ref[here].astype(f32)
        hidden_ref[here] = hidden
        d_gate_ref[here] += jnp.sum(unit * d_hidden, axis=1, keepdims=True)
        low = (gate_ref[here] * d_hidden * slope).astype(bf16)
        d_pre_ref[here] = low
        lows.append(low)
    for i, at in enumerate(range(0, count, chunk)):
        total_ref[at : at + chunk] += dot(lows[i], weights, NT)

    @pl.when(step == pl.num_programs(0) - 1)
    def _():
        d_logits = (probs_ref[...] * (chosen.astype(f32) - gate_ref[...]) * d_gate_ref[...]).astype(bf16)
        d_logits_ref[...] = d_logits
        d_rows_ref[...] = (total_ref[...] + dot(d_logits, small_ref[...], NT)).astype(bf16)


def run_expert(me, rows, w_in, weights, small_at, d_hidden, experts):
    count, width = rows.shape
    hidden_width = w_in.shape[1]
    block = 512
    row_blocks = pl.BlockSpec((count, block), lambda f, *_: (0, f))
    whole = lambda f, *_: (0, 0)
    grid_spec = pltpu.PrefetchScalarGridSpec(
        num_scalar_prefetch=1,
        grid=(hidden_width // block,),
        in_specs=[
            pl.BlockSpec((count, width), whole),
            pl.BlockSpec((width, block), lambda f, *_: (0, f)),
            pl.BlockSpec((width, LANES), lambda f, *_: (0, small_at)),
            row_blocks,
        ],
        out_specs=[
            row_blocks,
            row_blocks,
            pl.BlockSpec((count, width), whole),
            pl.BlockSpec((count, LANES), whole),
            pl.BlockSpec((count, 1), whole),
        ],
        scratch_shapes=[pltpu.VMEM((count, LANES), f32), pltpu.VMEM((count, width), f32), pltpu.VMEM((count, 1), f32)],
    )
    return pl.pallas_call(
        functools.partial(expert_kernel, experts),
        grid_spec=grid_spec,
        out_shape=[
            jax.ShapeDtypeStruct((count, hidden_width), bf16),
            jax.ShapeDtypeStruct((count, hidden_width), bf16),
            jax.ShapeDtypeStruct((count, width), bf16),
            jax.ShapeDtypeStruct((count, LANES), bf16),
            jax.ShapeDtypeStruct((count, 1), f32),
        ],
        compiler_params=pltpu.CompilerParams(vmem_limit_bytes=VMEM_BYTES),
        cost_estimate=cost(25),
        name="run_expert",
    )(me.reshape(1), rows, w_in, weights, d_hidden)


def expert_grads_kernel(gate_ref, rows_ref, hidden_ref, d_pre_ref, d_slots_ref, back_ref, d_logits_ref, part_in_ref, part_out_ref,
                        moe_ref, router_ref, turned_ref, d_out_ref, total_ref):
    step = pl.program_id(0)

    @pl.when(step == 0)
    def _():
        turned_ref[...] = rows_ref[...].T
        d_out_ref[...] = (gate_ref[...] * d_slots_ref[...].astype(f32)).astype(bf16)
        total_ref[...] = jnp.zeros_like(total_ref)
        router_ref[...] = dot(turned_ref[...], d_logits_ref[...], NN)

    hidden = hidden_ref[...]
    part_in_ref[...] = dot(turned_ref[...], d_pre_ref[...], NN).astype(bf16)
    part_out_ref[...] = dot(hidden, d_out_ref[...], TN).astype(bf16)
    total_ref[...] += dot(hidden, back_ref[...], NN)

    @pl.when(step == pl.num_programs(0) - 1)
    def _():
        moe_ref[...] = (gate_ref[...] * total_ref[...]).astype(bf16)


def expert_grads(gate, rows, hidden, d_pre, d_slots, w_back, d_logits):
    count, width = rows.shape
    hidden_width = hidden.shape[1]
    block = 512
    whole = lambda f: (0, 0)
    row_blocks = pl.BlockSpec((count, block), lambda f: (0, f))
    full = pl.BlockSpec((count, width), whole)
    return pl.pallas_call(
        expert_grads_kernel,
        grid=(hidden_width // block,),
        in_specs=[
            pl.BlockSpec((count, 1), whole),
            full,
            row_blocks,
            row_blocks,
            full,
            pl.BlockSpec((block, width), lambda f: (f, 0)),
            pl.BlockSpec((count, LANES), whole),
        ],
        out_specs=[
            pl.BlockSpec((width, block), lambda f: (0, f)),
            pl.BlockSpec((block, width), lambda f: (f, 0)),
            full,
            pl.BlockSpec((width, LANES), whole),
        ],
        out_shape=[
            jax.ShapeDtypeStruct((width, hidden_width), bf16),
            jax.ShapeDtypeStruct((hidden_width, width), bf16),
            jax.ShapeDtypeStruct((count, width), bf16),
            jax.ShapeDtypeStruct((width, LANES), f32),
        ],
        scratch_shapes=[pltpu.VMEM((width, count), bf16), pltpu.VMEM((count, width), bf16), pltpu.VMEM((count, width), f32)],
        compiler_params=pltpu.CompilerParams(vmem_limit_bytes=VMEM_BYTES),
        cost_estimate=cost(27),
        name="expert_grads",
    )(gate, rows, hidden, d_pre, d_slots, w_back, d_logits)


def row_factor(rows):
    return lax.rsqrt(jnp.mean(rows * rows, axis=1, keepdims=True) + EPSILON)


def middle_kernel(row_steps, mixed_ref, weight_ref, in_ref, gain_ref, slot_ref, rows_ref, slots_ref, normed_ref):
    step = pl.program_id(0)

    @pl.when(step < row_steps)
    def _():
        count = in_ref.shape[0]
        first = pl.multiple_of(step * count, count)
        chunks = [slice(at, at + ROWS) for at in range(0, count, ROWS)]
        gain = gain_ref[...]
        projected = [dot(mixed_ref[here], weight_ref[...], NN) for here in chunks]
        for here, attn in zip(chunks, projected):
            rows = in_ref[here].astype(f32) + attn
            rows_ref[here] = rows
            normed_ref[pl.ds(first + here.start, ROWS)] = (rows * row_factor(rows) * gain).astype(bf16)

    @pl.when(step >= row_steps)
    def _():
        fill_kernel(slot_ref, normed_ref, slots_ref, (step - row_steps) * slots_ref.shape[0])


def fill_kernel(slot_ref, rows_ref, slots_ref, first=0):
    slots, count = slots_ref.shape[0], rows_ref.shape[0]
    chunk = ROWS if slots % ROWS == 0 else slots
    for at in range(0, slots, chunk):
        slot = lax.broadcasted_iota(jnp.int32, (chunk, count), 0) + (first + at)
        place = jnp.where(slot == slot_ref[...], 1.0, 0.0).astype(bf16)
        slots_ref[at : at + chunk] = dot(place, rows_ref[...], NN).astype(bf16)


def read_slots(slot_ref, here, blocks_ref):
    slots = blocks_ref.shape[0]
    slot = lax.broadcasted_iota(jnp.int32, (ROWS, slots), 1)
    place = jnp.where(slot == slot_ref[here], 1.0, 0.0).astype(bf16)
    return dot(place, blocks_ref[...], NN)


def fill_slots(slot_row, rows, slots):
    return pl.pallas_call(
        fill_kernel,
        out_shape=jax.ShapeDtypeStruct((slots, rows.shape[1]), bf16),
        compiler_params=pltpu.CompilerParams(vmem_limit_bytes=VMEM_BYTES),
        cost_estimate=cost(3.5),
        name="fill_slots",
    )(slot_row, rows)


def run_middle(mixed, weights, at, rows_in, gain, slot_row, slots):
    count, width = rows_in.shape
    whole = lambda i: (0, 0)
    row_steps = 2 if count % (2 * ROWS) == 0 else 1
    slot_steps = 2 if slots % 32 == 0 else 1
    part = pl.BlockSpec((count // row_steps, width), lambda i: (jnp.minimum(i, row_steps - 1), 0))
    return pl.pallas_call(
        functools.partial(middle_kernel, row_steps),
        grid=(row_steps + slot_steps,),
        in_specs=[
            part,
            pl.BlockSpec((width, width), lambda i: (0, at)),
            part,
            pl.BlockSpec((1, width), whole),
            pl.BlockSpec((1, count), whole),
        ],
        out_specs=[part, pl.BlockSpec((slots // slot_steps, width), lambda i: (jnp.maximum(i - row_steps, 0), 0))],
        out_shape=[jax.ShapeDtypeStruct((count, width), f32), jax.ShapeDtypeStruct((slots, width), bf16)],
        scratch_shapes=[pltpu.VMEM((count, width), bf16)],
        compiler_params=pltpu.CompilerParams(vmem_limit_bytes=VMEM_BYTES),
        cost_estimate=cost(5),
        name="run_middle",
    )(mixed, weights, rows_in, gain, slot_row)


def middle_back_kernel(blocks_ref, slot_ref, rows_ref, gain_ref, top_ref, weight_ref, d_mid_ref, d_attn_ref, d_mixed_ref, d_gain_ref):
    gain = gain_ref[...]
    d_normed = read_slots(slot_ref, slice(None), blocks_ref)
    rows = rows_ref[...]
    factor = row_factor(rows)
    normed = rows * factor
    weighted = d_normed * gain
    product = d_normed * normed
    d_mid = top_ref[...].astype(f32) + factor * (weighted - normed * jnp.mean(product * gain, axis=1, keepdims=True))
    d_mid_ref[...] = d_mid
    d_attn = d_mid.astype(bf16)
    d_attn_ref[...] = d_attn
    d_mixed_ref[...] = dot(d_attn, weight_ref[...], NT).astype(bf16)

    @pl.when(pl.program_id(0) == 0)
    def _():
        d_gain_ref[...] = jnp.zeros_like(d_gain_ref)

    d_gain_ref[...] += jnp.sum(product, axis=0, keepdims=True)


def run_middle_back(blocks, slot_column, rows, gain, top, weights, at):
    count, width = rows.shape
    whole = lambda *_: (0, 0)
    part = pl.BlockSpec((ROWS, width), lambda i: (i, 0))
    return pl.pallas_call(
        middle_back_kernel,
        grid=(count // ROWS,),
        in_specs=[
            pl.BlockSpec(blocks.shape, whole),
            pl.BlockSpec((ROWS, 1), lambda i: (i, 0)),
            part,
            pl.BlockSpec((1, width), whole),
            part,
            pl.BlockSpec((width, width), lambda i: (0, at)),
        ],
        out_specs=[part, part, part, pl.BlockSpec((1, width), whole)],
        out_shape=[
            jax.ShapeDtypeStruct((count, width), f32),
            jax.ShapeDtypeStruct((count, width), bf16),
            jax.ShapeDtypeStruct((count, width), bf16),
            jax.ShapeDtypeStruct((1, width), f32),
        ],
        compiler_params=pltpu.CompilerParams(vmem_limit_bytes=VMEM_BYTES),
        cost_estimate=cost(7),
        name="run_middle_back",
    )(blocks, slot_column, rows, gain, top, weights)


def first_back_kernel(count, in_ref, gain_ref, d_mid_ref, *refs):
    d_in_ref = refs[2 * count]
    total = 0.0
    for part_ref, weight_ref in zip(refs[:count], refs[count:]):
        total = total + dot(part_ref[...], weight_ref[:, : part_ref.shape[1]], NT)
    rows = in_ref[...].astype(f32)
    factor = row_factor(rows)
    normed = rows * factor
    weighted = total * gain_ref[...]
    d_in_ref[...] = d_mid_ref[...] + factor * (weighted - normed * jnp.mean(weighted * normed, axis=1, keepdims=True))


def run_first_back(rows_in, gain, d_mid, parts, weights):
    count, width = rows_in.shape
    whole = lambda *_: (0, 0)
    part = pl.BlockSpec((ROWS, width), lambda i: (i, 0))
    return pl.pallas_call(
        functools.partial(first_back_kernel, len(parts)),
        grid=(count // ROWS,),
        in_specs=[part, pl.BlockSpec((1, width), whole), part]
        + [pl.BlockSpec((ROWS, columns.shape[1]), lambda i: (i, 0)) for columns in parts]
        + [pl.BlockSpec(weight.shape, whole) for weight in weights],
        out_specs=part,
        out_shape=jax.ShapeDtypeStruct(rows_in.shape, f32),
        compiler_params=pltpu.CompilerParams(vmem_limit_bytes=VMEM_BYTES),
        cost_estimate=cost(8),
        name="run_first_back",
    )(rows_in, gain, d_mid, *parts, *weights)


def output_kernel(blocks_ref, slot_ref, rows_ref, in_ref, live_ref, out_ref, sums_ref):
    rows = rows_ref[...]
    final = rows + read_slots(slot_ref, slice(None), blocks_ref)
    out_ref[...] = final.astype(bf16)
    live = live_ref[...]
    lane = lax.broadcasted_iota(jnp.int32, (1, LANES), 1)
    sums = jnp.where(lane == 3, jnp.sum(live, axis=0, keepdims=True), 0.0)
    for i, part in enumerate((in_ref[...].astype(f32), rows, final)):
        per_row = live * jnp.sum(part * part, axis=1, keepdims=True)
        sums = jnp.where(lane == i, jnp.sum(per_row, axis=0, keepdims=True), sums)

    @pl.when(pl.program_id(0) == 0)
    def _():
        sums_ref[...] = jnp.zeros_like(sums_ref)

    sums_ref[...] += sums


def run_output(blocks, slot_column, rows, rows_in, live):
    count, width = rows.shape
    whole = lambda *_: (0, 0)
    part = pl.BlockSpec((ROWS, width), lambda i: (i, 0))
    column = pl.BlockSpec((ROWS, 1), lambda i: (i, 0))
    return pl.pallas_call(
        output_kernel,
        grid=(count // ROWS,),
        in_specs=[pl.BlockSpec(blocks.shape, whole), column, part, part, column],
        out_specs=[part, pl.BlockSpec((1, LANES), whole)],
        out_shape=[jax.ShapeDtypeStruct((count, width), bf16), jax.ShapeDtypeStruct((1, LANES), f32)],
        compiler_params=pltpu.CompilerParams(vmem_limit_bytes=VMEM_BYTES),
        cost_estimate=cost(4),
        name="run_output",
    )(blocks, slot_column, rows, rows_in, live)


def out_grad_kernel(mixed_ref, d_attn_ref, router_ref, gain_ref, grad_ref):
    width = mixed_ref.shape[1]
    grad_ref[:, :width] = dot(mixed_ref[...], d_attn_ref[...], TN)
    column = jnp.broadcast_to(gain_ref[...], (LANES, width)).T
    lane = lax.broadcasted_iota(jnp.int32, column.shape, 1)
    grad_ref[:, width:] = jnp.where(lane == 1, column, router_ref[...])


def run_out_grad(mixed, d_attn, grad_router, grad_gain):
    width = mixed.shape[1]
    return pl.pallas_call(
        out_grad_kernel,
        out_shape=jax.ShapeDtypeStruct((width, width + LANES), f32),
        compiler_params=pltpu.CompilerParams(vmem_limit_bytes=VMEM_BYTES),
        cost_estimate=cost(3),
        name="run_out_grad",
    )(mixed, d_attn, grad_router, grad_gain)


def widen_kernel(*refs):
    half = len(refs) // 2
    for in_ref, out_ref in zip(refs[:half], refs[half:]):
        out_ref[...] = in_ref[...].astype(f32)


def widen(*arrays):
    rows, columns = arrays[0].shape
    part = pl.BlockSpec((rows // 3, columns), lambda i: (i, 0))
    return pl.pallas_call(
        widen_kernel,
        grid=(3,),
        in_specs=[part] * len(arrays),
        out_specs=[part] * len(arrays),
        out_shape=[jax.ShapeDtypeStruct(array.shape, f32) for array in arrays],
        cost_estimate=cost(2),
        name="widen",
    )(*arrays)


def project_kernel(in_ref, gain_ref, weight_ref, packed_ref, normed_ref):
    rows = in_ref[...].astype(f32)
    normed = (rows * row_factor(rows) * gain_ref[...]).astype(bf16)
    normed_ref[...] = normed
    packed_ref[...] = dot(normed, weight_ref[...], NN).astype(bf16)


def run_project(rows_in, gain, weights, columns):
    count, width = rows_in.shape
    whole = lambda i: (0, 0)
    return pl.pallas_call(
        project_kernel,
        grid=(count // ROWS,),
        in_specs=[
            pl.BlockSpec((ROWS, width), lambda i: (i, 0)),
            pl.BlockSpec((1, width), whole),
            pl.BlockSpec((width, columns), whole),
        ],
        out_specs=[pl.BlockSpec((ROWS, columns), lambda i: (i, 0)), pl.BlockSpec((ROWS, width), lambda i: (i, 0))],
        out_shape=[jax.ShapeDtypeStruct((count, columns), bf16), jax.ShapeDtypeStruct((count, width), bf16)],
        compiler_params=pltpu.CompilerParams(vmem_limit_bytes=VMEM_BYTES),
        cost_estimate=cost(4),
        name="run_project",
    )(rows_in, gain, weights)


HIGHEST = lax.Precision.HIGHEST
SEGMENT_LIMIT = 512
REACH = (SEGMENT_LIMIT + ROWS - LANES) // LANES


def norm_factor(values):
    return lax.rsqrt(jnp.mean(values * values, axis=-1, keepdims=True) + EPSILON)


def distances(axis):
    return [1 << i for i in reversed(range(lax.axis_size(axis).bit_length() - 1))]


def exchange(rows, axis, distance):
    return lax.ppermute(rows, axis, [(i, i ^ distance) for i in range(lax.axis_size(axis))])


def is_high(axis, distance):
    return (lax.axis_index(axis) & distance) != 0


def swap_blocks(blocks):
    return lax.all_to_all(blocks, "expert", split_axis=0, concat_axis=0, tiled=True)


def after(value, *earlier):
    return lax.optimization_barrier((value, *earlier))[0]


def both(mine, other, axis, distance, at=0):
    high = is_high(axis, distance)
    return jnp.stack([jnp.where(high, other, mine), jnp.where(high, mine, other)], axis=at)


def start_gather(near):
    return near[None], exchange(near[None], "dp", distances("dp")[0])


def finish_gather(terms):
    block, other = terms
    shape = block.shape[1:]
    for distance in distances("dp"):
        if other is None:
            other = exchange(block, "dp", distance)
        block = both(block, other, "dp", distance, 1).reshape(-1, *shape)
        other = None
    return block.reshape(-1, shape[-1])


def scatter_dp(rows):
    width = rows.shape[1]
    block = rows.reshape(lax.axis_size("dp"), -1, width)
    order = distances("dp")[::-1]
    for distance in order:
        halves = block.reshape(block.shape[0] // 2, 2, -1, width)
        high = is_high("dp", distance).astype(jnp.int32)
        keep = lax.dynamic_index_in_dim(halves, high, 1, keepdims=False)
        send = lax.dynamic_index_in_dim(halves, 1 - high, 1, keepdims=False)
        received = exchange(send.astype(bf16), "dp", distance)
        if distance != order[-1]:
            block = keep + received.astype(f32)
    return keep, received


def finish_dp(terms):
    keep, received = terms
    return (keep + received.astype(f32))[0].astype(bf16)


def join(parts):
    return parts[0] if len(parts) == 1 else jnp.concatenate(parts, axis=0)


def near_parts(rows):
    return swap_blocks(rows.reshape(lax.axis_size("expert"), -1, rows.shape[1]))


def gelu_and_slope(values):
    root = 0.7978845608028654
    square = values * values
    share = 0.5 + 0.5 * jnp.tanh(values * (root + root * 0.044715 * square))
    unit = values * share
    slope = share + 2.0 * unit * (1.0 - share) * (root + 3.0 * root * 0.044715 * square)
    return unit, slope


def body(
    inputs,
    cotangent,
    attn_gain,
    qkv_weight,
    out_weight,
    ffn_gain,
    router_weight,
    rel_bias,
    expert_in,
    expert_out,
    routes,
    positions,
    dropped,
    segment_ids,
    valid_mask,
    buckets,
):
    seq_count, seq_length, model_width = inputs.shape
    tokens = seq_count * seq_length
    bucket_count, head_count = rel_bias.shape
    head_dim = model_width // head_count
    experts = router_weight.shape[1]
    capacity = 5 * tokens // (4 * experts)
    slots = experts * capacity
    me = lax.axis_index("expert")

    width = STEP_HEADS * head_dim
    steps = head_count // STEP_HEADS
    groups = [(0, steps - 1), (steps - 1, 1)]
    small_at = 3 * (steps - 1) * width // LANES
    out_at = 3 * width // model_width

    bucket_windows = offset_windows(buckets, REACH)
    one_hot_windows = (bucket_windows[..., None] == jnp.arange(bucket_count, dtype=jnp.int32)).astype(f32)
    windows = jnp.einsum("gpb,bh->hgp", one_hot_windows, rel_bias, precision=HIGHEST)
    tiles = toeplitz_tiles(windows)
    all_masks = [mask_columns(segment_ids[seq], valid_mask[seq]) for seq in range(seq_count)]
    slot_index = jnp.where(
        dropped.reshape(tokens) == 1, slots, routes.reshape(tokens) * capacity + positions.reshape(tokens)
    )
    slot_row, slot_column = slot_index.reshape(1, tokens), slot_index.reshape(tokens, 1)
    live = valid_mask.reshape(tokens, 1).astype(f32)
    rows_in = inputs.reshape(tokens, model_width)
    top = cotangent.reshape(tokens, model_width)

    def send_slots(rows):
        return swap_blocks(rows.reshape(experts, capacity, model_width)).reshape(slots, model_width)

    near, rest = spread_shard(
        qkv_weight, out_weight, attn_gain, ffn_gain, router_weight, width, steps - 1, lax.axis_size("expert")
    )
    near = swap_blocks(near)
    near, rest, tiles, all_masks = lax.optimization_barrier((near, rest, tiles, all_masks))
    rest = swap_blocks(rest)
    filled_cotangent = fill_slots(slot_row, top, slots)
    terms = start_gather(near)
    terms, filled_cotangent, rest = lax.optimization_barrier((terms, filled_cotangent, rest))
    weights = [finish_gather(terms)]
    small = weights[0][:, small_at * LANES : small_at * LANES + SMALL_GAINS].astype(f32)
    gain_one, gain_two = small[:, 0][None], small[:, 1][None]

    bounds = [tile_bounds(segment_ids[seq]) for seq in range(seq_count)]
    packs, lses = [], []
    mixes = [None] * seq_count
    for g, (first, many) in enumerate(groups):
        if g == 0:
            packed, normed = run_project(rows_in, gain_one, weights[0], 3 * many * width)
        else:
            packed = jnp.dot(normed, weights[g][:, : 3 * many * width], preferred_element_type=f32).astype(bf16)
        packs.append([packed[seq * seq_length : (seq + 1) * seq_length] for seq in range(seq_count)])
        if g == 0:
            terms = start_gather(rest)
            packs[0], filled_cotangent = lax.optimization_barrier((packs[0], filled_cotangent))
            d_final_rows = send_slots(filled_cotangent)
        lses.append([])
        for seq in range(seq_count):
            mixes[seq], lse = attend_forward(
                packs[g][seq], *all_masks[seq], bounds[seq], tiles, mixes[seq], first, head_dim
            )
            lses[g].append(lse)
        if g == 0:
            terms, mixes, lses = lax.optimization_barrier((terms, mixes, lses))
            weights.append(finish_gather(terms))
    mixed = join(mixes)
    mixed, d_final_rows = lax.optimization_barrier((mixed, d_final_rows))
    mid_rows, filled = run_middle(mixed, weights[1], out_at, rows_in, gain_two, slot_row, slots)
    slot_rows = send_slots(filled)

    w_in, w_back = expert_in[0], expert_out[0]
    d_hidden = dot(after(d_final_rows, filled), w_back, NT).astype(bf16)
    slot_rows, d_hidden = lax.optimization_barrier((slot_rows, d_hidden))
    hidden, d_pre, d_rows, d_logits, gate = run_expert(me, slot_rows, w_in, weights[0], small_at, d_hidden, experts)
    d_returned = send_slots(d_rows)

    part_in, part_out, moe_rows, grad_router = expert_grads(
        gate, slot_rows, hidden, d_pre, d_final_rows, w_back, d_logits
    )
    d_returned, moe_rows, part_in, part_out, grad_router = lax.optimization_barrier(
        (d_returned, moe_rows, part_in, part_out, grad_router)
    )
    grad_expert_in = lax.psum_scatter(part_in, "dp", scatter_dimension=1, tiled=True)
    grad_expert_out = lax.psum_scatter(part_out, "dp", scatter_dimension=0, tiled=True)
    d_mid, d_attn, d_mixed, grad_gain_two = run_middle_back(
        d_returned, slot_column, mid_rows, gain_two, top, weights[1], out_at
    )
    moe_returned = send_slots(moe_rows)

    grad_out = run_out_grad(mixed, d_attn, grad_router, grad_gain_two)
    diagonals, all_parts, near_terms = [], [], []
    terms, waits = scatter_dp(grad_out), [moe_returned]
    for g, (first, many) in enumerate(groups):
        parts, diagonal = [], None
        for seq in range(seq_count):
            at = slice(seq * seq_length, (seq + 1) * seq_length)
            part, here = attend_backward(
                packs[g][seq], d_mixed[at], mixed[at], lses[g][seq], *all_masks[seq], bounds[seq], tiles, first, head_dim
            )
            parts.append(part)
            diagonal = here if diagonal is None else diagonal + here
        parts, diagonal, terms, waits = lax.optimization_barrier((parts, diagonal, terms, waits))
        if g == 0:
            moe_returned = waits[0]
        else:
            near_terms.append(waits[0])
        diagonals.append(diagonal)
        all_parts.append(join(parts))
        half = finish_dp(terms)
        grad_group = None
        for seq in range(seq_count):
            here = dot(normed[seq * seq_length : (seq + 1) * seq_length], parts[seq], TN)
            grad_group = here if grad_group is None else grad_group + here
        waits = [near_parts(half)]
        terms = scatter_dp(grad_group)
        if g < len(groups) - 1:
            output, sums = run_output(moe_returned, slot_column, mid_rows, rows_in, live)
            d_mixed = after(d_mixed, half, output)
    all_parts = lax.optimization_barrier((all_parts, terms[0]))[0]
    input_grad = run_first_back(rows_in, gain_one, d_mid, all_parts, weights)
    input_grad, terms, waits = lax.optimization_barrier((input_grad, terms, waits))
    near_terms.append(waits[0])
    grad_expert_in, grad_expert_out = widen(grad_expert_in, grad_expert_out)
    grad_rel = jnp.einsum("hgp,gpb->bh", jnp.concatenate(diagonals, axis=0), one_hot_windows, precision=HIGHEST)

    tail = jnp.concatenate([grad_rel.reshape(-1), sums[0, :4]])
    tail_size = tail.shape[0]
    tail = jnp.pad(tail, (0, -tail_size % model_width)).reshape(-1, model_width)
    for distance in distances("dp")[::-1]:
        tail = tail + exchange(tail, "dp", distance)
    pieces = []
    for unused in range(3):
        pieces.append(tail.astype(bf16))
        tail = tail - pieces[-1].astype(f32)
    receivers = lax.axis_size("expert")
    half = finish_dp(terms).reshape(receivers, -1, 3 * width)
    own_rows = half.shape[1]
    half = jnp.concatenate([half] + [jnp.broadcast_to(piece[None], (receivers, *piece.shape)) for piece in pieces], axis=1)
    last_near, grad_expert_in, grad_expert_out = lax.optimization_barrier(
        (swap_blocks(half), grad_expert_in, grad_expert_out)
    )
    near_terms.append(last_near[:, :own_rows])
    tail = jnp.sum(last_near[:, own_rows:].astype(f32), axis=0).reshape(3, -1)
    tail = (tail[0] + tail[1]) + tail[2]
    grad_rel = tail[: bucket_count * head_count].reshape(bucket_count, head_count)
    totals = tail[bucket_count * head_count : tail_size]
    stats = jnp.sqrt(totals[:3] / (totals[3] * model_width))

    dense_out, *dense_qkv = [jnp.sum(block.astype(f32), axis=0) for block in near_terms]
    grad_parts = [total.reshape(-1, many, 3, width) for total, (first, many) in zip(dense_qkv, groups)]
    grad_qkv = jnp.concatenate(grad_parts, axis=1).transpose(0, 2, 1, 3).reshape(-1, 3 * model_width)
    grad_gain_one = jnp.sum(grad_qkv * qkv_weight.astype(f32), axis=1) / attn_gain.astype(f32)
    return (
        output.reshape(inputs.shape),
        input_grad.reshape(inputs.shape),
        grad_gain_one,
        grad_qkv,
        dense_out[:, :model_width],
        dense_out[:, model_width + 1],
        dense_out[:, model_width + SMALL_GAINS : model_width + SMALL_GAINS + experts],
        grad_rel,
        grad_expert_in[None],
        grad_expert_out[None],
        stats,
    )


def solution(mesh):
    in_specs = (
        P(("dp", "expert"), None, None),
        P(("dp", "expert"), None, None),
        P(("dp", "expert")),
        P(("dp", "expert"), None),
        P(("dp", "expert"), None),
        P(("dp", "expert")),
        P(("dp", "expert"), None),
        P(),
        P("expert", None, None),
        P("expert", None, None),
        P(("dp", "expert"), None),
        P(("dp", "expert"), None),
        P(("dp", "expert"), None),
        P(("dp", "expert"), None),
        P(("dp", "expert"), None),
        P(),
    )
    out_specs = (
        P(("dp", "expert"), None, None),
        P(("dp", "expert"), None, None),
        P(("dp", "expert")),
        P(("dp", "expert"), None),
        P(("dp", "expert"), None),
        P(("dp", "expert")),
        P(("dp", "expert"), None),
        P(),
        P("expert", None, "dp"),
        P("expert", "dp", None),
        P(),
    )
    return jax.shard_map(body, mesh=mesh, in_specs=in_specs, out_specs=out_specs, check_vma=False)
```

```python
import functools

import jax
import jax.numpy as jnp
from jax import lax
from jax.experimental import pallas as pl
from jax.experimental.pallas import tpu as pltpu
from jax.sharding import PartitionSpec as P

EPSILON = 1e-06
MASK_STEP = 1e30
ROWS = 256
LANES = 128
STEP_HEADS = 4
VMEM_BYTES = 60 * 2**20
SMALL_GAINS = 2
bf16, f32 = jnp.bfloat16, jnp.float32
NT = (((1,), (1,)), ((), ()))
NN = (((1,), (0,)), ((), ()))
TN = (((0,), (0,)), ((), ()))


def cost(microseconds):
    return pl.CostEstimate(flops=int(microseconds * 1.1e9), bytes_accessed=0, transcendentals=0)


def dot(left, right, dims):
    return lax.dot_general(left, right, dims, preferred_element_type=f32)


def offset_windows(values, reach):
    chunks = (values.shape[0] + 1) // LANES
    turned = jnp.pad(values[::-1], (1, 0)).reshape(chunks, LANES)
    middle = chunks // 2
    return jnp.stack(
        [jnp.concatenate([turned[middle - g], turned[middle - g - 1]]) for g in range(-reach, reach + 1)]
    )


def toeplitz_kernel(reach, window_ref, tile_ref):
    for g in range(2 * reach + 1):
        row = window_ref[0, g : g + 1, :]
        full = jnp.broadcast_to(row, (LANES, 2 * LANES))
        turned = pltpu.roll(full, 0, 1, stride=1, stride_axis=0)
        tile_ref[0, g * LANES : (g + 1) * LANES, :] = turned[:, :LANES]


def toeplitz_tiles(windows):
    heads, groups, width = windows.shape
    return pl.pallas_call(
        functools.partial(toeplitz_kernel, groups // 2),
        grid=(heads,),
        in_specs=[pl.BlockSpec((1, groups, width), lambda n: (n, 0, 0))],
        out_specs=pl.BlockSpec((1, groups * LANES, LANES), lambda n: (n, 0, 0)),
        out_shape=jax.ShapeDtypeStruct((heads, groups * LANES, LANES), f32),
        compiler_params=pltpu.CompilerParams(vmem_limit_bytes=VMEM_BYTES),
        cost_estimate=cost(9),
        name="toeplitz_tiles",
    )(windows)


def head_lanes(rows, head, head_dim):
    lane = lax.broadcasted_iota(jnp.int32, rows.shape, 1)
    return jnp.where((lane >= head * head_dim) & (lane < (head + 1) * head_dim), rows, jnp.zeros_like(rows))


def head_rows(columns, head, head_dim):
    row = lax.broadcasted_iota(jnp.int32, columns.shape, 0)
    return jnp.where((row >= head * head_dim) & (row < (head + 1) * head_dim), columns, jnp.zeros_like(columns))


def bias_tile(bias_ref, head, offset):
    parts = [
        bias_ref[head, pl.ds(pl.multiple_of(offset - LANES * part, LANES), ROWS), :]
        for part in range(ROWS // LANES)
    ]
    return jnp.concatenate(parts, axis=1)


def forward_kernel(head_dim, reach, low_ref, high_ref, in_ref, small_ref, weight_ref, qx_ref, kx_ref, bias_ref, *refs):
    packed_ref, mix_ref, lse_ref, normed_ref, vt_ref = refs[-5:]
    length, width = mix_ref.shape
    heads = width // head_dim
    scale = head_dim ** (-0.5)
    chunks = [slice(at, at + ROWS) for at in range(0, length, ROWS)]

    @pl.when(pl.program_id(0) == 0)
    def _():
        gain = gain_row(small_ref, 0)
        for here in chunks:
            rows = in_ref[here].astype(f32)
            normed_ref[here] = (rows * row_factor(rows) * gain).astype(bf16)

    for here in chunks:
        packed_ref[here] = dot(normed_ref[here], weight_ref[...], NN).astype(bf16)
    q_ref, k_ref, v_ref = [packed_ref.at[:, part * width : (part + 1) * width] for part in range(3)]
    for c in range(width // LANES):
        vt_ref[c * LANES : (c + 1) * LANES, :] = v_ref[:, c * LANES : (c + 1) * LANES].T
    per = LANES // head_dim

    def one_block(qb, unused):
        first = pl.multiple_of(qb * ROWS, ROWS)
        qx = qx_ref[:, pl.ds(first, ROWS)]
        queries = []
        for c in range(width // LANES):
            pair = (q_ref[pl.ds(first, ROWS), c * LANES : (c + 1) * LANES] * jnp.asarray(scale, bf16)).T
            queries += [jnp.concatenate([head_rows(pair, h, head_dim), qx], axis=0) for h in range(per)]

        def one_tile(kb, carry):
            keys_at = pl.multiple_of(kb * ROWS, ROWS)
            offset = pl.multiple_of(keys_at - first + LANES * reach, LANES)
            kx = kx_ref[pl.ds(keys_at, ROWS), :]
            out = []
            all_scores = []
            for h in range(heads):
                c = h // per
                keys = jnp.concatenate([k_ref[pl.ds(keys_at, ROWS), c * LANES : (c + 1) * LANES], kx], axis=1)
                all_scores.append(dot(keys, queries[h], NN))
            soft = []
            for h in range(heads):
                peak, total, mixed = carry[h]
                scores = all_scores[h] + bias_tile(bias_ref, h, offset)
                new_peak = jnp.maximum(peak, jnp.max(scores, axis=0, keepdims=True))
                weights = jnp.exp(scores - new_peak)
                shrink = jnp.exp(peak - new_peak)
                total = total * shrink + jnp.sum(weights, axis=0, keepdims=True)
                soft.append((new_peak, total, shrink, weights.astype(bf16)))
            for h in range(heads):
                new_peak, total, shrink, weights = soft[h]
                values = vt_ref[h * head_dim : (h + 1) * head_dim, pl.ds(keys_at, ROWS)]
                mixed = carry[h][2] * shrink + dot(values, weights, NN)
                out.append((new_peak, total, mixed))
            return tuple(out)

        start = tuple(
            (jnp.full((1, ROWS), -3e38, f32), jnp.zeros((1, ROWS), f32), jnp.zeros((head_dim, ROWS), f32))
            for h in range(heads)
        )
        done = lax.fori_loop(low_ref[qb], high_ref[qb], one_tile, start)
        for c in range(width // LANES):
            rows = jnp.concatenate([done[h][2] / done[h][1] for h in range(c * per, (c + 1) * per)], axis=0)
            mix_ref[pl.ds(first, ROWS), c * LANES : (c + 1) * LANES] = rows.T.astype(bf16)
        for h in range(heads):
            lse_ref[0, h : h + 1, pl.ds(first, ROWS)] = done[h][0] + jnp.log(done[h][1])
        return unused

    lax.fori_loop(0, length // ROWS, one_block, 0)


def probs_kernel(head_dim, reach, low_ref, high_ref, q_ref, k_ref, qx_ref, kx_ref, bias_ref, lse_ref, probs_ref):
    length, width = q_ref.shape
    heads = width // head_dim
    scale = head_dim ** (-0.5)
    per = LANES // head_dim

    def one_block(qb, unused):
        first = pl.multiple_of(qb * ROWS, ROWS)
        qx = qx_ref[:, pl.ds(first, ROWS)]
        queries = []
        for c in range(width // LANES):
            pair = (q_ref[pl.ds(first, ROWS), c * LANES : (c + 1) * LANES] * jnp.asarray(scale, bf16)).T
            queries += [jnp.concatenate([head_rows(pair, h, head_dim), qx], axis=0) for h in range(per)]
        lses = [lse_ref[0, h : h + 1, pl.ds(first, ROWS)] for h in range(heads)]

        def one_tile(kb, unused):
            keys_at = pl.multiple_of(kb * ROWS, ROWS)
            offset = pl.multiple_of(keys_at - first + LANES * reach, LANES)
            kx = kx_ref[pl.ds(keys_at, ROWS), :]
            all_scores = []
            for h in range(heads):
                c = h // per
                keys = jnp.concatenate([k_ref[pl.ds(keys_at, ROWS), c * LANES : (c + 1) * LANES], kx], axis=1)
                all_scores.append(dot(keys, queries[h], NN))
            for h in range(heads):
                weights = jnp.exp(all_scores[h] + bias_tile(bias_ref, h, offset) - lses[h])
                probs_ref[h, qb, pl.ds(keys_at, ROWS), :] = weights.astype(bf16)
            return unused

        return lax.fori_loop(low_ref[qb], high_ref[qb], one_tile, unused)

    lax.fori_loop(0, length // ROWS, one_block, 0)


def diagonal_sums(tiles):
    groups = tiles.shape[0]
    step = LANES // 2
    zero = jnp.zeros((groups, step, LANES), f32)
    turned = jnp.concatenate([tiles[:, :step], zero], axis=2) + pltpu.roll(
        jnp.concatenate([tiles[:, step:], zero], axis=2), 2 * LANES - step, 2
    )
    while step > 8:
        step //= 2
        turned = turned[:, :step] + pltpu.roll(turned[:, step:], 2 * LANES - step, 2)
    while step > 1:
        step //= 2
        turned = turned + pltpu.roll(pltpu.roll(turned, 2 * LANES - step, 2), 8 - step, 1)
    return turned[:, 0]


def backward_kernel(head_dim, reach, low_ref, high_ref, q_ref, k_ref, v_ref, dmix_ref, mix_ref, probs_ref,
                    grad_ref, diag_ref, kt_ref, dk_ref, dv_ref, along_ref):
    length, width = q_ref.shape
    heads = width // head_dim
    scale = head_dim ** (-0.5)
    per = LANES // head_dim
    for c in range(width // LANES):
        kt_ref[c * LANES : (c + 1) * LANES, :] = k_ref[:, c * LANES : (c + 1) * LANES].T
    dk_ref[...] = jnp.zeros_like(dk_ref)
    dv_ref[...] = jnp.zeros_like(dv_ref)
    along_ref[...] = jnp.zeros_like(along_ref)

    def one_block(qb, unused):
        first = pl.multiple_of(qb * ROWS, ROWS)
        queries, d_mixes, deltas, d_turned = [], [], [], []
        for c in range(width // LANES):
            lanes = slice(c * LANES, (c + 1) * LANES)
            query = q_ref[pl.ds(first, ROWS), lanes] * jnp.asarray(scale, bf16)
            d_mix = dmix_ref[pl.ds(first, ROWS), lanes]
            product = (d_mix.astype(f32) * mix_ref[pl.ds(first, ROWS), lanes].astype(f32)).T
            d_mix_turned = d_mix.T
            for h in range(per):
                queries.append(head_lanes(query, h, head_dim))
                d_mixes.append(head_lanes(d_mix, h, head_dim))
                d_turned.append(head_rows(d_mix_turned, h, head_dim))
                deltas.append(jnp.sum(product[h * head_dim : (h + 1) * head_dim], axis=0, keepdims=True))

        def one_tile(kb, carry):
            keys_at = pl.multiple_of(kb * ROWS, ROWS)
            offset = pl.multiple_of(keys_at - first + LANES * reach, LANES)
            out = []
            low_weights, low_scores, all_weights = [], [], []
            for h in range(heads):
                lanes = slice(h // per * LANES, (h // per + 1) * LANES)
                all_weights.append(dot(v_ref[pl.ds(keys_at, ROWS), lanes], d_turned[h], NN))
            for h in range(heads):
                weights = probs_ref[h, qb, pl.ds(keys_at, ROWS), :]
                d_scores = weights.astype(f32) * (all_weights[h] - deltas[h])
                for part in range(ROWS // LANES):
                    at = pl.ds(pl.multiple_of(offset - LANES * part, LANES), ROWS)
                    along_ref[h, at, :] += d_scores[:, part * LANES : (part + 1) * LANES]
                low_weights.append(weights)
                low_scores.append(d_scores.astype(bf16))
            for h in range(heads):
                keys_turned = kt_ref[h * head_dim : (h + 1) * head_dim, pl.ds(keys_at, ROWS)]
                out.append(carry[h] + dot(keys_turned, low_scores[h], NN))
            for c in range(width // LANES):
                mine = range(c * per, (c + 1) * per)
                lanes = slice(c * LANES, (c + 1) * LANES)
                dv_ref[pl.ds(keys_at, ROWS), lanes] += dot(
                    jnp.concatenate([low_weights[h] for h in mine], axis=1), jnp.concatenate([d_mixes[h] for h in mine], axis=0), NN)
                dk_ref[pl.ds(keys_at, ROWS), lanes] += dot(
                    jnp.concatenate([low_scores[h] for h in mine], axis=1), jnp.concatenate([queries[h] for h in mine], axis=0), NN)
            return tuple(out)

        start = tuple(jnp.zeros((head_dim, ROWS), f32) for h in range(heads))
        done = lax.fori_loop(low_ref[qb], high_ref[qb], one_tile, start)
        for c in range(width // LANES):
            rows = jnp.concatenate([done[h] for h in range(c * per, (c + 1) * per)], axis=0) * scale
            grad_ref[pl.ds(first, ROWS), c * LANES : (c + 1) * LANES] = rows.T.astype(bf16)
        return unused

    lax.fori_loop(0, length // ROWS, one_block, 0)
    grad_ref[:, width : 2 * width] = dk_ref[...].astype(bf16)
    grad_ref[:, 2 * width :] = dv_ref[...].astype(bf16)
    for h in range(heads):
        diag_ref[h] = diagonal_sums(along_ref[h].reshape(2 * reach + 1, LANES, LANES))


def tile_bounds(segments):
    length = segments.shape[0]
    blocks = segments.reshape(length // ROWS, ROWS)
    starts = jnp.sum((segments[None, :] < blocks[:, :1]).astype(jnp.int32), axis=1)
    ends = jnp.sum((segments[None, :] <= blocks[:, -1:]).astype(jnp.int32), axis=1)
    return starts // ROWS, (ends + ROWS - 1) // ROWS


def mask_columns(segments, validity, segment_count=8):
    length = segments.shape[0]
    short = 1
    while short * (short + 1) < length:
        short += 1
    at = jnp.arange(length, dtype=jnp.int32)
    lane = jnp.arange(LANES, dtype=jnp.int32)[None, :]
    in_first = (lane >= segment_count) & (lane < segment_count + short)
    in_second = (lane >= segment_count + short) & (lane < segment_count + 2 * short + 1)
    mine = (
        (lane == segments[:, None])
        | (in_first & (lane - segment_count == (at % short)[:, None]))
        | (in_second & (lane - segment_count - short == (at % (short + 1))[:, None]))
    )
    used = lane < segment_count + 2 * short + 1
    query_side = jnp.where(used & ~mine, -MASK_STEP, 0.0).astype(bf16).T
    real = (validity == 1)[:, None]
    key_side = jnp.where(mine & jnp.where(real, lane < segment_count, lane >= segment_count), 1.0, 0.0).astype(bf16)
    return query_side, key_side


def attend_forward(rows_in, smalls, small_at, weights, query_side, key_side, bounds, tiles, mixed, first, steps, head_dim):
    length, model_width = rows_in.shape
    width = STEP_HEADS * head_dim
    reach = tiles.shape[1] // LANES // 2
    shared = [] if mixed is None else [mixed]
    whole = lambda *_: (0, 0)
    grid_spec = pltpu.PrefetchScalarGridSpec(
        num_scalar_prefetch=2,
        grid=(steps,),
        in_specs=[
            pl.BlockSpec((length, model_width), whole),
            pl.BlockSpec((model_width, LANES), lambda p, *_: (0, small_at)),
            pl.BlockSpec((model_width, 3 * width), lambda p, *_: (0, p)),
            pl.BlockSpec((LANES, length), whole),
            pl.BlockSpec((length, LANES), whole),
            pl.BlockSpec((STEP_HEADS, tiles.shape[1], LANES), lambda p, *_: (first + p, 0, 0)),
        ]
        + [pl.BlockSpec(memory_space=pl.ANY)] * len(shared),
        out_specs=[
            pl.BlockSpec((length, 3 * width), lambda p, *_: (0, p)),
            pl.BlockSpec((length, width), lambda p, *_: (0, first + p)),
            pl.BlockSpec((1, STEP_HEADS, length), lambda p, *_: (p, 0, 0)),
            pl.BlockSpec((length, model_width), whole),
        ],
        scratch_shapes=[pltpu.VMEM((width, length), bf16)],
    )
    return pl.pallas_call(
        functools.partial(forward_kernel, head_dim, reach),
        grid_spec=grid_spec,
        out_shape=[
            jax.ShapeDtypeStruct((length, 3 * width * steps), bf16),
            jax.ShapeDtypeStruct((length, tiles.shape[0] * head_dim), bf16),
            jax.ShapeDtypeStruct((steps, STEP_HEADS, length), f32),
            jax.ShapeDtypeStruct((length, model_width), bf16),
        ],
        input_output_aliases={8: 1} if shared else {},
        compiler_params=pltpu.CompilerParams(vmem_limit_bytes=VMEM_BYTES),
        cost_estimate=cost(1),
        name="attend_forward",
    )(*bounds, rows_in, smalls, weights, query_side, key_side, tiles, *shared)


def attend_probs(packed, lse, query_side, key_side, bounds, tiles, first, head_dim):
    length = packed.shape[0]
    width = STEP_HEADS * head_dim
    steps = packed.shape[1] // 3 // width
    reach = tiles.shape[1] // LANES // 2
    whole = lambda *_: (0, 0)
    blocks = length // ROWS
    grid_spec = pltpu.PrefetchScalarGridSpec(
        num_scalar_prefetch=2,
        grid=(steps,),
        in_specs=[
            pl.BlockSpec((length, width), lambda p, *_: (0, 3 * p)),
            pl.BlockSpec((length, width), lambda p, *_: (0, 3 * p + 1)),
            pl.BlockSpec((LANES, length), whole),
            pl.BlockSpec((length, LANES), whole),
            pl.BlockSpec((STEP_HEADS, tiles.shape[1], LANES), lambda p, *_: (first + p, 0, 0)),
            pl.BlockSpec((1, STEP_HEADS, length), lambda p, *_: (p, 0, 0)),
        ],
        out_specs=pl.BlockSpec((STEP_HEADS, blocks, length, ROWS), lambda p, *_: (p, 0, 0, 0)),
    )
    return pl.pallas_call(
        functools.partial(probs_kernel, head_dim, reach),
        grid_spec=grid_spec,
        out_shape=jax.ShapeDtypeStruct((steps * STEP_HEADS, blocks, length, ROWS), bf16),
        compiler_params=pltpu.CompilerParams(vmem_limit_bytes=56 * 2**20),
        cost_estimate=cost(9 * steps),
        name="attend_probs",
    )(*bounds, packed, packed, query_side, key_side, tiles, lse)


def attend_backward(packed, d_mix, mix, probs, bounds, groups, first, head_dim):
    length = packed.shape[0]
    width = STEP_HEADS * head_dim
    steps = packed.shape[1] // 3 // width
    whole = lambda *_: (0, 0)
    grid_spec = pltpu.PrefetchScalarGridSpec(
        num_scalar_prefetch=2,
        grid=(steps,),
        in_specs=[
            pl.BlockSpec((length, width), lambda p, *_: (0, 3 * p)),
            pl.BlockSpec((length, width), lambda p, *_: (0, 3 * p + 1)),
            pl.BlockSpec((length, width), lambda p, *_: (0, 3 * p + 2)),
            pl.BlockSpec((length, width), lambda p, *_: (0, first + p)),
            pl.BlockSpec((length, width), lambda p, *_: (0, first + p)),
            pl.BlockSpec((STEP_HEADS, *probs.shape[1:]), lambda p, *_: (p, 0, 0, 0)),
        ],
        out_specs=[
            pl.BlockSpec((length, 3 * width), lambda p, *_: (0, p)),
            pl.BlockSpec((STEP_HEADS, groups, 2 * LANES), lambda p, *_: (p, 0, 0)),
        ],
        scratch_shapes=[
            pltpu.VMEM((width, length), bf16),
            pltpu.VMEM((length, width), f32),
            pltpu.VMEM((length, width), f32),
            pltpu.VMEM((STEP_HEADS, groups * LANES, LANES), f32),
        ],
    )
    return pl.pallas_call(
        functools.partial(backward_kernel, head_dim, groups // 2),
        grid_spec=grid_spec,
        out_shape=[
            jax.ShapeDtypeStruct((length, 3 * width * steps), bf16),
            jax.ShapeDtypeStruct((steps * STEP_HEADS, groups, 2 * LANES), f32),
        ],
        compiler_params=pltpu.CompilerParams(vmem_limit_bytes=40 * 2**20),
        cost_estimate=cost(15 * steps),
        name="attend_backward",
    )(*bounds, packed, packed, packed, d_mix, mix, probs)


def spread_kernel(width, near_steps, weight_ref, out_weight_ref, first_ref, second_ref, router_ref, *outs):
    receivers, count = outs[0].shape[:2]
    steps = weight_ref.shape[1] // (3 * width)
    row = lax.broadcasted_iota(jnp.int32, (count, count), 0)
    same = row == lax.broadcasted_iota(jnp.int32, (count, count), 1)
    columns = [
        jnp.sum(jnp.where(same, jnp.broadcast_to(ref[...].astype(f32), same.shape), 0.0), axis=1, keepdims=True)
        for ref in (first_ref, second_ref)
    ]
    columns.append(dot(jnp.where(same, 1.0, 0.0).astype(bf16), router_ref[...], NT))
    used = SMALL_GAINS + router_ref.shape[0]
    columns.append(jnp.zeros((count, -used % LANES), f32))
    pieces = [
        weight_ref[:, (part * steps + p) * width : (part * steps + p + 1) * width] for p in range(steps) for part in range(3)
    ]
    groups = [
        pieces[: 3 * near_steps] + [jnp.concatenate(columns, axis=1).astype(bf16)],
        pieces[3 * near_steps :] + [out_weight_ref[...]],
    ]
    for group, out_ref in zip(groups, outs):
        at = 0
        for piece in group:
            out_ref[:, :, at : at + piece.shape[1]] = jnp.broadcast_to(piece[None], (receivers, *piece.shape))
            at += piece.shape[1]


def spread_shard(weight, out_weight, first_gain, second_gain, router, width, near_steps, receivers):
    rows, columns = weight.shape
    small = SMALL_GAINS + router.shape[1]
    small += -small % LANES
    near = 3 * width * near_steps
    return pl.pallas_call(
        functools.partial(spread_kernel, width, near_steps),
        out_shape=[
            jax.ShapeDtypeStruct((receivers, rows, near + small), bf16),
            jax.ShapeDtypeStruct((receivers, rows, columns - near + out_weight.shape[1]), bf16),
        ],
        compiler_params=pltpu.CompilerParams(vmem_limit_bytes=VMEM_BYTES),
        cost_estimate=cost(2),
        name="spread_shard",
    )(weight, out_weight, first_gain.reshape(1, rows), second_gain.reshape(1, rows), router.T)


def expert_kernel(experts, me_ref, rows_ref, in_ref, small_ref, d_hidden_ref, d_rows_ref, d_logits_ref, gate_ref,
                  probs_ref, total_ref, d_gate_ref):
    step = pl.program_id(0)
    lane = lax.broadcasted_iota(jnp.int32, probs_ref.shape, 1)
    chosen = lane == me_ref[0] + SMALL_GAINS

    @pl.when(step == 0)
    def _():
        logits = dot(rows_ref[...], small_ref[...], NN)
        logits = jnp.where((lane >= SMALL_GAINS) & (lane < SMALL_GAINS + experts), logits, -MASK_STEP)
        raised = jnp.exp(logits - jnp.max(logits, axis=1, keepdims=True))
        probs = raised / jnp.sum(raised, axis=1, keepdims=True)
        probs_ref[...] = probs
        gate_ref[...] = jnp.sum(jnp.where(chosen, probs, 0.0), axis=1, keepdims=True)
        total_ref[...] = jnp.zeros_like(total_ref)
        d_gate_ref[...] = jnp.zeros_like(d_gate_ref)

    count = rows_ref.shape[0]
    chunk = 256 if count % 256 == 0 else count
    weights = in_ref[...]
    pres = [dot(rows_ref[at : at + chunk], weights, NN) for at in range(0, count, chunk)]
    lows = []
    for i, at in enumerate(range(0, count, chunk)):
        here = slice(at, at + chunk)
        unit, slope = gelu_and_slope(pres[i])
        d_hidden = d_hidden_ref[here].astype(f32)
        d_gate_ref[here] += jnp.sum(unit * d_hidden, axis=1, keepdims=True)
        lows.append((d_hidden * slope).astype(bf16))
    for i, at in enumerate(range(0, count, chunk)):
        total_ref[at : at + chunk] += dot(lows[i], weights, NT)

    @pl.when(step == pl.num_programs(0) - 1)
    def _():
        d_logits = (probs_ref[...] * (chosen.astype(f32) - gate_ref[...]) * d_gate_ref[...]).astype(bf16)
        d_logits_ref[...] = d_logits
        d_rows_ref[...] = (gate_ref[...] * total_ref[...] + dot(d_logits, small_ref[...], NT)).astype(bf16)


def run_expert(me, rows, w_in, weights, small_at, d_hidden, experts):
    count, width = rows.shape
    hidden_width = w_in.shape[1]
    block = 512
    whole = lambda f, *_: (0, 0)
    grid_spec = pltpu.PrefetchScalarGridSpec(
        num_scalar_prefetch=1,
        grid=(hidden_width // block,),
        in_specs=[
            pl.BlockSpec((count, width), whole),
            pl.BlockSpec((width, block), lambda f, *_: (0, f)),
            pl.BlockSpec((width, LANES), lambda f, *_: (0, small_at)),
            pl.BlockSpec((count, block), lambda f, *_: (0, f)),
        ],
        out_specs=[
            pl.BlockSpec((count, width), whole),
            pl.BlockSpec((count, LANES), whole),
            pl.BlockSpec((count, 1), whole),
        ],
        scratch_shapes=[pltpu.VMEM((count, LANES), f32), pltpu.VMEM((count, width), f32), pltpu.VMEM((count, 1), f32)],
    )
    return pl.pallas_call(
        functools.partial(expert_kernel, experts),
        grid_spec=grid_spec,
        out_shape=[
            jax.ShapeDtypeStruct((count, width), bf16),
            jax.ShapeDtypeStruct((count, LANES), bf16),
            jax.ShapeDtypeStruct((count, 1), f32),
        ],
        compiler_params=pltpu.CompilerParams(vmem_limit_bytes=VMEM_BYTES),
        cost_estimate=cost(18),
        name="run_expert",
    )(me.reshape(1), rows, w_in, weights, d_hidden)


def expert_grads_kernel(gate_ref, rows_ref, in_ref, d_hidden_ref, d_slots_ref, back_ref, d_logits_ref, parts_ref,
                        moe_ref, router_ref, d_out_ref, total_ref):
    step = pl.program_id(0)

    @pl.when(step == 0)
    def _():
        d_out_ref[...] = (gate_ref[...] * d_slots_ref[...].astype(f32)).astype(bf16)
        total_ref[...] = jnp.zeros_like(total_ref)
        router_ref[...] = dot(rows_ref[...], d_logits_ref[...], TN)

    count = rows_ref.shape[0]
    chunk = 256 if count % 256 == 0 else count
    pres = [dot(rows_ref[at : at + chunk], in_ref[...], NN) for at in range(0, count, chunk)]
    units, lows = [], []
    for i, at in enumerate(range(0, count, chunk)):
        here = slice(at, at + chunk)
        unit, slope = gelu_and_slope(pres[i])
        units.append(unit.astype(bf16))
        lows.append((gate_ref[here] * d_hidden_ref[here].astype(f32) * slope).astype(bf16))
    hidden = jnp.concatenate(units, axis=0)
    parts_ref[0, 0] = dot(jnp.concatenate(lows, axis=0), rows_ref[...], TN).astype(bf16)
    parts_ref[0, 1] = dot(hidden, d_out_ref[...], TN).astype(bf16)
    total_ref[...] += dot(hidden, back_ref[...], NN)

    @pl.when(step == pl.num_programs(0) - 1)
    def _():
        moe_ref[...] = (gate_ref[...] * total_ref[...]).astype(bf16)


def expert_grads(gate, rows, w_in, d_hidden, d_slots, w_back, d_logits, owners):
    count, width = rows.shape
    block = w_in.shape[1] // owners
    whole = lambda f: (0, 0)
    full = pl.BlockSpec((count, width), whole)
    return pl.pallas_call(
        expert_grads_kernel,
        grid=(owners,),
        in_specs=[
            pl.BlockSpec((count, 1), whole),
            full,
            pl.BlockSpec((width, block), lambda f: (0, f)),
            pl.BlockSpec((count, block), lambda f: (0, f)),
            full,
            pl.BlockSpec((block, width), lambda f: (f, 0)),
            pl.BlockSpec((count, LANES), whole),
        ],
        out_specs=[
            pl.BlockSpec((1, 2, block, width), lambda f: (f, 0, 0, 0)),
            full,
            pl.BlockSpec((width, LANES), whole),
        ],
        out_shape=[
            jax.ShapeDtypeStruct((owners, 2, block, width), bf16),
            jax.ShapeDtypeStruct((count, width), bf16),
            jax.ShapeDtypeStruct((width, LANES), f32),
        ],
        scratch_shapes=[pltpu.VMEM((count, width), bf16), pltpu.VMEM((count, width), f32)],
        compiler_params=pltpu.CompilerParams(vmem_limit_bytes=VMEM_BYTES),
        cost_estimate=cost(35),
        name="expert_grads",
    )(gate, rows, w_in, d_hidden, d_slots, w_back, d_logits)


def gain_row(small_ref, lane):
    return small_ref[...].astype(f32).T[lane : lane + 1]


def row_factor(rows):
    return lax.rsqrt(jnp.mean(rows * rows, axis=1, keepdims=True) + EPSILON)


def middle_kernel(row_steps, mixed_ref, weight_ref, in_ref, small_ref, slot_ref, rows_ref, slots_ref, normed_ref):
    step = pl.program_id(0)

    @pl.when(step < row_steps)
    def _():
        count = in_ref.shape[0]
        first = pl.multiple_of(step * count, count)
        chunks = [slice(at, at + ROWS) for at in range(0, count, ROWS)]
        gain = gain_row(small_ref, 1)
        projected = [dot(mixed_ref[here], weight_ref[...], NN) for here in chunks]
        for here, attn in zip(chunks, projected):
            rows = in_ref[here].astype(f32) + attn
            rows_ref[here] = rows
            normed_ref[pl.ds(first + here.start, ROWS)] = (rows * row_factor(rows) * gain).astype(bf16)

    @pl.when(step >= row_steps)
    def _():
        fill_kernel(slot_ref, normed_ref, slots_ref, (step - row_steps) * slots_ref.shape[0])


def fill_kernel(slot_ref, rows_ref, slots_ref, first=0):
    slots, count = slots_ref.shape[0], rows_ref.shape[0]
    chunk = ROWS if slots % ROWS == 0 else slots
    for at in range(0, slots, chunk):
        slot = lax.broadcasted_iota(jnp.int32, (chunk, count), 0) + (first + at)
        place = jnp.where(slot == slot_ref[...], 1.0, 0.0).astype(bf16)
        slots_ref[at : at + chunk] = dot(place, rows_ref[...], NN).astype(bf16)


def across(row):
    return jnp.broadcast_to(row.astype(f32), (LANES, row.shape[1])).T


def read_slots(slot_ref, blocks_ref):
    slots = blocks_ref.shape[0]
    mine = jnp.concatenate([across(slot_ref[...])] * pl.cdiv(slots, LANES), axis=1)[:, :slots]
    slot = lax.broadcasted_iota(jnp.int32, mine.shape, 1).astype(f32)
    return dot(jnp.where(slot == mine, 1.0, 0.0).astype(bf16), blocks_ref[...], NN)


def fill_slots(slot_row, rows, slots):
    return pl.pallas_call(
        fill_kernel,
        out_shape=jax.ShapeDtypeStruct((slots, rows.shape[1]), bf16),
        compiler_params=pltpu.CompilerParams(vmem_limit_bytes=VMEM_BYTES),
        cost_estimate=cost(3.5),
        name="fill_slots",
    )(slot_row, rows)


def run_middle(mixed, weights, at, rows_in, smalls, small_at, slot_row, slots):
    count, width = rows_in.shape
    whole = lambda i: (0, 0)
    row_steps = 2 if count % (2 * ROWS) == 0 else 1
    slot_steps = 2 if slots % 32 == 0 else 1
    part = pl.BlockSpec((count // row_steps, width), lambda i: (jnp.minimum(i, row_steps - 1), 0))
    return pl.pallas_call(
        functools.partial(middle_kernel, row_steps),
        grid=(row_steps + slot_steps,),
        in_specs=[
            part,
            pl.BlockSpec((width, width), lambda i: (0, at)),
            part,
            pl.BlockSpec((width, LANES), lambda i: (0, small_at)),
            pl.BlockSpec((1, count), whole),
        ],
        out_specs=[part, pl.BlockSpec((slots // slot_steps, width), lambda i: (jnp.maximum(i - row_steps, 0), 0))],
        out_shape=[jax.ShapeDtypeStruct((count, width), f32), jax.ShapeDtypeStruct((slots, width), bf16)],
        scratch_shapes=[pltpu.VMEM((count, width), bf16)],
        compiler_params=pltpu.CompilerParams(vmem_limit_bytes=VMEM_BYTES),
        cost_estimate=cost(5),
        name="run_middle",
    )(mixed, weights, rows_in, smalls, slot_row)


def middle_back_kernel(blocks_ref, slot_ref, rows_ref, small_ref, top_ref, weight_ref, d_mid_ref, d_mixed_ref, d_gain_ref):
    gain = gain_row(small_ref, 1)
    d_normed = read_slots(slot_ref, blocks_ref)
    rows = rows_ref[...]
    factor = row_factor(rows)
    normed = rows * factor
    weighted = d_normed * gain
    product = d_normed * normed
    d_mid = top_ref[...].astype(f32) + factor * (weighted - normed * jnp.mean(product * gain, axis=1, keepdims=True))
    d_mid = d_mid.astype(bf16)
    d_mid_ref[...] = d_mid
    d_mixed_ref[...] = dot(d_mid, weight_ref[...], NT).astype(bf16)

    @pl.when(pl.program_id(0) == 0)
    def _():
        d_gain_ref[...] = jnp.zeros_like(d_gain_ref)

    d_gain_ref[...] += jnp.sum(product, axis=0, keepdims=True)


def run_middle_back(blocks, slot_row, rows, smalls, small_at, top, weights, at):
    count, width = rows.shape
    whole = lambda *_: (0, 0)
    part = pl.BlockSpec((ROWS, width), lambda i: (i, 0))
    return pl.pallas_call(
        middle_back_kernel,
        grid=(count // ROWS,),
        in_specs=[
            pl.BlockSpec(blocks.shape, whole),
            pl.BlockSpec((1, ROWS), lambda i: (0, i)),
            part,
            pl.BlockSpec((width, LANES), lambda i: (0, small_at)),
            part,
            pl.BlockSpec((width, width), lambda i: (0, at)),
        ],
        out_specs=[part, part, pl.BlockSpec((1, width), whole)],
        out_shape=[
            jax.ShapeDtypeStruct((count, width), bf16),
            jax.ShapeDtypeStruct((count, width), bf16),
            jax.ShapeDtypeStruct((1, width), f32),
        ],
        compiler_params=pltpu.CompilerParams(vmem_limit_bytes=VMEM_BYTES),
        cost_estimate=cost(7),
        name="run_middle_back",
    )(blocks, slot_row, rows, smalls, top, weights)


def first_back_kernel(count, small_at, in_ref, d_mid_ref, *refs):
    d_in_ref = refs[2 * count]
    total = 0.0
    for part_ref, weight_ref in zip(refs[:count], refs[count:]):
        total = total + dot(part_ref[...], weight_ref[:, : part_ref.shape[1]], NT)
    rows = in_ref[...].astype(f32)
    factor = row_factor(rows)
    normed = rows * factor
    weighted = total * gain_row(refs[count].at[:, small_at * LANES : (small_at + 1) * LANES], 0)
    d_in_ref[...] = d_mid_ref[...].astype(f32) + factor * (weighted - normed * jnp.mean(weighted * normed, axis=1, keepdims=True))


def run_first_back(rows_in, small_at, d_mid, parts, weights):
    count, width = rows_in.shape
    whole = lambda *_: (0, 0)
    part = pl.BlockSpec((ROWS, width), lambda i: (i, 0))
    return pl.pallas_call(
        functools.partial(first_back_kernel, len(parts), small_at),
        grid=(count // ROWS,),
        in_specs=[part, part]
        + [pl.BlockSpec((ROWS, columns.shape[1]), lambda i: (i, 0)) for columns in parts]
        + [pl.BlockSpec(weight.shape, whole) for weight in weights],
        out_specs=part,
        out_shape=jax.ShapeDtypeStruct(rows_in.shape, f32),
        compiler_params=pltpu.CompilerParams(vmem_limit_bytes=VMEM_BYTES),
        cost_estimate=cost(8),
        name="run_first_back",
    )(rows_in, d_mid, *parts, *weights)


def output_kernel(blocks_ref, slot_ref, rows_ref, in_ref, live_ref, out_ref, sums_ref):
    rows = rows_ref[...]
    final = rows + read_slots(slot_ref, blocks_ref)
    out_ref[...] = final.astype(bf16)
    live = across(live_ref[...])[:, :1]
    lane = lax.broadcasted_iota(jnp.int32, (1, LANES), 1)
    sums = jnp.where(lane == 3, jnp.sum(live, axis=0, keepdims=True), 0.0)
    for i, part in enumerate((in_ref[...].astype(f32), rows, final)):
        per_row = live * jnp.sum(part * part, axis=1, keepdims=True)
        sums = jnp.where(lane == i, jnp.sum(per_row, axis=0, keepdims=True), sums)

    @pl.when(pl.program_id(0) == 0)
    def _():
        sums_ref[...] = jnp.zeros_like(sums_ref)

    sums_ref[...] += sums


def run_output(blocks, slot_row, rows, rows_in, live):
    count, width = rows.shape
    whole = lambda *_: (0, 0)
    part = pl.BlockSpec((ROWS, width), lambda i: (i, 0))
    column = pl.BlockSpec((1, ROWS), lambda i: (0, i))
    return pl.pallas_call(
        output_kernel,
        grid=(count // ROWS,),
        in_specs=[pl.BlockSpec(blocks.shape, whole), column, part, part, column],
        out_specs=[part, pl.BlockSpec((1, LANES), whole)],
        out_shape=[jax.ShapeDtypeStruct((count, width), bf16), jax.ShapeDtypeStruct((1, LANES), f32)],
        compiler_params=pltpu.CompilerParams(vmem_limit_bytes=VMEM_BYTES),
        cost_estimate=cost(4),
        name="run_output",
    )(blocks, slot_row, rows, rows_in, live)


def dense_grads_kernel(mixed_ref, d_attn_ref, router_ref, gain_ref, normed_ref, parts_ref, grad_ref):
    width = d_attn_ref.shape[1]
    grad_ref[:, :width] = dot(mixed_ref[...], d_attn_ref[...], TN)
    lane = lax.broadcasted_iota(jnp.int32, router_ref.shape, 1)
    grad_ref[:, width : width + LANES] = jnp.where(lane == 1, across(gain_ref[...]), router_ref[...])
    grad_ref[:, width + LANES :] = dot(normed_ref[...], parts_ref[...], TN)


def run_dense_grads(mixed, d_attn, grad_router, grad_gain, normed, parts):
    count, width = mixed.shape
    columns = parts.shape[1]
    block = ROWS if width % ROWS == 0 else width
    whole = lambda i: (0, 0)
    part = pl.BlockSpec((count, block), lambda i: (0, i))
    return pl.pallas_call(
        dense_grads_kernel,
        grid=(width // block,),
        in_specs=[
            part,
            pl.BlockSpec((count, width), whole),
            pl.BlockSpec((block, LANES), lambda i: (i, 0)),
            pl.BlockSpec((1, block), lambda i: (0, i)),
            part,
            pl.BlockSpec((count, columns), whole),
        ],
        out_specs=pl.BlockSpec((block, width + LANES + columns), lambda i: (i, 0)),
        out_shape=jax.ShapeDtypeStruct((width, width + LANES + columns), f32),
        compiler_params=pltpu.CompilerParams(vmem_limit_bytes=VMEM_BYTES),
        cost_estimate=cost(7),
        name="run_dense_grads",
    )(mixed, d_attn, grad_router, grad_gain, normed, parts)


def widen_kernel(sums_ref, in_ref, out_ref):
    in_ref[...] = sums_ref[0, 0].astype(f32).T
    out_ref[...] = sums_ref[0, 1].astype(f32)


def widen(sums):
    block, width = sums.shape[2:]
    step = ROWS if block % ROWS == 0 else LANES
    return pl.pallas_call(
        widen_kernel,
        grid=(block // step,),
        in_specs=[pl.BlockSpec((1, 2, step, width), lambda i: (0, 0, i, 0))],
        out_specs=[pl.BlockSpec((width, step), lambda i: (0, i)), pl.BlockSpec((step, width), lambda i: (i, 0))],
        out_shape=[jax.ShapeDtypeStruct((width, block), f32), jax.ShapeDtypeStruct((block, width), f32)],
        cost_estimate=cost(2),
        name="widen",
    )(sums)


HIGHEST = lax.Precision.HIGHEST
SEGMENT_LIMIT = 512
REACH = (SEGMENT_LIMIT + ROWS - LANES) // LANES


def norm_factor(values):
    return lax.rsqrt(jnp.mean(values * values, axis=-1, keepdims=True) + EPSILON)


def distances(axis):
    return [1 << i for i in reversed(range(lax.axis_size(axis).bit_length() - 1))]


def exchange(rows, axis, distance):
    return lax.ppermute(rows, axis, [(i, i ^ distance) for i in range(lax.axis_size(axis))])


def is_high(axis, distance):
    return (lax.axis_index(axis) & distance) != 0


def swap_blocks(blocks):
    return lax.all_to_all(blocks, "expert", split_axis=0, concat_axis=0, tiled=True)


def after(value, *earlier):
    return lax.optimization_barrier((value, *earlier))[0]


def both(mine, other, axis, distance, at=0):
    high = is_high(axis, distance)
    return jnp.stack([jnp.where(high, other, mine), jnp.where(high, mine, other)], axis=at)


def start_gather(near):
    return near[None], exchange(near[None], "dp", distances("dp")[0])


def finish_gather(terms):
    block, other = terms
    shape = block.shape[1:]
    for distance in distances("dp"):
        if other is None:
            other = exchange(block, "dp", distance)
        block = both(block, other, "dp", distance, 1).reshape(-1, *shape)
        other = None
    return block.reshape(-1, shape[-1])


def scatter_dp(rows):
    width = rows.shape[1]
    block = rows.reshape(lax.axis_size("dp"), -1, width)
    order = distances("dp")[::-1]
    for distance in order:
        halves = block.reshape(block.shape[0] // 2, 2, -1, width)
        high = is_high("dp", distance).astype(jnp.int32)
        keep = lax.dynamic_index_in_dim(halves, high, 1, keepdims=False)
        send = lax.dynamic_index_in_dim(halves, 1 - high, 1, keepdims=False)
        received = exchange(send.astype(bf16), "dp", distance)
        if distance != order[-1]:
            block = keep + received.astype(f32)
    return keep, received


def finish_dp(terms):
    keep, received = terms
    return (keep + received.astype(f32))[0].astype(bf16)


def join(parts):
    return parts[0] if len(parts) == 1 else jnp.concatenate(parts, axis=0)


def near_parts(rows):
    return swap_blocks(rows.reshape(lax.axis_size("expert"), -1, rows.shape[1]))


def gelu_and_slope(values):
    root = 0.7978845608028654
    square = values * values
    share = 0.5 + 0.5 * jnp.tanh(values * (root + root * 0.044715 * square))
    unit = values * share
    slope = share + 2.0 * unit * (1.0 - share) * (root + 3.0 * root * 0.044715 * square)
    return unit, slope


def body(
    inputs,
    cotangent,
    attn_gain,
    qkv_weight,
    out_weight,
    ffn_gain,
    router_weight,
    rel_bias,
    expert_in,
    expert_out,
    routes,
    positions,
    dropped,
    segment_ids,
    valid_mask,
    buckets,
):
    seq_count, seq_length, model_width = inputs.shape
    tokens = seq_count * seq_length
    bucket_count, head_count = rel_bias.shape
    head_dim = model_width // head_count
    experts = router_weight.shape[1]
    capacity = 5 * tokens // (4 * experts)
    slots = experts * capacity
    me = lax.axis_index("expert")

    width = STEP_HEADS * head_dim
    steps = head_count // STEP_HEADS
    groups = [(0, steps - 1), (steps - 1, 1)]
    small_at = 3 * (steps - 1) * width // LANES
    out_at = 3 * width // model_width

    bucket_windows = offset_windows(buckets, REACH)
    one_hot_windows = (bucket_windows[..., None] == jnp.arange(bucket_count, dtype=jnp.int32)).astype(f32)
    windows = jnp.einsum("gpb,bh->hgp", one_hot_windows, rel_bias, precision=HIGHEST)
    tiles = toeplitz_tiles(windows)
    all_masks = [mask_columns(segment_ids[seq], valid_mask[seq]) for seq in range(seq_count)]
    slot_index = jnp.where(
        dropped.reshape(tokens) == 1, slots, routes.reshape(tokens) * capacity + positions.reshape(tokens)
    )
    slot_row, live = slot_index.reshape(1, tokens), valid_mask.reshape(1, tokens)
    rows_in = inputs.reshape(tokens, model_width)
    top = cotangent.reshape(tokens, model_width)

    def send_slots(rows):
        return swap_blocks(rows.reshape(experts, capacity, model_width)).reshape(slots, model_width)

    near, rest = spread_shard(
        qkv_weight, out_weight, attn_gain, ffn_gain, router_weight, width, steps - 1, lax.axis_size("expert")
    )
    near = swap_blocks(near)
    bounds = [tile_bounds(segment_ids[seq]) for seq in range(seq_count)]
    near, rest, tiles = lax.optimization_barrier((near, rest, tiles))
    rest = swap_blocks(rest)
    filled_cotangent = fill_slots(slot_row, top, slots)
    terms = start_gather(near)
    terms, filled_cotangent, rest, all_masks, bounds = lax.optimization_barrier(
        (terms, filled_cotangent, rest, all_masks, bounds)
    )
    weights = [finish_gather(terms)]

    packs, lses, normeds = [], [], None
    mixes = [None] * seq_count
    for g, (first, many) in enumerate(groups):
        if g == 0:
            terms = start_gather(rest)
            weights[0], filled_cotangent = lax.optimization_barrier((weights[0], filled_cotangent))
            d_final_rows = send_slots(filled_cotangent)
        done = [
            attend_forward(
                rows_in[seq * seq_length : (seq + 1) * seq_length],
                weights[0],
                small_at,
                weights[g],
                *all_masks[seq],
                bounds[seq],
                tiles,
                mixes[seq],
                first,
                many,
                head_dim,
            )
            for seq in range(seq_count)
        ]
        packs.append([packed for packed, unused, unused, unused in done])
        mixes = [mixed for unused, mixed, unused, unused in done]
        lses.append([lse for unused, unused, lse, unused in done])
        if g == 0:
            normeds = [normed for unused, unused, unused, normed in done]
            terms, mixes, lses, packs, normeds = lax.optimization_barrier((terms, mixes, lses, packs, normeds))
            weights.append(finish_gather(terms))
    mixed = join(mixes)
    mixed, d_final_rows = lax.optimization_barrier((mixed, d_final_rows))
    mid_rows, filled = run_middle(mixed, weights[1], out_at, rows_in, weights[0], small_at, slot_row, slots)
    slot_rows = send_slots(filled)

    w_in, w_back = expert_in[0], expert_out[0]
    d_hidden = dot(after(d_final_rows, filled), w_back, NT).astype(bf16)
    held_packs = lax.optimization_barrier((packs, filled))[0]
    probs = [
        [
            attend_probs(
                held_packs[g][seq], lses[g][seq], *all_masks[seq], bounds[seq], tiles, first, head_dim
            )
            for seq in range(seq_count)
        ]
        for g, (first, many) in enumerate(groups)
    ]
    slot_rows, d_hidden, probs = lax.optimization_barrier((slot_rows, d_hidden, probs))
    d_rows, d_logits, gate = run_expert(me, slot_rows, w_in, weights[0], small_at, d_hidden, experts)
    d_returned = send_slots(d_rows)

    expert_parts, moe_rows, grad_router = expert_grads(
        gate, slot_rows, w_in, d_hidden, d_final_rows, w_back, d_logits, lax.axis_size("dp")
    )
    d_returned, moe_rows, expert_parts, grad_router = lax.optimization_barrier(
        (d_returned, moe_rows, expert_parts, grad_router)
    )
    expert_sums = lax.psum_scatter(expert_parts, "dp", scatter_dimension=0, tiled=True)
    d_mid, d_mixed, grad_gain_two = run_middle_back(
        d_returned, slot_row, mid_rows, weights[0], small_at, top, weights[1], out_at
    )
    moe_returned = send_slots(moe_rows)

    diagonals, all_parts = [], []
    terms = None
    for g, (first, many) in enumerate(groups):
        parts, diagonal = [], None
        for seq in range(seq_count):
            at = slice(seq * seq_length, (seq + 1) * seq_length)
            part, here = attend_backward(
                packs[g][seq], d_mixed[at], mixed[at], probs[g][seq], bounds[seq], 2 * REACH + 1, first, head_dim
            )
            parts.append(part)
            diagonal = here if diagonal is None else diagonal + here
        parts = join(parts)
        if g == 0:
            grads = run_dense_grads(mixed, d_mid, grad_router, grad_gain_two, join(normeds), parts)
            grads, parts, diagonal, moe_returned = lax.optimization_barrier((grads, parts, diagonal, moe_returned))
            terms = scatter_dp(grads)
            output, sums = run_output(moe_returned, slot_row, mid_rows, rows_in, live)
            d_mixed, output, sums = lax.optimization_barrier((d_mixed, output, sums))
        else:
            parts, diagonal, terms = lax.optimization_barrier((parts, diagonal, terms))
            half, parts = lax.optimization_barrier((finish_dp(terms), parts))
            waits = [near_parts(half)]
            terms = scatter_dp(dot(join(normeds), parts, TN))
        diagonals.append(diagonal)
        all_parts.append(parts)
    held, all_parts = lax.optimization_barrier((terms[0], all_parts))
    terms = (held, terms[1])
    input_grad = run_first_back(rows_in, small_at, d_mid, all_parts, weights)
    input_grad, terms, waits = lax.optimization_barrier((input_grad, terms, waits))
    near_terms = list(waits)
    grad_expert_in, grad_expert_out = widen(expert_sums)
    grad_rel = jnp.einsum("hgp,gpb->bh", jnp.concatenate(diagonals, axis=0), one_hot_windows, precision=HIGHEST)

    tail = jnp.concatenate([grad_rel.reshape(-1), sums[0, :4]])
    tail_size = tail.shape[0]
    tail = jnp.pad(tail, (0, -tail_size % model_width)).reshape(-1, model_width)
    for distance in distances("dp")[::-1]:
        tail = tail + exchange(tail, "dp", distance)
    pieces = []
    for unused in range(3):
        pieces.append(tail.astype(bf16))
        tail = tail - pieces[-1].astype(f32)
    receivers = lax.axis_size("expert")
    half = finish_dp(terms).reshape(receivers, -1, 3 * width)
    own_rows = half.shape[1]
    half = jnp.concatenate([half] + [jnp.broadcast_to(piece[None], (receivers, *piece.shape)) for piece in pieces], axis=1)
    last_near, grad_expert_in, grad_expert_out = lax.optimization_barrier(
        (swap_blocks(half), grad_expert_in, grad_expert_out)
    )
    near_terms.append(last_near[:, :own_rows])
    tail = jnp.sum(last_near[:, own_rows:].astype(f32), axis=0).reshape(3, -1)
    tail = (tail[0] + tail[1]) + tail[2]
    grad_rel = tail[: bucket_count * head_count].reshape(bucket_count, head_count)
    totals = tail[bucket_count * head_count : tail_size]
    stats = jnp.sqrt(totals[:3] / (totals[3] * model_width))

    dense_out, last_qkv = [jnp.sum(block.astype(f32), axis=0) for block in near_terms]
    dense_qkv = [dense_out[:, model_width + LANES :], last_qkv]
    grad_parts = [total.reshape(-1, many, 3, width) for total, (first, many) in zip(dense_qkv, groups)]
    grad_qkv = jnp.concatenate(grad_parts, axis=1).transpose(0, 2, 1, 3).reshape(-1, 3 * model_width)
    grad_gain_one = jnp.sum(grad_qkv * qkv_weight.astype(f32), axis=1) / attn_gain.astype(f32)
    return (
        output.reshape(inputs.shape),
        input_grad.reshape(inputs.shape),
        grad_gain_one,
        grad_qkv,
        dense_out[:, :model_width],
        dense_out[:, model_width + 1],
        dense_out[:, model_width + SMALL_GAINS : model_width + SMALL_GAINS + experts],
        grad_rel,
        grad_expert_in[None],
        grad_expert_out[None],
        stats,
    )


def solution(mesh):
    in_specs = (
        P(("dp", "expert"), None, None),
        P(("dp", "expert"), None, None),
        P(("dp", "expert")),
        P(("dp", "expert"), None),
        P(("dp", "expert"), None),
        P(("dp", "expert")),
        P(("dp", "expert"), None),
        P(),
        P("expert", None, None),
        P("expert", None, None),
        P(("dp", "expert"), None),
        P(("dp", "expert"), None),
        P(("dp", "expert"), None),
        P(("dp", "expert"), None),
        P(("dp", "expert"), None),
        P(),
    )
    out_specs = (
        P(("dp", "expert"), None, None),
        P(("dp", "expert"), None, None),
        P(("dp", "expert")),
        P(("dp", "expert"), None),
        P(("dp", "expert"), None),
        P(("dp", "expert")),
        P(("dp", "expert"), None),
        P(),
        P("expert", None, "dp"),
        P("expert", "dp", None),
        P(),
    )
    return jax.shard_map(body, mesh=mesh, in_specs=in_specs, out_specs=out_specs, check_vma=False)
```

```python
import functools

import jax
import jax.numpy as jnp
from jax import lax
from jax.experimental import pallas as pl
from jax.experimental.pallas import tpu as pltpu
from jax.sharding import PartitionSpec as P

EPSILON = 1e-06
MASK_STEP = 1e30
ROWS = 256
LANES = 128
STEP_HEADS = 4
VMEM_BYTES = 60 * 2**20
SMALL_GAINS = 2
bf16, f32 = jnp.bfloat16, jnp.float32
NT = (((1,), (1,)), ((), ()))
NN = (((1,), (0,)), ((), ()))
TN = (((0,), (0,)), ((), ()))


def cost(microseconds):
    return pl.CostEstimate(flops=int(microseconds * 1.1e9), bytes_accessed=0, transcendentals=0)


def dot(left, right, dims):
    return lax.dot_general(left, right, dims, preferred_element_type=f32)


def offset_windows(values, reach):
    chunks = (values.shape[0] + 1) // LANES
    turned = jnp.pad(values[::-1], (1, 0)).reshape(chunks, LANES)
    middle = chunks // 2
    return jnp.stack(
        [jnp.concatenate([turned[middle - g], turned[middle - g - 1]]) for g in range(-reach, reach + 1)]
    )


def toeplitz_kernel(reach, window_ref, tile_ref):
    for g in range(2 * reach + 1):
        row = window_ref[0, g : g + 1, :]
        full = jnp.broadcast_to(row, (LANES, 2 * LANES))
        turned = pltpu.roll(full, 0, 1, stride=1, stride_axis=0)
        tile_ref[0, g * LANES : (g + 1) * LANES, :] = turned[:, :LANES]


def toeplitz_tiles(windows):
    heads, groups, width = windows.shape
    return pl.pallas_call(
        functools.partial(toeplitz_kernel, groups // 2),
        grid=(heads,),
        in_specs=[pl.BlockSpec((1, groups, width), lambda n: (n, 0, 0))],
        out_specs=pl.BlockSpec((1, groups * LANES, LANES), lambda n: (n, 0, 0)),
        out_shape=jax.ShapeDtypeStruct((heads, groups * LANES, LANES), f32),
        compiler_params=pltpu.CompilerParams(vmem_limit_bytes=VMEM_BYTES),
        cost_estimate=cost(9),
        name="toeplitz_tiles",
    )(windows)


def head_lanes(rows, head, head_dim):
    lane = lax.broadcasted_iota(jnp.int32, rows.shape, 1)
    return jnp.where((lane >= head * head_dim) & (lane < (head + 1) * head_dim), rows, jnp.zeros_like(rows))


def head_rows(columns, head, head_dim):
    row = lax.broadcasted_iota(jnp.int32, columns.shape, 0)
    return jnp.where((row >= head * head_dim) & (row < (head + 1) * head_dim), columns, jnp.zeros_like(columns))


def bias_tile(bias_ref, head, offset):
    parts = [
        bias_ref[head, pl.ds(pl.multiple_of(offset - LANES * part, LANES), ROWS), :]
        for part in range(ROWS // LANES)
    ]
    return jnp.concatenate(parts, axis=1)


def forward_kernel(head_dim, reach, low_ref, high_ref, in_ref, small_ref, weight_ref, qx_ref, kx_ref, bias_ref, *refs):
    packed_ref, mix_ref, lse_ref, normed_ref, vt_ref = refs[-5:]
    length, width = mix_ref.shape
    heads = width // head_dim
    scale = head_dim ** (-0.5)
    chunks = [slice(at, at + ROWS) for at in range(0, length, ROWS)]

    @pl.when(pl.program_id(0) == 0)
    def _():
        gain = gain_row(small_ref, 0)
        for here in chunks:
            rows = in_ref[here].astype(f32)
            normed_ref[here] = (rows * row_factor(rows) * gain).astype(bf16)

    for here in chunks:
        packed_ref[here] = dot(normed_ref[here], weight_ref[...], NN).astype(bf16)
    q_ref, k_ref, v_ref = [packed_ref.at[:, part * width : (part + 1) * width] for part in range(3)]
    for c in range(width // LANES):
        vt_ref[c * LANES : (c + 1) * LANES, :] = v_ref[:, c * LANES : (c + 1) * LANES].T
    per = LANES // head_dim

    def one_block(qb, unused):
        first = pl.multiple_of(qb * ROWS, ROWS)
        qx = qx_ref[:, pl.ds(first, ROWS)]
        queries = []
        for c in range(width // LANES):
            pair = (q_ref[pl.ds(first, ROWS), c * LANES : (c + 1) * LANES] * jnp.asarray(scale, bf16)).T
            queries += [jnp.concatenate([head_rows(pair, h, head_dim), qx], axis=0) for h in range(per)]

        def one_tile(kb, carry):
            keys_at = pl.multiple_of(kb * ROWS, ROWS)
            offset = pl.multiple_of(keys_at - first + LANES * reach, LANES)
            kx = kx_ref[pl.ds(keys_at, ROWS), :]
            out = []
            all_scores = []
            for h in range(heads):
                c = h // per
                keys = jnp.concatenate([k_ref[pl.ds(keys_at, ROWS), c * LANES : (c + 1) * LANES], kx], axis=1)
                all_scores.append(dot(keys, queries[h], NN))
            soft = []
            for h in range(heads):
                peak, total, mixed = carry[h]
                scores = all_scores[h] + bias_tile(bias_ref, h, offset)
                new_peak = jnp.maximum(peak, jnp.max(scores, axis=0, keepdims=True))
                weights = jnp.exp(scores - new_peak)
                shrink = jnp.exp(peak - new_peak)
                total = total * shrink + jnp.sum(weights, axis=0, keepdims=True)
                soft.append((new_peak, total, shrink, weights.astype(bf16)))
            for h in range(heads):
                new_peak, total, shrink, weights = soft[h]
                values = vt_ref[h * head_dim : (h + 1) * head_dim, pl.ds(keys_at, ROWS)]
                mixed = carry[h][2] * shrink + dot(values, weights, NN)
                out.append((new_peak, total, mixed))
            return tuple(out)

        start = tuple(
            (jnp.full((1, ROWS), -3e38, f32), jnp.zeros((1, ROWS), f32), jnp.zeros((head_dim, ROWS), f32))
            for h in range(heads)
        )
        done = lax.fori_loop(low_ref[qb], high_ref[qb], one_tile, start)
        for c in range(width // LANES):
            rows = jnp.concatenate([done[h][2] / done[h][1] for h in range(c * per, (c + 1) * per)], axis=0)
            mix_ref[pl.ds(first, ROWS), c * LANES : (c + 1) * LANES] = rows.T.astype(bf16)
        for h in range(heads):
            lse_ref[0, h : h + 1, pl.ds(first, ROWS)] = done[h][0] + jnp.log(done[h][1])
        return unused

    lax.fori_loop(0, length // ROWS, one_block, 0)


def probs_kernel(head_dim, reach, low_ref, high_ref, q_ref, k_ref, qx_ref, kx_ref, bias_ref, lse_ref, probs_ref):
    length, width = q_ref.shape
    heads = width // head_dim
    scale = head_dim ** (-0.5)
    per = LANES // head_dim

    def one_block(qb, unused):
        first = pl.multiple_of(qb * ROWS, ROWS)
        qx = qx_ref[:, pl.ds(first, ROWS)]
        queries = []
        for c in range(width // LANES):
            pair = (q_ref[pl.ds(first, ROWS), c * LANES : (c + 1) * LANES] * jnp.asarray(scale, bf16)).T
            queries += [jnp.concatenate([head_rows(pair, h, head_dim), qx], axis=0) for h in range(per)]
        lses = [lse_ref[0, h : h + 1, pl.ds(first, ROWS)] for h in range(heads)]

        def one_tile(kb, unused):
            keys_at = pl.multiple_of(kb * ROWS, ROWS)
            offset = pl.multiple_of(keys_at - first + LANES * reach, LANES)
            kx = kx_ref[pl.ds(keys_at, ROWS), :]
            all_scores = []
            for h in range(heads):
                c = h // per
                keys = jnp.concatenate([k_ref[pl.ds(keys_at, ROWS), c * LANES : (c + 1) * LANES], kx], axis=1)
                all_scores.append(dot(keys, queries[h], NN))
            for h in range(heads):
                weights = jnp.exp(all_scores[h] + bias_tile(bias_ref, h, offset) - lses[h])
                probs_ref[h, qb, pl.ds(keys_at, ROWS), :] = weights.astype(bf16)
            return unused

        return lax.fori_loop(low_ref[qb], high_ref[qb], one_tile, unused)

    lax.fori_loop(0, length // ROWS, one_block, 0)


def diagonal_sums(tiles):
    groups = tiles.shape[0]
    step = LANES // 2
    zero = jnp.zeros((groups, step, LANES), f32)
    turned = jnp.concatenate([tiles[:, :step], zero], axis=2) + pltpu.roll(
        jnp.concatenate([tiles[:, step:], zero], axis=2), 2 * LANES - step, 2
    )
    while step > 8:
        step //= 2
        turned = turned[:, :step] + pltpu.roll(turned[:, step:], 2 * LANES - step, 2)
    while step > 1:
        step //= 2
        turned = turned + pltpu.roll(pltpu.roll(turned, 2 * LANES - step, 2), 8 - step, 1)
    return turned[:, 0]


def backward_kernel(head_dim, reach, low_ref, high_ref, q_ref, k_ref, v_ref, dmix_ref, mix_ref, probs_ref,
                    grad_ref, diag_ref, kt_ref, dk_ref, dv_ref, along_ref):
    length, width = q_ref.shape
    heads = width // head_dim
    scale = head_dim ** (-0.5)
    per = LANES // head_dim
    for c in range(width // LANES):
        kt_ref[c * LANES : (c + 1) * LANES, :] = k_ref[:, c * LANES : (c + 1) * LANES].T
    dk_ref[...] = jnp.zeros_like(dk_ref)
    dv_ref[...] = jnp.zeros_like(dv_ref)
    along_ref[...] = jnp.zeros_like(along_ref)

    def one_block(qb, unused):
        first = pl.multiple_of(qb * ROWS, ROWS)
        queries, d_mixes, deltas, d_turned = [], [], [], []
        for c in range(width // LANES):
            lanes = slice(c * LANES, (c + 1) * LANES)
            query = q_ref[pl.ds(first, ROWS), lanes] * jnp.asarray(scale, bf16)
            d_mix = dmix_ref[pl.ds(first, ROWS), lanes]
            product = (d_mix.astype(f32) * mix_ref[pl.ds(first, ROWS), lanes].astype(f32)).T
            d_mix_turned = d_mix.T
            for h in range(per):
                queries.append(head_lanes(query, h, head_dim))
                d_mixes.append(head_lanes(d_mix, h, head_dim))
                d_turned.append(head_rows(d_mix_turned, h, head_dim))
                deltas.append(jnp.sum(product[h * head_dim : (h + 1) * head_dim], axis=0, keepdims=True))

        def one_tile(kb, carry):
            keys_at = pl.multiple_of(kb * ROWS, ROWS)
            offset = pl.multiple_of(keys_at - first + LANES * reach, LANES)
            out = []
            low_weights, low_scores, all_weights = [], [], []
            for h in range(heads):
                lanes = slice(h // per * LANES, (h // per + 1) * LANES)
                all_weights.append(dot(v_ref[pl.ds(keys_at, ROWS), lanes], d_turned[h], NN))
            for h in range(heads):
                weights = probs_ref[h, qb, pl.ds(keys_at, ROWS), :]
                d_scores = weights.astype(f32) * (all_weights[h] - deltas[h])
                for part in range(ROWS // LANES):
                    at = pl.ds(pl.multiple_of(offset - LANES * part, LANES), ROWS)
                    along_ref[h, at, :] += d_scores[:, part * LANES : (part + 1) * LANES]
                low_weights.append(weights)
                low_scores.append(d_scores.astype(bf16))
            for h in range(heads):
                keys_turned = kt_ref[h * head_dim : (h + 1) * head_dim, pl.ds(keys_at, ROWS)]
                out.append(carry[h] + dot(keys_turned, low_scores[h], NN))
            for c in range(width // LANES):
                mine = range(c * per, (c + 1) * per)
                lanes = slice(c * LANES, (c + 1) * LANES)
                dv_ref[pl.ds(keys_at, ROWS), lanes] += dot(
                    jnp.concatenate([low_weights[h] for h in mine], axis=1), jnp.concatenate([d_mixes[h] for h in mine], axis=0), NN)
                dk_ref[pl.ds(keys_at, ROWS), lanes] += dot(
                    jnp.concatenate([low_scores[h] for h in mine], axis=1), jnp.concatenate([queries[h] for h in mine], axis=0), NN)
            return tuple(out)

        start = tuple(jnp.zeros((head_dim, ROWS), f32) for h in range(heads))
        done = lax.fori_loop(low_ref[qb], high_ref[qb], one_tile, start)
        for c in range(width // LANES):
            rows = jnp.concatenate([done[h] for h in range(c * per, (c + 1) * per)], axis=0) * scale
            grad_ref[pl.ds(first, ROWS), c * LANES : (c + 1) * LANES] = rows.T.astype(bf16)
        return unused

    lax.fori_loop(0, length // ROWS, one_block, 0)
    grad_ref[:, width : 2 * width] = dk_ref[...].astype(bf16)
    grad_ref[:, 2 * width :] = dv_ref[...].astype(bf16)
    for h in range(heads):
        diag_ref[h] = diagonal_sums(along_ref[h].reshape(2 * reach + 1, LANES, LANES))


def tile_bounds(segments):
    length = segments.shape[0]
    blocks = segments.reshape(length // ROWS, ROWS)
    starts = jnp.sum((segments[None, :] < blocks[:, :1]).astype(jnp.int32), axis=1)
    ends = jnp.sum((segments[None, :] <= blocks[:, -1:]).astype(jnp.int32), axis=1)
    return starts // ROWS, (ends + ROWS - 1) // ROWS


def mask_columns(segments, validity, segment_count=8):
    length = segments.shape[0]
    short = 1
    while short * (short + 1) < length:
        short += 1
    at = jnp.arange(length, dtype=jnp.int32)
    lane = jnp.arange(LANES, dtype=jnp.int32)[None, :]
    in_first = (lane >= segment_count) & (lane < segment_count + short)
    in_second = (lane >= segment_count + short) & (lane < segment_count + 2 * short + 1)
    mine = (
        (lane == segments[:, None])
        | (in_first & (lane - segment_count == (at % short)[:, None]))
        | (in_second & (lane - segment_count - short == (at % (short + 1))[:, None]))
    )
    used = lane < segment_count + 2 * short + 1
    query_side = jnp.where(used & ~mine, -MASK_STEP, 0.0).astype(bf16).T
    real = (validity == 1)[:, None]
    key_side = jnp.where(mine & jnp.where(real, lane < segment_count, lane >= segment_count), 1.0, 0.0).astype(bf16)
    return query_side, key_side


def attend_forward(rows_in, smalls, small_at, weights, query_side, key_side, bounds, tiles, mixed, first, steps, head_dim):
    length, model_width = rows_in.shape
    width = STEP_HEADS * head_dim
    reach = tiles.shape[1] // LANES // 2
    shared = [] if mixed is None else [mixed]
    whole = lambda *_: (0, 0)
    grid_spec = pltpu.PrefetchScalarGridSpec(
        num_scalar_prefetch=2,
        grid=(steps,),
        in_specs=[
            pl.BlockSpec((length, model_width), whole),
            pl.BlockSpec((model_width, LANES), lambda p, *_: (0, small_at)),
            pl.BlockSpec((model_width, 3 * width), lambda p, *_: (0, p)),
            pl.BlockSpec((LANES, length), whole),
            pl.BlockSpec((length, LANES), whole),
            pl.BlockSpec((STEP_HEADS, tiles.shape[1], LANES), lambda p, *_: (first + p, 0, 0)),
        ]
        + [pl.BlockSpec(memory_space=pl.ANY)] * len(shared),
        out_specs=[
            pl.BlockSpec((length, 3 * width), lambda p, *_: (0, p)),
            pl.BlockSpec((length, width), lambda p, *_: (0, first + p)),
            pl.BlockSpec((1, STEP_HEADS, length), lambda p, *_: (p, 0, 0)),
            pl.BlockSpec((length, model_width), whole),
        ],
        scratch_shapes=[pltpu.VMEM((width, length), bf16)],
    )
    return pl.pallas_call(
        functools.partial(forward_kernel, head_dim, reach),
        grid_spec=grid_spec,
        out_shape=[
            jax.ShapeDtypeStruct((length, 3 * width * steps), bf16),
            jax.ShapeDtypeStruct((length, tiles.shape[0] * head_dim), bf16),
            jax.ShapeDtypeStruct((steps, STEP_HEADS, length), f32),
            jax.ShapeDtypeStruct((length, model_width), bf16),
        ],
        input_output_aliases={8: 1} if shared else {},
        compiler_params=pltpu.CompilerParams(vmem_limit_bytes=56 * 2**20),
        cost_estimate=cost(1),
        name="attend_forward",
    )(*bounds, rows_in, smalls, weights, query_side, key_side, tiles, *shared)


def attend_probs(packed, lse, query_side, key_side, bounds, tiles, first, head_dim):
    length = packed.shape[0]
    width = STEP_HEADS * head_dim
    steps = packed.shape[1] // 3 // width
    reach = tiles.shape[1] // LANES // 2
    whole = lambda *_: (0, 0)
    blocks = length // ROWS
    grid_spec = pltpu.PrefetchScalarGridSpec(
        num_scalar_prefetch=2,
        grid=(steps,),
        in_specs=[
            pl.BlockSpec((length, width), lambda p, *_: (0, 3 * p)),
            pl.BlockSpec((length, width), lambda p, *_: (0, 3 * p + 1)),
            pl.BlockSpec((LANES, length), whole),
            pl.BlockSpec((length, LANES), whole),
            pl.BlockSpec((STEP_HEADS, tiles.shape[1], LANES), lambda p, *_: (first + p, 0, 0)),
            pl.BlockSpec((1, STEP_HEADS, length), lambda p, *_: (p, 0, 0)),
        ],
        out_specs=pl.BlockSpec((STEP_HEADS, blocks, length, ROWS), lambda p, *_: (p, 0, 0, 0)),
    )
    return pl.pallas_call(
        functools.partial(probs_kernel, head_dim, reach),
        grid_spec=grid_spec,
        out_shape=jax.ShapeDtypeStruct((steps * STEP_HEADS, blocks, length, ROWS), bf16),
        compiler_params=pltpu.CompilerParams(vmem_limit_bytes=56 * 2**20),
        cost_estimate=cost(9 * steps),
        name="attend_probs",
    )(*bounds, packed, packed, query_side, key_side, tiles, lse)


def attend_backward(packed, d_mix, mix, probs, bounds, groups, first, head_dim):
    length = packed.shape[0]
    width = STEP_HEADS * head_dim
    steps = packed.shape[1] // 3 // width
    whole = lambda *_: (0, 0)
    grid_spec = pltpu.PrefetchScalarGridSpec(
        num_scalar_prefetch=2,
        grid=(steps,),
        in_specs=[
            pl.BlockSpec((length, width), lambda p, *_: (0, 3 * p)),
            pl.BlockSpec((length, width), lambda p, *_: (0, 3 * p + 1)),
            pl.BlockSpec((length, width), lambda p, *_: (0, 3 * p + 2)),
            pl.BlockSpec((length, width), lambda p, *_: (0, first + p)),
            pl.BlockSpec((length, width), lambda p, *_: (0, first + p)),
            pl.BlockSpec((STEP_HEADS, *probs.shape[1:]), lambda p, *_: (p, 0, 0, 0)),
        ],
        out_specs=[
            pl.BlockSpec((length, 3 * width), lambda p, *_: (0, p)),
            pl.BlockSpec((STEP_HEADS, groups, 2 * LANES), lambda p, *_: (p, 0, 0)),
        ],
        scratch_shapes=[
            pltpu.VMEM((width, length), bf16),
            pltpu.VMEM((length, width), f32),
            pltpu.VMEM((length, width), f32),
            pltpu.VMEM((STEP_HEADS, groups * LANES, LANES), f32),
        ],
    )
    return pl.pallas_call(
        functools.partial(backward_kernel, head_dim, groups // 2),
        grid_spec=grid_spec,
        out_shape=[
            jax.ShapeDtypeStruct((length, 3 * width * steps), bf16),
            jax.ShapeDtypeStruct((steps * STEP_HEADS, groups, 2 * LANES), f32),
        ],
        compiler_params=pltpu.CompilerParams(vmem_limit_bytes=40 * 2**20),
        cost_estimate=cost(15 * steps),
        name="attend_backward",
    )(*bounds, packed, packed, packed, d_mix, mix, probs)


def spread_kernel(width, near_steps, weight_ref, out_weight_ref, first_ref, second_ref, router_ref, *outs):
    receivers, count = outs[0].shape[:2]
    steps = weight_ref.shape[1] // (3 * width)
    row = lax.broadcasted_iota(jnp.int32, (count, count), 0)
    same = row == lax.broadcasted_iota(jnp.int32, (count, count), 1)
    columns = [
        jnp.sum(jnp.where(same, jnp.broadcast_to(ref[...].astype(f32), same.shape), 0.0), axis=1, keepdims=True)
        for ref in (first_ref, second_ref)
    ]
    columns.append(dot(jnp.where(same, 1.0, 0.0).astype(bf16), router_ref[...], NT))
    used = SMALL_GAINS + router_ref.shape[0]
    columns.append(jnp.zeros((count, -used % LANES), f32))
    pieces = [
        weight_ref[:, (part * steps + p) * width : (part * steps + p + 1) * width] for p in range(steps) for part in range(3)
    ]
    groups = [
        pieces[: 3 * near_steps] + [jnp.concatenate(columns, axis=1).astype(bf16)],
        pieces[3 * near_steps :] + [out_weight_ref[...]],
    ]
    for group, out_ref in zip(groups, outs):
        at = 0
        for piece in group:
            out_ref[:, :, at : at + piece.shape[1]] = jnp.broadcast_to(piece[None], (receivers, *piece.shape))
            at += piece.shape[1]


def spread_shard(weight, out_weight, first_gain, second_gain, router, width, near_steps, receivers):
    rows, columns = weight.shape
    small = SMALL_GAINS + router.shape[1]
    small += -small % LANES
    near = 3 * width * near_steps
    return pl.pallas_call(
        functools.partial(spread_kernel, width, near_steps),
        out_shape=[
            jax.ShapeDtypeStruct((receivers, rows, near + small), bf16),
            jax.ShapeDtypeStruct((receivers, rows, columns - near + out_weight.shape[1]), bf16),
        ],
        compiler_params=pltpu.CompilerParams(vmem_limit_bytes=VMEM_BYTES),
        cost_estimate=cost(2),
        name="spread_shard",
    )(weight, out_weight, first_gain.reshape(1, rows), second_gain.reshape(1, rows), router.T)


def expert_kernel(experts, me_ref, rows_ref, in_ref, small_ref, d_hidden_ref, d_rows_ref, d_logits_ref, gate_ref,
                  probs_ref, total_ref, d_gate_ref):
    step = pl.program_id(0)
    lane = lax.broadcasted_iota(jnp.int32, probs_ref.shape, 1)
    chosen = lane == me_ref[0] + SMALL_GAINS

    @pl.when(step == 0)
    def _():
        logits = dot(rows_ref[...], small_ref[...], NN)
        logits = jnp.where((lane >= SMALL_GAINS) & (lane < SMALL_GAINS + experts), logits, -MASK_STEP)
        raised = jnp.exp(logits - jnp.max(logits, axis=1, keepdims=True))
        probs = raised / jnp.sum(raised, axis=1, keepdims=True)
        probs_ref[...] = probs
        gate_ref[...] = jnp.sum(jnp.where(chosen, probs, 0.0), axis=1, keepdims=True)
        total_ref[...] = jnp.zeros_like(total_ref)
        d_gate_ref[...] = jnp.zeros_like(d_gate_ref)

    count = rows_ref.shape[0]
    chunk = 256 if count % 256 == 0 else count
    weights = in_ref[...]
    pres = [dot(rows_ref[at : at + chunk], weights, NN) for at in range(0, count, chunk)]
    lows = []
    for i, at in enumerate(range(0, count, chunk)):
        here = slice(at, at + chunk)
        unit, slope = gelu_and_slope(pres[i].astype(bf16))
        d_hidden = d_hidden_ref[here]
        d_gate_ref[here] += jnp.sum((unit * d_hidden).astype(f32), axis=1, keepdims=True)
        lows.append(d_hidden * slope)
    for i, at in enumerate(range(0, count, chunk)):
        total_ref[at : at + chunk] += dot(lows[i], weights, NT)

    @pl.when(step == pl.num_programs(0) - 1)
    def _():
        d_logits = (probs_ref[...] * (chosen.astype(f32) - gate_ref[...]) * d_gate_ref[...]).astype(bf16)
        d_logits_ref[...] = d_logits
        d_rows_ref[...] = (gate_ref[...] * total_ref[...] + dot(d_logits, small_ref[...], NT)).astype(bf16)


def run_expert(me, rows, w_in, weights, small_at, d_hidden, experts):
    count, width = rows.shape
    hidden_width = w_in.shape[1]
    block = 512
    whole = lambda f, *_: (0, 0)
    grid_spec = pltpu.PrefetchScalarGridSpec(
        num_scalar_prefetch=1,
        grid=(hidden_width // block,),
        in_specs=[
            pl.BlockSpec((count, width), whole),
            pl.BlockSpec((width, block), lambda f, *_: (0, f)),
            pl.BlockSpec((width, LANES), lambda f, *_: (0, small_at)),
            pl.BlockSpec((count, block), lambda f, *_: (0, f)),
        ],
        out_specs=[
            pl.BlockSpec((count, width), whole),
            pl.BlockSpec((count, LANES), whole),
            pl.BlockSpec((count, 1), whole),
        ],
        scratch_shapes=[pltpu.VMEM((count, LANES), f32), pltpu.VMEM((count, width), f32), pltpu.VMEM((count, 1), f32)],
    )
    return pl.pallas_call(
        functools.partial(expert_kernel, experts),
        grid_spec=grid_spec,
        out_shape=[
            jax.ShapeDtypeStruct((count, width), bf16),
            jax.ShapeDtypeStruct((count, LANES), bf16),
            jax.ShapeDtypeStruct((count, 1), f32),
        ],
        compiler_params=pltpu.CompilerParams(vmem_limit_bytes=VMEM_BYTES),
        cost_estimate=cost(18),
        name="run_expert",
    )(me.reshape(1), rows, w_in, weights, d_hidden)


def expert_grads_kernel(gate_ref, rows_ref, in_ref, d_hidden_ref, d_slots_ref, back_ref, d_logits_ref, parts_ref,
                        moe_ref, router_ref, d_out_ref, total_ref):
    step = pl.program_id(0)

    @pl.when(step == 0)
    def _():
        d_out_ref[...] = (gate_ref[...] * d_slots_ref[...].astype(f32)).astype(bf16)
        total_ref[...] = jnp.zeros_like(total_ref)
        router_ref[...] = dot(rows_ref[...], d_logits_ref[...], TN)

    count = rows_ref.shape[0]
    chunk = 256 if count % 256 == 0 else count
    pres = [dot(rows_ref[at : at + chunk], in_ref[...], NN) for at in range(0, count, chunk)]
    units, lows = [], []
    for i, at in enumerate(range(0, count, chunk)):
        here = slice(at, at + chunk)
        unit, slope = gelu_and_slope(pres[i])
        units.append(unit.astype(bf16))
        lows.append((gate_ref[here] * d_hidden_ref[here].astype(f32) * slope).astype(bf16))
    hidden = jnp.concatenate(units, axis=0)
    parts_ref[0, 0] = dot(jnp.concatenate(lows, axis=0), rows_ref[...], TN).astype(bf16)
    parts_ref[0, 1] = dot(hidden, d_out_ref[...], TN).astype(bf16)
    total_ref[...] += dot(hidden, back_ref[...], NN)

    @pl.when(step == pl.num_programs(0) - 1)
    def _():
        moe_ref[...] = (gate_ref[...] * total_ref[...]).astype(bf16)


def expert_grads(gate, rows, w_in, d_hidden, d_slots, w_back, d_logits, owners):
    count, width = rows.shape
    block = w_in.shape[1] // owners
    whole = lambda f: (0, 0)
    full = pl.BlockSpec((count, width), whole)
    return pl.pallas_call(
        expert_grads_kernel,
        grid=(owners,),
        in_specs=[
            pl.BlockSpec((count, 1), whole),
            full,
            pl.BlockSpec((width, block), lambda f: (0, f)),
            pl.BlockSpec((count, block), lambda f: (0, f)),
            full,
            pl.BlockSpec((block, width), lambda f: (f, 0)),
            pl.BlockSpec((count, LANES), whole),
        ],
        out_specs=[
            pl.BlockSpec((1, 2, block, width), lambda f: (f, 0, 0, 0)),
            full,
            pl.BlockSpec((width, LANES), whole),
        ],
        out_shape=[
            jax.ShapeDtypeStruct((owners, 2, block, width), bf16),
            jax.ShapeDtypeStruct((count, width), bf16),
            jax.ShapeDtypeStruct((width, LANES), f32),
        ],
        scratch_shapes=[pltpu.VMEM((count, width), bf16), pltpu.VMEM((count, width), f32)],
        compiler_params=pltpu.CompilerParams(vmem_limit_bytes=VMEM_BYTES),
        cost_estimate=cost(35),
        name="expert_grads",
    )(gate, rows, w_in, d_hidden, d_slots, w_back, d_logits)


def gain_row(small_ref, lane):
    return small_ref[...].astype(f32).T[lane : lane + 1]


def row_factor(rows):
    return lax.rsqrt(jnp.mean(rows * rows, axis=1, keepdims=True) + EPSILON)


def middle_kernel(row_steps, mixed_ref, weight_ref, in_ref, small_ref, slot_ref, rows_ref, slots_ref, normed_ref):
    step = pl.program_id(0)

    @pl.when(step < row_steps)
    def _():
        count = in_ref.shape[0]
        first = pl.multiple_of(step * count, count)
        chunks = [slice(at, at + ROWS) for at in range(0, count, ROWS)]
        gain = gain_row(small_ref, 1)
        projected = [dot(mixed_ref[here], weight_ref[...], NN) for here in chunks]
        for here, attn in zip(chunks, projected):
            rows = in_ref[here].astype(f32) + attn
            rows_ref[here] = rows
            normed_ref[pl.ds(first + here.start, ROWS)] = (rows * row_factor(rows) * gain).astype(bf16)

    @pl.when(step >= row_steps)
    def _():
        fill_kernel(slot_ref, normed_ref, slots_ref, (step - row_steps) * slots_ref.shape[0])


def fill_kernel(slot_ref, rows_ref, slots_ref, first=0):
    slots, count = slots_ref.shape[0], rows_ref.shape[0]
    chunk = ROWS if slots % ROWS == 0 else slots
    for at in range(0, slots, chunk):
        slot = lax.broadcasted_iota(jnp.int32, (chunk, count), 0) + (first + at)
        place = jnp.where(slot == slot_ref[...], 1.0, 0.0).astype(bf16)
        slots_ref[at : at + chunk] = dot(place, rows_ref[...], NN).astype(bf16)


def across(row):
    return jnp.broadcast_to(row.astype(f32), (LANES, row.shape[1])).T


def read_slots(slot_ref, blocks_ref):
    slots = blocks_ref.shape[0]
    mine = jnp.concatenate([across(slot_ref[...])] * pl.cdiv(slots, LANES), axis=1)[:, :slots]
    slot = lax.broadcasted_iota(jnp.int32, mine.shape, 1).astype(f32)
    return dot(jnp.where(slot == mine, 1.0, 0.0).astype(bf16), blocks_ref[...], NN)


def fill_slots(slot_row, rows, slots):
    return pl.pallas_call(
        fill_kernel,
        out_shape=jax.ShapeDtypeStruct((slots, rows.shape[1]), bf16),
        compiler_params=pltpu.CompilerParams(vmem_limit_bytes=VMEM_BYTES),
        cost_estimate=cost(3.5),
        name="fill_slots",
    )(slot_row, rows)


def run_middle(mixed, weights, at, rows_in, smalls, small_at, slot_row, slots):
    count, width = rows_in.shape
    whole = lambda i: (0, 0)
    row_steps = 2 if count % (2 * ROWS) == 0 else 1
    slot_steps = 2 if slots % 32 == 0 else 1
    part = pl.BlockSpec((count // row_steps, width), lambda i: (jnp.minimum(i, row_steps - 1), 0))
    return pl.pallas_call(
        functools.partial(middle_kernel, row_steps),
        grid=(row_steps + slot_steps,),
        in_specs=[
            part,
            pl.BlockSpec((width, width), lambda i: (0, at)),
            part,
            pl.BlockSpec((width, LANES), lambda i: (0, small_at)),
            pl.BlockSpec((1, count), whole),
        ],
        out_specs=[part, pl.BlockSpec((slots // slot_steps, width), lambda i: (jnp.maximum(i - row_steps, 0), 0))],
        out_shape=[jax.ShapeDtypeStruct((count, width), f32), jax.ShapeDtypeStruct((slots, width), bf16)],
        scratch_shapes=[pltpu.VMEM((count, width), bf16)],
        compiler_params=pltpu.CompilerParams(vmem_limit_bytes=VMEM_BYTES),
        cost_estimate=cost(5),
        name="run_middle",
    )(mixed, weights, rows_in, smalls, slot_row)


def middle_back_kernel(blocks_ref, slot_ref, rows_ref, small_ref, top_ref, weight_ref, d_mid_ref, d_mixed_ref, d_gain_ref):
    gain = gain_row(small_ref, 1)
    d_normed = read_slots(slot_ref, blocks_ref)
    rows = rows_ref[...]
    factor = row_factor(rows)
    normed = rows * factor
    weighted = d_normed * gain
    product = d_normed * normed
    d_mid = top_ref[...].astype(f32) + factor * (weighted - normed * jnp.mean(product * gain, axis=1, keepdims=True))
    d_mid = d_mid.astype(bf16)
    d_mid_ref[...] = d_mid
    d_mixed_ref[...] = dot(d_mid, weight_ref[...], NT).astype(bf16)

    @pl.when(pl.program_id(0) == 0)
    def _():
        d_gain_ref[...] = jnp.zeros_like(d_gain_ref)

    d_gain_ref[...] += jnp.sum(product, axis=0, keepdims=True)


def run_middle_back(blocks, slot_row, rows, smalls, small_at, top, weights, at):
    count, width = rows.shape
    whole = lambda *_: (0, 0)
    part = pl.BlockSpec((ROWS, width), lambda i: (i, 0))
    return pl.pallas_call(
        middle_back_kernel,
        grid=(count // ROWS,),
        in_specs=[
            pl.BlockSpec(blocks.shape, whole),
            pl.BlockSpec((1, ROWS), lambda i: (0, i)),
            part,
            pl.BlockSpec((width, LANES), lambda i: (0, small_at)),
            part,
            pl.BlockSpec((width, width), lambda i: (0, at)),
        ],
        out_specs=[part, part, pl.BlockSpec((1, width), whole)],
        out_shape=[
            jax.ShapeDtypeStruct((count, width), bf16),
            jax.ShapeDtypeStruct((count, width), bf16),
            jax.ShapeDtypeStruct((1, width), f32),
        ],
        compiler_params=pltpu.CompilerParams(vmem_limit_bytes=VMEM_BYTES),
        cost_estimate=cost(7),
        name="run_middle_back",
    )(blocks, slot_row, rows, smalls, top, weights)


def first_back_kernel(count, small_at, in_ref, d_mid_ref, *refs):
    d_in_ref = refs[2 * count]
    total = 0.0
    for part_ref, weight_ref in zip(refs[:count], refs[count:]):
        total = total + dot(part_ref[...], weight_ref[:, : part_ref.shape[1]], NT)
    rows = in_ref[...].astype(f32)
    factor = row_factor(rows)
    normed = rows * factor
    weighted = total * gain_row(refs[count].at[:, small_at * LANES : (small_at + 1) * LANES], 0)
    d_in_ref[...] = d_mid_ref[...].astype(f32) + factor * (weighted - normed * jnp.mean(weighted * normed, axis=1, keepdims=True))


def run_first_back(rows_in, small_at, d_mid, parts, weights):
    count, width = rows_in.shape
    whole = lambda *_: (0, 0)
    part = pl.BlockSpec((ROWS, width), lambda i: (i, 0))
    return pl.pallas_call(
        functools.partial(first_back_kernel, len(parts), small_at),
        grid=(count // ROWS,),
        in_specs=[part, part]
        + [pl.BlockSpec((ROWS, columns.shape[1]), lambda i: (i, 0)) for columns in parts]
        + [pl.BlockSpec(weight.shape, whole) for weight in weights],
        out_specs=part,
        out_shape=jax.ShapeDtypeStruct(rows_in.shape, f32),
        compiler_params=pltpu.CompilerParams(vmem_limit_bytes=VMEM_BYTES),
        cost_estimate=cost(8),
        name="run_first_back",
    )(rows_in, d_mid, *parts, *weights)


def output_kernel(blocks_ref, slot_ref, rows_ref, in_ref, live_ref, out_ref, sums_ref):
    rows = rows_ref[...]
    final = rows + read_slots(slot_ref, blocks_ref)
    out_ref[...] = final.astype(bf16)
    live = across(live_ref[...])[:, :1]
    lane = lax.broadcasted_iota(jnp.int32, (1, LANES), 1)
    sums = jnp.where(lane == 3, jnp.sum(live, axis=0, keepdims=True), 0.0)
    for i, part in enumerate((in_ref[...].astype(f32), rows, final)):
        per_row = live * jnp.sum(part * part, axis=1, keepdims=True)
        sums = jnp.where(lane == i, jnp.sum(per_row, axis=0, keepdims=True), sums)

    @pl.when(pl.program_id(0) == 0)
    def _():
        sums_ref[...] = jnp.zeros_like(sums_ref)

    sums_ref[...] += sums


def run_output(blocks, slot_row, rows, rows_in, live):
    count, width = rows.shape
    whole = lambda *_: (0, 0)
    part = pl.BlockSpec((ROWS, width), lambda i: (i, 0))
    column = pl.BlockSpec((1, ROWS), lambda i: (0, i))
    return pl.pallas_call(
        output_kernel,
        grid=(count // ROWS,),
        in_specs=[pl.BlockSpec(blocks.shape, whole), column, part, part, column],
        out_specs=[part, pl.BlockSpec((1, LANES), whole)],
        out_shape=[jax.ShapeDtypeStruct((count, width), bf16), jax.ShapeDtypeStruct((1, LANES), f32)],
        compiler_params=pltpu.CompilerParams(vmem_limit_bytes=VMEM_BYTES),
        cost_estimate=cost(4),
        name="run_output",
    )(blocks, slot_row, rows, rows_in, live)


def dense_grads_kernel(mixed_ref, d_attn_ref, router_ref, gain_ref, normed_ref, parts_ref, grad_ref):
    width = d_attn_ref.shape[1]
    grad_ref[:, :width] = dot(mixed_ref[...], d_attn_ref[...], TN).astype(bf16)
    lane = lax.broadcasted_iota(jnp.int32, router_ref.shape, 1)
    grad_ref[:, width : width + LANES] = jnp.where(lane == 1, across(gain_ref[...]), router_ref[...]).astype(bf16)
    grad_ref[:, width + LANES :] = dot(normed_ref[...], parts_ref[...], TN).astype(bf16)


def run_dense_grads(mixed, d_attn, grad_router, grad_gain, normed, parts):
    count, width = mixed.shape
    columns = parts.shape[1]
    block = ROWS if width % ROWS == 0 else width
    whole = lambda i: (0, 0)
    part = pl.BlockSpec((count, block), lambda i: (0, i))
    return pl.pallas_call(
        dense_grads_kernel,
        grid=(width // block,),
        in_specs=[
            part,
            pl.BlockSpec((count, width), whole),
            pl.BlockSpec((block, LANES), lambda i: (i, 0)),
            pl.BlockSpec((1, block), lambda i: (0, i)),
            part,
            pl.BlockSpec((count, columns), whole),
        ],
        out_specs=pl.BlockSpec((block, width + LANES + columns), lambda i: (i, 0)),
        out_shape=jax.ShapeDtypeStruct((width, width + LANES + columns), bf16),
        compiler_params=pltpu.CompilerParams(vmem_limit_bytes=VMEM_BYTES),
        cost_estimate=cost(7),
        name="run_dense_grads",
    )(mixed, d_attn, grad_router, grad_gain, normed, parts)


def widen_kernel(sums_ref, in_ref, out_ref):
    in_ref[...] = sums_ref[0, 0].astype(f32).T
    out_ref[...] = sums_ref[0, 1].astype(f32)


def widen(sums):
    block, width = sums.shape[2:]
    step = ROWS if block % ROWS == 0 else LANES
    return pl.pallas_call(
        widen_kernel,
        grid=(block // step,),
        in_specs=[pl.BlockSpec((1, 2, step, width), lambda i: (0, 0, i, 0))],
        out_specs=[pl.BlockSpec((width, step), lambda i: (0, i)), pl.BlockSpec((step, width), lambda i: (i, 0))],
        out_shape=[jax.ShapeDtypeStruct((width, block), f32), jax.ShapeDtypeStruct((block, width), f32)],
        cost_estimate=cost(2),
        name="widen",
    )(sums)


def place_kernel(me_ref, *refs):
    out_ref = refs[-1]
    for r, piece in enumerate(refs[:-1]):
        out_ref[pl.ds(lax.bitwise_xor(me_ref[0], r), 1)] = piece[...][None]


def place_pieces(me, pieces):
    return pl.pallas_call(
        place_kernel,
        in_specs=[pl.BlockSpec(memory_space=pltpu.SMEM)] + [pl.BlockSpec(memory_space=pltpu.VMEM)] * len(pieces),
        out_shape=jax.ShapeDtypeStruct((len(pieces), *pieces[0].shape), pieces[0].dtype),
        compiler_params=pltpu.CompilerParams(vmem_limit_bytes=16 * 2**20),
        cost_estimate=cost(2),
        name="place_pieces",
    )(me.reshape(1), *pieces)


HIGHEST = lax.Precision.HIGHEST
SEGMENT_LIMIT = 512
REACH = (SEGMENT_LIMIT + ROWS - LANES) // LANES


def norm_factor(values):
    return lax.rsqrt(jnp.mean(values * values, axis=-1, keepdims=True) + EPSILON)


def distances(axis):
    return [1 << i for i in reversed(range(lax.axis_size(axis).bit_length() - 1))]


def exchange(rows, axis, distance):
    return lax.ppermute(rows, axis, [(i, i ^ distance) for i in range(lax.axis_size(axis))])


def is_high(axis, distance):
    return (lax.axis_index(axis) & distance) != 0


def swap_blocks(blocks):
    return lax.all_to_all(blocks, "expert", split_axis=0, concat_axis=0, tiled=True)


def after(value, *earlier):
    return lax.optimization_barrier((value, *earlier))[0]


def start_gather(near):
    return [near] + [exchange(near, "dp", distance) for distance in distances("dp")]


def finish_gather(terms):
    near = terms[0]
    pieces = dict(zip([0] + distances("dp"), terms))
    for r in range(lax.axis_size("dp")):
        if r not in pieces:
            lowest = r & -r
            pieces[r] = exchange(pieces[r ^ lowest], "dp", lowest)
    block = place_pieces(lax.axis_index("dp"), [pieces[r] for r in range(len(pieces))])
    return block.reshape(-1, near.shape[-1])


def scatter_dp(rows):
    width = rows.shape[1]
    block = rows.reshape(lax.axis_size("dp"), -1, width)
    order = distances("dp")[::-1]
    for distance in order:
        halves = block.reshape(block.shape[0] // 2, 2, -1, width)
        high = is_high("dp", distance).astype(jnp.int32)
        keep = lax.dynamic_index_in_dim(halves, high, 1, keepdims=False)
        send = lax.dynamic_index_in_dim(halves, 1 - high, 1, keepdims=False)
        received = exchange(send.astype(bf16), "dp", distance)
        if distance != order[-1]:
            block = keep.astype(f32) + received.astype(f32)
    return keep, received


def finish_dp(terms):
    keep, received = terms
    return (keep.astype(f32) + received.astype(f32))[0].astype(bf16)


def join(parts):
    return parts[0] if len(parts) == 1 else jnp.concatenate(parts, axis=0)


def near_parts(rows):
    return swap_blocks(rows.reshape(lax.axis_size("expert"), -1, rows.shape[1]))


def gelu_and_slope(values):
    root = 0.7978845608028654
    square = values * values
    share = 0.5 + 0.5 * jnp.tanh(values * (root + root * 0.044715 * square))
    unit = values * share
    slope = share + 2.0 * unit * (1.0 - share) * (root + 3.0 * root * 0.044715 * square)
    return unit, slope


def body(
    inputs,
    cotangent,
    attn_gain,
    qkv_weight,
    out_weight,
    ffn_gain,
    router_weight,
    rel_bias,
    expert_in,
    expert_out,
    routes,
    positions,
    dropped,
    segment_ids,
    valid_mask,
    buckets,
):
    seq_count, seq_length, model_width = inputs.shape
    tokens = seq_count * seq_length
    bucket_count, head_count = rel_bias.shape
    head_dim = model_width // head_count
    experts = router_weight.shape[1]
    capacity = 5 * tokens // (4 * experts)
    slots = experts * capacity
    me = lax.axis_index("expert")

    width = STEP_HEADS * head_dim
    steps = head_count // STEP_HEADS
    groups = [(0, steps - 1), (steps - 1, 1)]
    small_at = 3 * (steps - 1) * width // LANES
    out_at = 3 * width // model_width

    bucket_windows = offset_windows(buckets, REACH)
    one_hot_windows = (bucket_windows[..., None] == jnp.arange(bucket_count, dtype=jnp.int32)).astype(f32)
    windows = jnp.einsum("gpb,bh->hgp", one_hot_windows, rel_bias, precision=HIGHEST)
    tiles = toeplitz_tiles(windows)
    all_masks = [mask_columns(segment_ids[seq], valid_mask[seq]) for seq in range(seq_count)]
    slot_index = jnp.where(
        dropped.reshape(tokens) == 1, slots, routes.reshape(tokens) * capacity + positions.reshape(tokens)
    )
    slot_row, live = slot_index.reshape(1, tokens), valid_mask.reshape(1, tokens)
    rows_in = inputs.reshape(tokens, model_width)
    top = cotangent.reshape(tokens, model_width)

    def send_slots(rows):
        return swap_blocks(rows.reshape(experts, capacity, model_width)).reshape(slots, model_width)

    near, rest = spread_shard(
        qkv_weight, out_weight, attn_gain, ffn_gain, router_weight, width, steps - 1, lax.axis_size("expert")
    )
    near = swap_blocks(near)
    bounds = [tile_bounds(segment_ids[seq]) for seq in range(seq_count)]
    near, rest, tiles = lax.optimization_barrier((near, rest, tiles))
    rest = swap_blocks(rest)
    filled_cotangent = fill_slots(slot_row, top, slots)
    terms = start_gather(near)
    terms, filled_cotangent, rest, all_masks, bounds = lax.optimization_barrier(
        (terms, filled_cotangent, rest, all_masks, bounds)
    )
    weights = [finish_gather(terms)]

    packs, lses, normeds = [], [], None
    mixes = [None] * seq_count
    for g, (first, many) in enumerate(groups):
        if g == 0:
            terms = start_gather(rest)
            weights[0], filled_cotangent = lax.optimization_barrier((weights[0], filled_cotangent))
            d_final_rows = send_slots(filled_cotangent)
        done = [
            attend_forward(
                rows_in[seq * seq_length : (seq + 1) * seq_length],
                weights[0],
                small_at,
                weights[g],
                *all_masks[seq],
                bounds[seq],
                tiles,
                mixes[seq],
                first,
                many,
                head_dim,
            )
            for seq in range(seq_count)
        ]
        packs.append([packed for packed, unused, unused, unused in done])
        mixes = [mixed for unused, mixed, unused, unused in done]
        lses.append([lse for unused, unused, lse, unused in done])
        if g == 0:
            normeds = [normed for unused, unused, unused, normed in done]
            terms, mixes, lses, packs, normeds = lax.optimization_barrier((terms, mixes, lses, packs, normeds))
            weights.append(finish_gather(terms))
    mixed = join(mixes)
    mixed, d_final_rows = lax.optimization_barrier((mixed, d_final_rows))
    mid_rows, filled = run_middle(mixed, weights[1], out_at, rows_in, weights[0], small_at, slot_row, slots)
    slot_rows = send_slots(filled)

    w_in, w_back = expert_in[0], expert_out[0]
    d_hidden = dot(after(d_final_rows, filled), w_back, NT).astype(bf16)
    held_packs = lax.optimization_barrier((packs, filled))[0]
    probs = [
        [
            attend_probs(
                held_packs[g][seq], lses[g][seq], *all_masks[seq], bounds[seq], tiles, first, head_dim
            )
            for seq in range(seq_count)
        ]
        for g, (first, many) in enumerate(groups)
    ]
    slot_rows, d_hidden, probs = lax.optimization_barrier((slot_rows, d_hidden, probs))
    d_rows, d_logits, gate = run_expert(me, slot_rows, w_in, weights[0], small_at, d_hidden, experts)
    d_returned = send_slots(d_rows)

    expert_parts, moe_rows, grad_router = expert_grads(
        gate, slot_rows, w_in, d_hidden, d_final_rows, w_back, d_logits, lax.axis_size("dp")
    )
    d_returned, moe_rows, expert_parts, grad_router = lax.optimization_barrier(
        (d_returned, moe_rows, expert_parts, grad_router)
    )
    expert_sums = lax.psum_scatter(expert_parts, "dp", scatter_dimension=0, tiled=True)
    d_mid, d_mixed, grad_gain_two = run_middle_back(
        d_returned, slot_row, mid_rows, weights[0], small_at, top, weights[1], out_at
    )
    moe_returned = send_slots(moe_rows)

    diagonals, all_parts = [], []
    terms = None
    for g, (first, many) in enumerate(groups):
        parts, diagonal = [], None
        for seq in range(seq_count):
            at = slice(seq * seq_length, (seq + 1) * seq_length)
            part, here = attend_backward(
                packs[g][seq], d_mixed[at], mixed[at], probs[g][seq], bounds[seq], 2 * REACH + 1, first, head_dim
            )
            parts.append(part)
            diagonal = here if diagonal is None else diagonal + here
        parts = join(parts)
        if g == 0:
            grads = run_dense_grads(mixed, d_mid, grad_router, grad_gain_two, join(normeds), parts)
            grads, parts, diagonal, moe_returned = lax.optimization_barrier((grads, parts, diagonal, moe_returned))
            terms = scatter_dp(grads)
        else:
            parts, diagonal, terms = lax.optimization_barrier((parts, diagonal, terms))
            half, parts = lax.optimization_barrier((finish_dp(terms), parts))
            waits = [near_parts(half)]
            terms = scatter_dp(dot(join(normeds), parts, TN).astype(bf16))
        diagonals.append(diagonal)
        all_parts.append(parts)
    held, moe_returned = lax.optimization_barrier((terms[0], moe_returned))
    terms = (held, terms[1])
    output, sums = run_output(moe_returned, slot_row, mid_rows, rows_in, live)
    all_parts, output, sums = lax.optimization_barrier((all_parts, output, sums))
    input_grad = run_first_back(rows_in, small_at, d_mid, all_parts, weights)
    input_grad, terms, waits = lax.optimization_barrier((input_grad, terms, waits))
    near_terms = list(waits)
    grad_expert_in, grad_expert_out = widen(expert_sums)
    grad_rel = jnp.einsum("hgp,gpb->bh", jnp.concatenate(diagonals, axis=0), one_hot_windows, precision=HIGHEST)

    tail = jnp.concatenate([grad_rel.reshape(-1), sums[0, :4]])
    tail_size = tail.shape[0]
    tail = jnp.pad(tail, (0, -tail_size % model_width)).reshape(-1, model_width)
    for distance in distances("dp")[::-1]:
        tail = tail + exchange(tail, "dp", distance)
    pieces = []
    for unused in range(3):
        pieces.append(tail.astype(bf16))
        tail = tail - pieces[-1].astype(f32)
    receivers = lax.axis_size("expert")
    half = finish_dp(terms).reshape(receivers, -1, 3 * width)
    own_rows = half.shape[1]
    half = jnp.concatenate([half] + [jnp.broadcast_to(piece[None], (receivers, *piece.shape)) for piece in pieces], axis=1)
    last_near, grad_expert_in, grad_expert_out = lax.optimization_barrier(
        (swap_blocks(half), grad_expert_in, grad_expert_out)
    )
    near_terms.append(last_near[:, :own_rows])
    tail = jnp.sum(last_near[:, own_rows:].astype(f32), axis=0).reshape(3, -1)
    tail = (tail[0] + tail[1]) + tail[2]
    grad_rel = tail[: bucket_count * head_count].reshape(bucket_count, head_count)
    totals = tail[bucket_count * head_count : tail_size]
    stats = jnp.sqrt(totals[:3] / (totals[3] * model_width))

    dense_out, last_qkv = [jnp.sum(block.astype(f32), axis=0) for block in near_terms]
    dense_qkv = [dense_out[:, model_width + LANES :], last_qkv]
    grad_parts = [total.reshape(-1, many, 3, width) for total, (first, many) in zip(dense_qkv, groups)]
    grad_qkv = jnp.concatenate(grad_parts, axis=1).transpose(0, 2, 1, 3).reshape(-1, 3 * model_width)
    grad_gain_one = jnp.sum(grad_qkv * qkv_weight.astype(f32), axis=1) / attn_gain.astype(f32)
    return (
        output.reshape(inputs.shape),
        input_grad.reshape(inputs.shape),
        grad_gain_one,
        grad_qkv,
        dense_out[:, :model_width],
        dense_out[:, model_width + 1],
        dense_out[:, model_width + SMALL_GAINS : model_width + SMALL_GAINS + experts],
        grad_rel,
        grad_expert_in[None],
        grad_expert_out[None],
        stats,
    )


def solution(mesh):
    in_specs = (
        P(("dp", "expert"), None, None),
        P(("dp", "expert"), None, None),
        P(("dp", "expert")),
        P(("dp", "expert"), None),
        P(("dp", "expert"), None),
        P(("dp", "expert")),
        P(("dp", "expert"), None),
        P(),
        P("expert", None, None),
        P("expert", None, None),
        P(("dp", "expert"), None),
        P(("dp", "expert"), None),
        P(("dp", "expert"), None),
        P(("dp", "expert"), None),
        P(("dp", "expert"), None),
        P(),
    )
    out_specs = (
        P(("dp", "expert"), None, None),
        P(("dp", "expert"), None, None),
        P(("dp", "expert")),
        P(("dp", "expert"), None),
        P(("dp", "expert"), None),
        P(("dp", "expert")),
        P(("dp", "expert"), None),
        P(),
        P("expert", None, "dp"),
        P("expert", "dp", None),
        P(),
    )
    return jax.shard_map(body, mesh=mesh, in_specs=in_specs, out_specs=out_specs, check_vma=False)
```

```python
import functools

import jax
import jax.numpy as jnp
from jax import lax
from jax.experimental import pallas as pl
from jax.experimental.pallas import tpu as pltpu
from jax.sharding import PartitionSpec as P

EPSILON = 1e-06
MASK_STEP = 1e30
ROWS = 256
LANES = 128
STEP_HEADS = 4
VMEM_BYTES = 60 * 2**20
SMALL_GAINS = 2
bf16, f32 = jnp.bfloat16, jnp.float32
NT = (((1,), (1,)), ((), ()))
NN = (((1,), (0,)), ((), ()))
TN = (((0,), (0,)), ((), ()))


def cost(microseconds):
    return pl.CostEstimate(flops=int(microseconds * 1.1e9), bytes_accessed=0, transcendentals=0)


def dot(left, right, dims):
    return lax.dot_general(left, right, dims, preferred_element_type=f32)


def offset_windows(values, reach):
    chunks = (values.shape[0] + 1) // LANES
    turned = jnp.pad(values[::-1], (1, 0)).reshape(chunks, LANES)
    middle = chunks // 2
    return jnp.stack(
        [jnp.concatenate([turned[middle - g], turned[middle - g - 1]]) for g in range(-reach, reach + 1)]
    )


def toeplitz_kernel(reach, window_ref, tile_ref):
    for g in range(2 * reach + 1):
        row = window_ref[0, g : g + 1, :]
        full = jnp.broadcast_to(row, (LANES, 2 * LANES))
        turned = pltpu.roll(full, 0, 1, stride=1, stride_axis=0)
        tile_ref[0, g * LANES : (g + 1) * LANES, :] = turned[:, :LANES]


def toeplitz_tiles(windows):
    heads, groups, width = windows.shape
    return pl.pallas_call(
        functools.partial(toeplitz_kernel, groups // 2),
        grid=(heads,),
        in_specs=[pl.BlockSpec((1, groups, width), lambda n: (n, 0, 0))],
        out_specs=pl.BlockSpec((1, groups * LANES, LANES), lambda n: (n, 0, 0)),
        out_shape=jax.ShapeDtypeStruct((heads, groups * LANES, LANES), f32),
        compiler_params=pltpu.CompilerParams(vmem_limit_bytes=VMEM_BYTES),
        cost_estimate=cost(9),
        name="toeplitz_tiles",
    )(windows)


def head_lanes(rows, head, head_dim):
    lane = lax.broadcasted_iota(jnp.int32, rows.shape, 1)
    return jnp.where((lane >= head * head_dim) & (lane < (head + 1) * head_dim), rows, jnp.zeros_like(rows))


def head_rows(columns, head, head_dim):
    row = lax.broadcasted_iota(jnp.int32, columns.shape, 0)
    return jnp.where((row >= head * head_dim) & (row < (head + 1) * head_dim), columns, jnp.zeros_like(columns))


def bias_tile(bias_ref, head, offset):
    parts = [
        bias_ref[head, pl.ds(pl.multiple_of(offset - LANES * part, LANES), ROWS), :]
        for part in range(ROWS // LANES)
    ]
    return jnp.concatenate(parts, axis=1)


def forward_kernel(head_dim, reach, normalize, low_ref, high_ref, in_ref, small_ref, weight_ref, qx_ref, kx_ref, bias_ref, *refs):
    packed_ref, mix_ref, lse_ref, normed_ref, vt_ref = refs[-5:] if normalize else (*refs[-4:-1], in_ref, refs[-1])
    length, width = mix_ref.shape
    heads = width // head_dim
    scale = head_dim ** (-0.5)
    chunks = [slice(at, at + ROWS) for at in range(0, length, ROWS)]

    if normalize:

        @pl.when(pl.program_id(0) == 0)
        def _():
            gain = gain_row(small_ref, 0)
            for here in chunks:
                rows = in_ref[here].astype(f32)
                normed_ref[here] = (rows * row_factor(rows) * gain).astype(bf16)

    for here in chunks:
        packed_ref[here] = dot(normed_ref[here], weight_ref[...], NN).astype(bf16)
    q_ref, k_ref, v_ref = [packed_ref.at[:, part * width : (part + 1) * width] for part in range(3)]
    for c in range(width // LANES):
        vt_ref[c * LANES : (c + 1) * LANES, :] = v_ref[:, c * LANES : (c + 1) * LANES].T
    per = LANES // head_dim

    def one_block(qb, unused):
        first = pl.multiple_of(qb * ROWS, ROWS)
        qx = qx_ref[:, pl.ds(first, ROWS)]
        queries = []
        for c in range(width // LANES):
            pair = (q_ref[pl.ds(first, ROWS), c * LANES : (c + 1) * LANES] * jnp.asarray(scale, bf16)).T
            queries += [jnp.concatenate([head_rows(pair, h, head_dim), qx], axis=0) for h in range(per)]

        def one_tile(kb, carry):
            keys_at = pl.multiple_of(kb * ROWS, ROWS)
            offset = pl.multiple_of(keys_at - first + LANES * reach, LANES)
            kx = kx_ref[pl.ds(keys_at, ROWS), :]
            out = []
            all_scores = []
            for h in range(heads):
                c = h // per
                keys = jnp.concatenate([k_ref[pl.ds(keys_at, ROWS), c * LANES : (c + 1) * LANES], kx], axis=1)
                all_scores.append(dot(keys, queries[h], NN))
            soft = []
            for h in range(heads):
                peak, total, mixed = carry[h]
                scores = all_scores[h] + bias_tile(bias_ref, h, offset)
                new_peak = jnp.maximum(peak, jnp.max(scores, axis=0, keepdims=True))
                weights = jnp.exp(scores - new_peak)
                shrink = jnp.exp(peak - new_peak)
                total = total * shrink + jnp.sum(weights, axis=0, keepdims=True)
                soft.append((new_peak, total, shrink, weights.astype(bf16)))
            for h in range(heads):
                new_peak, total, shrink, weights = soft[h]
                values = vt_ref[h * head_dim : (h + 1) * head_dim, pl.ds(keys_at, ROWS)]
                mixed = carry[h][2] * shrink + dot(values, weights, NN)
                out.append((new_peak, total, mixed))
            return tuple(out)

        start = tuple(
            (jnp.full((1, ROWS), -3e38, f32), jnp.zeros((1, ROWS), f32), jnp.zeros((head_dim, ROWS), f32))
            for h in range(heads)
        )
        done = lax.fori_loop(low_ref[qb], high_ref[qb], one_tile, start)
        for c in range(width // LANES):
            rows = jnp.concatenate([done[h][2] / done[h][1] for h in range(c * per, (c + 1) * per)], axis=0)
            mix_ref[pl.ds(first, ROWS), c * LANES : (c + 1) * LANES] = rows.T.astype(bf16)
        for h in range(heads):
            lse_ref[0, h : h + 1, pl.ds(first, ROWS)] = done[h][0] + jnp.log(done[h][1])
        return unused

    lax.fori_loop(0, length // ROWS, one_block, 0)


def probs_kernel(head_dim, reach, low_ref, high_ref, q_ref, k_ref, qx_ref, kx_ref, bias_ref, lse_ref, probs_ref):
    length, width = q_ref.shape
    heads = width // head_dim
    scale = head_dim ** (-0.5)
    per = LANES // head_dim

    def one_block(qb, unused):
        first = pl.multiple_of(qb * ROWS, ROWS)
        qx = qx_ref[:, pl.ds(first, ROWS)]
        queries = []
        for c in range(width // LANES):
            pair = (q_ref[pl.ds(first, ROWS), c * LANES : (c + 1) * LANES] * jnp.asarray(scale, bf16)).T
            queries += [jnp.concatenate([head_rows(pair, h, head_dim), qx], axis=0) for h in range(per)]
        lses = [lse_ref[0, h : h + 1, pl.ds(first, ROWS)] for h in range(heads)]

        def one_tile(kb, unused):
            keys_at = pl.multiple_of(kb * ROWS, ROWS)
            offset = pl.multiple_of(keys_at - first + LANES * reach, LANES)
            kx = kx_ref[pl.ds(keys_at, ROWS), :]
            all_scores = []
            for h in range(heads):
                c = h // per
                keys = jnp.concatenate([k_ref[pl.ds(keys_at, ROWS), c * LANES : (c + 1) * LANES], kx], axis=1)
                all_scores.append(dot(keys, queries[h], NN))
            for h in range(heads):
                weights = jnp.exp(all_scores[h] + bias_tile(bias_ref, h, offset) - lses[h])
                probs_ref[h, qb, pl.ds(keys_at, ROWS), :] = weights.astype(bf16)
            return unused

        return lax.fori_loop(low_ref[qb], high_ref[qb], one_tile, unused)

    lax.fori_loop(0, length // ROWS, one_block, 0)


def diagonal_sums(tiles):
    groups = tiles.shape[0]
    step = LANES // 2
    zero = jnp.zeros((groups, step, LANES), f32)
    turned = jnp.concatenate([tiles[:, :step], zero], axis=2) + pltpu.roll(
        jnp.concatenate([tiles[:, step:], zero], axis=2), 2 * LANES - step, 2
    )
    while step > 8:
        step //= 2
        turned = turned[:, :step] + pltpu.roll(turned[:, step:], 2 * LANES - step, 2)
    while step > 1:
        step //= 2
        turned = turned + pltpu.roll(pltpu.roll(turned, 2 * LANES - step, 2), 8 - step, 1)
    return turned[:, 0]


def backward_kernel(head_dim, reach, low_ref, high_ref, q_ref, k_ref, v_ref, dmix_ref, mix_ref, probs_ref,
                    grad_ref, diag_ref, kt_ref, dk_ref, dv_ref, along_ref):
    length, width = q_ref.shape
    heads = width // head_dim
    scale = head_dim ** (-0.5)
    per = LANES // head_dim
    for c in range(width // LANES):
        kt_ref[c * LANES : (c + 1) * LANES, :] = k_ref[:, c * LANES : (c + 1) * LANES].T
    dk_ref[...] = jnp.zeros_like(dk_ref)
    dv_ref[...] = jnp.zeros_like(dv_ref)
    along_ref[...] = jnp.zeros_like(along_ref)

    def one_block(qb, unused):
        first = pl.multiple_of(qb * ROWS, ROWS)
        queries, d_mixes, deltas, d_turned = [], [], [], []
        for c in range(width // LANES):
            lanes = slice(c * LANES, (c + 1) * LANES)
            query = q_ref[pl.ds(first, ROWS), lanes] * jnp.asarray(scale, bf16)
            d_mix = dmix_ref[pl.ds(first, ROWS), lanes]
            product = (d_mix.astype(f32) * mix_ref[pl.ds(first, ROWS), lanes].astype(f32)).T
            d_mix_turned = d_mix.T
            for h in range(per):
                queries.append(head_lanes(query, h, head_dim))
                d_mixes.append(head_lanes(d_mix, h, head_dim))
                d_turned.append(head_rows(d_mix_turned, h, head_dim))
                deltas.append(jnp.sum(product[h * head_dim : (h + 1) * head_dim], axis=0, keepdims=True))

        def one_tile(kb, carry):
            keys_at = pl.multiple_of(kb * ROWS, ROWS)
            offset = pl.multiple_of(keys_at - first + LANES * reach, LANES)
            out = []
            low_weights, low_scores, all_weights = [], [], []
            for h in range(heads):
                lanes = slice(h // per * LANES, (h // per + 1) * LANES)
                all_weights.append(dot(v_ref[pl.ds(keys_at, ROWS), lanes], d_turned[h], NN))
            for h in range(heads):
                weights = probs_ref[h, qb, pl.ds(keys_at, ROWS), :]
                d_scores = weights.astype(f32) * (all_weights[h] - deltas[h])
                for part in range(ROWS // LANES):
                    at = pl.ds(pl.multiple_of(offset - LANES * part, LANES), ROWS)
                    along_ref[h, at, :] += d_scores[:, part * LANES : (part + 1) * LANES]
                low_weights.append(weights)
                low_scores.append(d_scores.astype(bf16))
            for h in range(heads):
                keys_turned = kt_ref[h * head_dim : (h + 1) * head_dim, pl.ds(keys_at, ROWS)]
                out.append(carry[h] + dot(keys_turned, low_scores[h], NN))
            for c in range(width // LANES):
                mine = range(c * per, (c + 1) * per)
                lanes = slice(c * LANES, (c + 1) * LANES)
                dv_ref[pl.ds(keys_at, ROWS), lanes] += dot(
                    jnp.concatenate([low_weights[h] for h in mine], axis=1), jnp.concatenate([d_mixes[h] for h in mine], axis=0), NN)
                dk_ref[pl.ds(keys_at, ROWS), lanes] += dot(
                    jnp.concatenate([low_scores[h] for h in mine], axis=1), jnp.concatenate([queries[h] for h in mine], axis=0), NN)
            return tuple(out)

        start = tuple(jnp.zeros((head_dim, ROWS), f32) for h in range(heads))
        done = lax.fori_loop(low_ref[qb], high_ref[qb], one_tile, start)
        for c in range(width // LANES):
            rows = jnp.concatenate([done[h] for h in range(c * per, (c + 1) * per)], axis=0) * scale
            grad_ref[pl.ds(first, ROWS), c * LANES : (c + 1) * LANES] = rows.T.astype(bf16)
        return unused

    lax.fori_loop(0, length // ROWS, one_block, 0)
    grad_ref[:, width : 2 * width] = dk_ref[...].astype(bf16)
    grad_ref[:, 2 * width :] = dv_ref[...].astype(bf16)
    for h in range(heads):
        diag_ref[h] = diagonal_sums(along_ref[h].reshape(2 * reach + 1, LANES, LANES))


def tile_bounds(segments):
    length = segments.shape[0]
    blocks = segments.reshape(length // ROWS, ROWS)
    starts = jnp.sum((segments[None, :] < blocks[:, :1]).astype(jnp.int32), axis=1)
    ends = jnp.sum((segments[None, :] <= blocks[:, -1:]).astype(jnp.int32), axis=1)
    return starts // ROWS, (ends + ROWS - 1) // ROWS


def mask_columns(segments, validity, segment_count=8):
    length = segments.shape[0]
    short = 1
    while short * (short + 1) < length:
        short += 1
    at = jnp.arange(length, dtype=jnp.int32)
    lane = jnp.arange(LANES, dtype=jnp.int32)[None, :]
    in_first = (lane >= segment_count) & (lane < segment_count + short)
    in_second = (lane >= segment_count + short) & (lane < segment_count + 2 * short + 1)
    mine = (
        (lane == segments[:, None])
        | (in_first & (lane - segment_count == (at % short)[:, None]))
        | (in_second & (lane - segment_count - short == (at % (short + 1))[:, None]))
    )
    used = lane < segment_count + 2 * short + 1
    query_side = jnp.where(used & ~mine, -MASK_STEP, 0.0).astype(bf16).T
    real = (validity == 1)[:, None]
    key_side = jnp.where(mine & jnp.where(real, lane < segment_count, lane >= segment_count), 1.0, 0.0).astype(bf16)
    return query_side, key_side


def attend_forward(rows_in, smalls, small_at, weights, query_side, key_side, bounds, tiles, mixed, first, steps, head_dim):
    length, model_width = rows_in.shape
    width = STEP_HEADS * head_dim
    reach = tiles.shape[1] // LANES // 2
    shared = [] if mixed is None else [mixed]
    whole = lambda *_: (0, 0)
    grid_spec = pltpu.PrefetchScalarGridSpec(
        num_scalar_prefetch=2,
        grid=(steps,),
        in_specs=[
            pl.BlockSpec((length, model_width), whole),
            pl.BlockSpec((model_width, LANES), lambda p, *_: (0, small_at)),
            pl.BlockSpec((model_width, 3 * width), lambda p, *_: (0, p)),
            pl.BlockSpec((LANES, length), whole),
            pl.BlockSpec((length, LANES), whole),
            pl.BlockSpec((STEP_HEADS, tiles.shape[1], LANES), lambda p, *_: (first + p, 0, 0)),
        ]
        + [pl.BlockSpec(memory_space=pl.ANY)] * len(shared),
        out_specs=[
            pl.BlockSpec((length, 3 * width), lambda p, *_: (0, p)),
            pl.BlockSpec((length, width), lambda p, *_: (0, first + p)),
            pl.BlockSpec((1, STEP_HEADS, length), lambda p, *_: (p, 0, 0)),
        ]
        + [pl.BlockSpec((length, model_width), whole)] * (not shared),
        scratch_shapes=[pltpu.VMEM((width, length), bf16)],
    )
    return pl.pallas_call(
        functools.partial(forward_kernel, head_dim, reach, not shared),
        grid_spec=grid_spec,
        out_shape=[
            jax.ShapeDtypeStruct((length, 3 * width * steps), bf16),
            jax.ShapeDtypeStruct((length, tiles.shape[0] * head_dim), bf16),
            jax.ShapeDtypeStruct((steps, STEP_HEADS, length), f32),
        ]
        + [jax.ShapeDtypeStruct((length, model_width), bf16)] * (not shared),
        input_output_aliases={8: 1} if shared else {},
        compiler_params=pltpu.CompilerParams(vmem_limit_bytes=56 * 2**20),
        cost_estimate=cost(1),
        name="attend_forward",
    )(*bounds, rows_in, smalls, weights, query_side, key_side, tiles, *shared)


def attend_probs(packed, lse, query_side, key_side, bounds, tiles, first, head_dim):
    length = packed.shape[0]
    width = STEP_HEADS * head_dim
    steps = packed.shape[1] // 3 // width
    reach = tiles.shape[1] // LANES // 2
    whole = lambda *_: (0, 0)
    blocks = length // ROWS
    grid_spec = pltpu.PrefetchScalarGridSpec(
        num_scalar_prefetch=2,
        grid=(steps,),
        in_specs=[
            pl.BlockSpec((length, width), lambda p, *_: (0, 3 * p)),
            pl.BlockSpec((length, width), lambda p, *_: (0, 3 * p + 1)),
            pl.BlockSpec((LANES, length), whole),
            pl.BlockSpec((length, LANES), whole),
            pl.BlockSpec((STEP_HEADS, tiles.shape[1], LANES), lambda p, *_: (first + p, 0, 0)),
            pl.BlockSpec((1, STEP_HEADS, length), lambda p, *_: (p, 0, 0)),
        ],
        out_specs=pl.BlockSpec((STEP_HEADS, blocks, length, ROWS), lambda p, *_: (p, 0, 0, 0)),
    )
    return pl.pallas_call(
        functools.partial(probs_kernel, head_dim, reach),
        grid_spec=grid_spec,
        out_shape=jax.ShapeDtypeStruct((steps * STEP_HEADS, blocks, length, ROWS), bf16),
        compiler_params=pltpu.CompilerParams(vmem_limit_bytes=56 * 2**20),
        cost_estimate=cost(9 * steps),
        name="attend_probs",
    )(*bounds, packed, packed, query_side, key_side, tiles, lse)


def attend_backward(packed, d_mix, mix, probs, bounds, groups, first, head_dim):
    length = packed.shape[0]
    width = STEP_HEADS * head_dim
    steps = packed.shape[1] // 3 // width
    whole = lambda *_: (0, 0)
    grid_spec = pltpu.PrefetchScalarGridSpec(
        num_scalar_prefetch=2,
        grid=(steps,),
        in_specs=[
            pl.BlockSpec((length, width), lambda p, *_: (0, 3 * p)),
            pl.BlockSpec((length, width), lambda p, *_: (0, 3 * p + 1)),
            pl.BlockSpec((length, width), lambda p, *_: (0, 3 * p + 2)),
            pl.BlockSpec((length, width), lambda p, *_: (0, first + p)),
            pl.BlockSpec((length, width), lambda p, *_: (0, first + p)),
            pl.BlockSpec((STEP_HEADS, *probs.shape[1:]), lambda p, *_: (p, 0, 0, 0)),
        ],
        out_specs=[
            pl.BlockSpec((length, 3 * width), lambda p, *_: (0, p)),
            pl.BlockSpec((STEP_HEADS, groups, 2 * LANES), lambda p, *_: (p, 0, 0)),
        ],
        scratch_shapes=[
            pltpu.VMEM((width, length), bf16),
            pltpu.VMEM((length, width), f32),
            pltpu.VMEM((length, width), f32),
            pltpu.VMEM((STEP_HEADS, groups * LANES, LANES), f32),
        ],
    )
    return pl.pallas_call(
        functools.partial(backward_kernel, head_dim, groups // 2),
        grid_spec=grid_spec,
        out_shape=[
            jax.ShapeDtypeStruct((length, 3 * width * steps), bf16),
            jax.ShapeDtypeStruct((steps * STEP_HEADS, groups, 2 * LANES), f32),
        ],
        compiler_params=pltpu.CompilerParams(vmem_limit_bytes=56 * 2**20),
        cost_estimate=cost(15 * steps),
        name="attend_backward",
    )(*bounds, packed, packed, packed, d_mix, mix, probs)


def spread_kernel(width, near_steps, weight_ref, out_weight_ref, first_ref, second_ref, router_ref, *outs):
    receivers, count = outs[0].shape[:2]
    steps = weight_ref.shape[1] // (3 * width)
    row = lax.broadcasted_iota(jnp.int32, (count, count), 0)
    same = row == lax.broadcasted_iota(jnp.int32, (count, count), 1)
    columns = [
        jnp.sum(jnp.where(same, jnp.broadcast_to(ref[...].astype(f32), same.shape), 0.0), axis=1, keepdims=True)
        for ref in (first_ref, second_ref)
    ]
    columns.append(dot(jnp.where(same, 1.0, 0.0).astype(bf16), router_ref[...], NT))
    used = SMALL_GAINS + router_ref.shape[0]
    columns.append(jnp.zeros((count, -used % LANES), f32))
    pieces = [
        weight_ref[:, (part * steps + p) * width : (part * steps + p + 1) * width] for p in range(steps) for part in range(3)
    ]
    groups = [
        pieces[: 3 * near_steps] + [jnp.concatenate(columns, axis=1).astype(bf16)],
        pieces[3 * near_steps :] + [out_weight_ref[...]],
    ]
    for group, out_ref in zip(groups, outs):
        at = 0
        for piece in group:
            out_ref[:, :, at : at + piece.shape[1]] = jnp.broadcast_to(piece[None], (receivers, *piece.shape))
            at += piece.shape[1]


def spread_shard(weight, out_weight, first_gain, second_gain, router, width, near_steps, receivers):
    rows, columns = weight.shape
    small = SMALL_GAINS + router.shape[1]
    small += -small % LANES
    near = 3 * width * near_steps
    return pl.pallas_call(
        functools.partial(spread_kernel, width, near_steps),
        out_shape=[
            jax.ShapeDtypeStruct((receivers, rows, near + small), bf16),
            jax.ShapeDtypeStruct((receivers, rows, columns - near + out_weight.shape[1]), bf16),
        ],
        compiler_params=pltpu.CompilerParams(vmem_limit_bytes=VMEM_BYTES),
        cost_estimate=cost(2),
        name="spread_shard",
    )(weight, out_weight, first_gain.reshape(1, rows), second_gain.reshape(1, rows), router.T)


def expert_kernel(experts, me_ref, rows_ref, in_ref, small_ref, d_hidden_ref, d_rows_ref, d_logits_ref, gate_ref,
                  probs_ref, total_ref, d_gate_ref):
    step = pl.program_id(0)
    lane = lax.broadcasted_iota(jnp.int32, probs_ref.shape, 1)
    chosen = lane == me_ref[0] + SMALL_GAINS

    @pl.when(step == 0)
    def _():
        logits = dot(rows_ref[...], small_ref[...], NN)
        logits = jnp.where((lane >= SMALL_GAINS) & (lane < SMALL_GAINS + experts), logits, -MASK_STEP)
        raised = jnp.exp(logits - jnp.max(logits, axis=1, keepdims=True))
        probs = raised / jnp.sum(raised, axis=1, keepdims=True)
        probs_ref[...] = probs
        gate_ref[...] = jnp.sum(jnp.where(chosen, probs, 0.0), axis=1, keepdims=True)
        total_ref[...] = jnp.zeros_like(total_ref)
        d_gate_ref[...] = jnp.zeros_like(d_gate_ref)

    count = rows_ref.shape[0]
    chunk = 256 if count % 256 == 0 else count
    weights = in_ref[...]
    pres = [dot(rows_ref[at : at + chunk], weights, NN) for at in range(0, count, chunk)]
    lows = []
    for i, at in enumerate(range(0, count, chunk)):
        here = slice(at, at + chunk)
        unit, slope = gelu_and_slope(pres[i].astype(bf16))
        d_hidden = d_hidden_ref[here]
        d_gate_ref[here] += jnp.sum((unit * d_hidden).astype(f32), axis=1, keepdims=True)
        lows.append(d_hidden * slope)
    for i, at in enumerate(range(0, count, chunk)):
        total_ref[at : at + chunk] += dot(lows[i], weights, NT)

    @pl.when(step == pl.num_programs(0) - 1)
    def _():
        d_logits = (probs_ref[...] * (chosen.astype(f32) - gate_ref[...]) * d_gate_ref[...]).astype(bf16)
        d_logits_ref[...] = d_logits
        d_rows_ref[...] = (gate_ref[...] * total_ref[...] + dot(d_logits, small_ref[...], NT)).astype(bf16)


def run_expert(me, rows, w_in, weights, small_at, d_hidden, experts):
    count, width = rows.shape
    hidden_width = w_in.shape[1]
    block = 768 if hidden_width % 768 == 0 else 512
    whole = lambda f, *_: (0, 0)
    grid_spec = pltpu.PrefetchScalarGridSpec(
        num_scalar_prefetch=1,
        grid=(hidden_width // block,),
        in_specs=[
            pl.BlockSpec((count, width), whole),
            pl.BlockSpec((width, block), lambda f, *_: (0, f)),
            pl.BlockSpec((width, LANES), lambda f, *_: (0, small_at)),
            pl.BlockSpec((count, block), lambda f, *_: (0, f)),
        ],
        out_specs=[
            pl.BlockSpec((count, width), whole),
            pl.BlockSpec((count, LANES), whole),
            pl.BlockSpec((count, 1), whole),
        ],
        scratch_shapes=[pltpu.VMEM((count, LANES), f32), pltpu.VMEM((count, width), f32), pltpu.VMEM((count, 1), f32)],
    )
    return pl.pallas_call(
        functools.partial(expert_kernel, experts),
        grid_spec=grid_spec,
        out_shape=[
            jax.ShapeDtypeStruct((count, width), bf16),
            jax.ShapeDtypeStruct((count, LANES), bf16),
            jax.ShapeDtypeStruct((count, 1), f32),
        ],
        compiler_params=pltpu.CompilerParams(vmem_limit_bytes=VMEM_BYTES),
        cost_estimate=cost(18),
        name="run_expert",
    )(me.reshape(1), rows, w_in, weights, d_hidden)


def expert_grads_kernel(gate_ref, rows_ref, in_ref, d_hidden_ref, d_slots_ref, back_ref, d_logits_ref, parts_ref,
                        moe_ref, router_ref, d_out_ref, total_ref):
    step = pl.program_id(0)

    @pl.when(step == 0)
    def _():
        d_out_ref[...] = (gate_ref[...] * d_slots_ref[...].astype(f32)).astype(bf16)
        total_ref[...] = jnp.zeros_like(total_ref)
        router_ref[...] = dot(rows_ref[...], d_logits_ref[...], TN)

    count = rows_ref.shape[0]
    chunk = 256 if count % 256 == 0 else count
    pres = [dot(rows_ref[at : at + chunk], in_ref[...], NN) for at in range(0, count, chunk)]
    units, lows = [], []
    for i, at in enumerate(range(0, count, chunk)):
        here = slice(at, at + chunk)
        unit, slope = gelu_and_slope(pres[i])
        units.append(unit.astype(bf16))
        lows.append((gate_ref[here] * d_hidden_ref[here].astype(f32) * slope).astype(bf16))
    hidden = jnp.concatenate(units, axis=0)
    parts_ref[0, 0] = dot(jnp.concatenate(lows, axis=0), rows_ref[...], TN).astype(bf16)
    parts_ref[0, 1] = dot(hidden, d_out_ref[...], TN).astype(bf16)
    total_ref[...] += dot(hidden, back_ref[...], NN)

    @pl.when(step == pl.num_programs(0) - 1)
    def _():
        moe_ref[...] = (gate_ref[...] * total_ref[...]).astype(bf16)


def expert_grads(gate, rows, w_in, d_hidden, d_slots, w_back, d_logits, owners):
    count, width = rows.shape
    block = w_in.shape[1] // owners
    whole = lambda f: (0, 0)
    full = pl.BlockSpec((count, width), whole)
    return pl.pallas_call(
        expert_grads_kernel,
        grid=(owners,),
        in_specs=[
            pl.BlockSpec((count, 1), whole),
            full,
            pl.BlockSpec((width, block), lambda f: (0, f)),
            pl.BlockSpec((count, block), lambda f: (0, f)),
            full,
            pl.BlockSpec((block, width), lambda f: (f, 0)),
            pl.BlockSpec((count, LANES), whole),
        ],
        out_specs=[
            pl.BlockSpec((1, 2, block, width), lambda f: (f, 0, 0, 0)),
            full,
            pl.BlockSpec((width, LANES), whole),
        ],
        out_shape=[
            jax.ShapeDtypeStruct((owners, 2, block, width), bf16),
            jax.ShapeDtypeStruct((count, width), bf16),
            jax.ShapeDtypeStruct((width, LANES), f32),
        ],
        scratch_shapes=[pltpu.VMEM((count, width), bf16), pltpu.VMEM((count, width), f32)],
        compiler_params=pltpu.CompilerParams(vmem_limit_bytes=VMEM_BYTES),
        cost_estimate=cost(35),
        name="expert_grads",
    )(gate, rows, w_in, d_hidden, d_slots, w_back, d_logits)


def gain_row(small_ref, lane):
    return small_ref[...].astype(f32).T[lane : lane + 1]


def row_factor(rows):
    return lax.rsqrt(jnp.mean(rows * rows, axis=1, keepdims=True) + EPSILON)


def middle_kernel(row_steps, mixed_ref, weight_ref, in_ref, small_ref, slot_ref, rows_ref, slots_ref, normed_ref):
    step = pl.program_id(0)

    @pl.when(step < row_steps)
    def _():
        count = in_ref.shape[0]
        first = pl.multiple_of(step * count, count)
        chunks = [slice(at, at + ROWS) for at in range(0, count, ROWS)]
        gain = gain_row(small_ref, 1)
        projected = [dot(mixed_ref[here], weight_ref[...], NN) for here in chunks]
        for here, attn in zip(chunks, projected):
            rows = in_ref[here].astype(f32) + attn
            rows_ref[here] = rows
            normed_ref[pl.ds(first + here.start, ROWS)] = (rows * row_factor(rows) * gain).astype(bf16)

    @pl.when(step >= row_steps)
    def _():
        fill_kernel(slot_ref, normed_ref, slots_ref, (step - row_steps) * slots_ref.shape[0])


def fill_kernel(slot_ref, rows_ref, slots_ref, first=0):
    slots, count = slots_ref.shape[0], rows_ref.shape[0]
    chunk = ROWS if slots % ROWS == 0 else slots
    for at in range(0, slots, chunk):
        slot = lax.broadcasted_iota(jnp.int32, (chunk, count), 0) + (first + at)
        place = jnp.where(slot == slot_ref[...], 1.0, 0.0).astype(bf16)
        slots_ref[at : at + chunk] = dot(place, rows_ref[...], NN).astype(bf16)


def across(row):
    return jnp.broadcast_to(row.astype(f32), (LANES, row.shape[1])).T


def row_chunks(ref):
    return [slice(at, at + ROWS) for at in range(0, ref.shape[0], ROWS)]


def row_block(count):
    return 2 * ROWS if count % (2 * ROWS) == 0 else ROWS


def read_slots(slot_row, blocks_ref):
    slots = blocks_ref.shape[0]
    mine = jnp.concatenate([across(slot_row)] * pl.cdiv(slots, LANES), axis=1)[:, :slots]
    slot = lax.broadcasted_iota(jnp.int32, mine.shape, 1).astype(f32)
    return dot(jnp.where(slot == mine, 1.0, 0.0).astype(bf16), blocks_ref[...], NN)


def fill_slots(slot_row, rows, slots):
    return pl.pallas_call(
        fill_kernel,
        out_shape=jax.ShapeDtypeStruct((slots, rows.shape[1]), bf16),
        compiler_params=pltpu.CompilerParams(vmem_limit_bytes=VMEM_BYTES),
        cost_estimate=cost(3.5),
        name="fill_slots",
    )(slot_row, rows)


def run_middle(mixed, weights, at, rows_in, smalls, small_at, slot_row, slots):
    count, width = rows_in.shape
    whole = lambda i: (0, 0)
    row_steps = 2 if count % (2 * ROWS) == 0 else 1
    slot_steps = 2 if slots % 32 == 0 else 1
    part = pl.BlockSpec((count // row_steps, width), lambda i: (jnp.minimum(i, row_steps - 1), 0))
    return pl.pallas_call(
        functools.partial(middle_kernel, row_steps),
        grid=(row_steps + slot_steps,),
        in_specs=[
            part,
            pl.BlockSpec((width, width), lambda i: (0, at)),
            part,
            pl.BlockSpec((width, LANES), lambda i: (0, small_at)),
            pl.BlockSpec((1, count), whole),
        ],
        out_specs=[part, pl.BlockSpec((slots // slot_steps, width), lambda i: (jnp.maximum(i - row_steps, 0), 0))],
        out_shape=[jax.ShapeDtypeStruct((count, width), f32), jax.ShapeDtypeStruct((slots, width), bf16)],
        scratch_shapes=[pltpu.VMEM((count, width), bf16)],
        compiler_params=pltpu.CompilerParams(vmem_limit_bytes=VMEM_BYTES),
        cost_estimate=cost(5),
        name="run_middle",
    )(mixed, weights, rows_in, smalls, slot_row)


def middle_back_kernel(blocks_ref, slot_ref, rows_ref, small_ref, top_ref, weight_ref, d_mid_ref, d_mixed_ref, d_gain_ref):
    @pl.when(pl.program_id(0) == 0)
    def _():
        d_gain_ref[...] = jnp.zeros_like(d_gain_ref)

    gain = gain_row(small_ref, 1)
    chunks = row_chunks(rows_ref)
    picked = [read_slots(slot_ref[:, here], blocks_ref) for here in chunks]
    lows = []
    for here, d_normed in zip(chunks, picked):
        rows = rows_ref[here]
        factor = row_factor(rows)
        normed = rows * factor
        weighted = d_normed * gain
        product = d_normed * normed
        d_mid = top_ref[here].astype(f32) + factor * (weighted - normed * jnp.mean(product * gain, axis=1, keepdims=True))
        lows.append(d_mid.astype(bf16))
        d_mid_ref[here] = lows[-1]
        d_gain_ref[...] += jnp.sum(product, axis=0, keepdims=True)
    for here, low in zip(chunks, lows):
        d_mixed_ref[here] = dot(low, weight_ref[...], NT).astype(bf16)


def run_middle_back(blocks, slot_row, rows, smalls, small_at, top, weights, at):
    count, width = rows.shape
    whole = lambda *_: (0, 0)
    part = pl.BlockSpec((row_block(count), width), lambda i: (i, 0))
    return pl.pallas_call(
        middle_back_kernel,
        grid=(count // row_block(count),),
        in_specs=[
            pl.BlockSpec(blocks.shape, whole),
            pl.BlockSpec((1, row_block(count)), lambda i: (0, i)),
            part,
            pl.BlockSpec((width, LANES), lambda i: (0, small_at)),
            part,
            pl.BlockSpec((width, width), lambda i: (0, at)),
        ],
        out_specs=[part, part, pl.BlockSpec((1, width), whole)],
        out_shape=[
            jax.ShapeDtypeStruct((count, width), bf16),
            jax.ShapeDtypeStruct((count, width), bf16),
            jax.ShapeDtypeStruct((1, width), f32),
        ],
        compiler_params=pltpu.CompilerParams(vmem_limit_bytes=VMEM_BYTES),
        cost_estimate=cost(7),
        name="run_middle_back",
    )(blocks, slot_row, rows, smalls, top, weights)


def first_back_kernel(count, small_at, in_ref, d_mid_ref, *refs):
    d_in_ref = refs[2 * count]
    gain = gain_row(refs[count].at[:, small_at * LANES : (small_at + 1) * LANES], 0)
    chunks = row_chunks(in_ref)
    sums = []
    for here in chunks:
        total = 0.0
        for part_ref, weight_ref in zip(refs[:count], refs[count:]):
            total = total + dot(part_ref[here], weight_ref[:, : part_ref.shape[1]], NT)
        sums.append(total)
    for here, total in zip(chunks, sums):
        rows = in_ref[here].astype(f32)
        factor = row_factor(rows)
        normed = rows * factor
        weighted = total * gain
        d_in_ref[here] = d_mid_ref[here].astype(f32) + factor * (
            weighted - normed * jnp.mean(weighted * normed, axis=1, keepdims=True)
        )


def run_first_back(rows_in, small_at, d_mid, parts, weights):
    count, width = rows_in.shape
    whole = lambda *_: (0, 0)
    part = pl.BlockSpec((row_block(count), width), lambda i: (i, 0))
    return pl.pallas_call(
        functools.partial(first_back_kernel, len(parts), small_at),
        grid=(count // row_block(count),),
        in_specs=[part, part]
        + [pl.BlockSpec((row_block(count), columns.shape[1]), lambda i: (i, 0)) for columns in parts]
        + [pl.BlockSpec(weight.shape, whole) for weight in weights],
        out_specs=part,
        out_shape=jax.ShapeDtypeStruct(rows_in.shape, f32),
        compiler_params=pltpu.CompilerParams(vmem_limit_bytes=VMEM_BYTES),
        cost_estimate=cost(8),
        name="run_first_back",
    )(rows_in, d_mid, *parts, *weights)


def output_kernel(blocks_ref, slot_ref, rows_ref, in_ref, live_ref, out_ref, sums_ref):
    chunks = row_chunks(rows_ref)
    picked = [read_slots(slot_ref[:, here], blocks_ref) for here in chunks]
    lane = lax.broadcasted_iota(jnp.int32, (1, LANES), 1)
    total = jnp.zeros((1, LANES), f32)
    for here, moe in zip(chunks, picked):
        rows = rows_ref[here]
        final = rows + moe
        out_ref[here] = final.astype(bf16)
        live = across(live_ref[:, here])[:, :1]
        sums = jnp.where(lane == 3, jnp.sum(live, axis=0, keepdims=True), 0.0)
        for i, part in enumerate((in_ref[here].astype(f32), rows, final)):
            per_row = live * jnp.sum(part * part, axis=1, keepdims=True)
            sums = jnp.where(lane == i, jnp.sum(per_row, axis=0, keepdims=True), sums)
        total += sums

    @pl.when(pl.program_id(0) == 0)
    def _():
        sums_ref[...] = jnp.zeros_like(sums_ref)

    sums_ref[...] += total


def run_output(blocks, slot_row, rows, rows_in, live):
    count, width = rows.shape
    whole = lambda *_: (0, 0)
    part = pl.BlockSpec((row_block(count), width), lambda i: (i, 0))
    column = pl.BlockSpec((1, row_block(count)), lambda i: (0, i))
    return pl.pallas_call(
        output_kernel,
        grid=(count // row_block(count),),
        in_specs=[pl.BlockSpec(blocks.shape, whole), column, part, part, column],
        out_specs=[part, pl.BlockSpec((1, LANES), whole)],
        out_shape=[jax.ShapeDtypeStruct((count, width), bf16), jax.ShapeDtypeStruct((1, LANES), f32)],
        compiler_params=pltpu.CompilerParams(vmem_limit_bytes=VMEM_BYTES),
        cost_estimate=cost(4),
        name="run_output",
    )(blocks, slot_row, rows, rows_in, live)


def dense_grads_kernel(mixed_ref, d_attn_ref, router_ref, gain_ref, normed_ref, parts_ref, grad_ref):
    width = d_attn_ref.shape[1]
    grad_ref[:, :width] = dot(mixed_ref[...], d_attn_ref[...], TN).astype(bf16)
    lane = lax.broadcasted_iota(jnp.int32, router_ref.shape, 1)
    grad_ref[:, width : width + LANES] = jnp.where(lane == 1, across(gain_ref[...]), router_ref[...]).astype(bf16)
    grad_ref[:, width + LANES :] = dot(normed_ref[...], parts_ref[...], TN).astype(bf16)


def run_dense_grads(mixed, d_attn, grad_router, grad_gain, normed, parts):
    count, width = mixed.shape
    columns = parts.shape[1]
    block = ROWS if width % ROWS == 0 else width
    whole = lambda i: (0, 0)
    part = pl.BlockSpec((count, block), lambda i: (0, i))
    return pl.pallas_call(
        dense_grads_kernel,
        grid=(width // block,),
        in_specs=[
            part,
            pl.BlockSpec((count, width), whole),
            pl.BlockSpec((block, LANES), lambda i: (i, 0)),
            pl.BlockSpec((1, block), lambda i: (0, i)),
            part,
            pl.BlockSpec((count, columns), whole),
        ],
        out_specs=pl.BlockSpec((block, width + LANES + columns), lambda i: (i, 0)),
        out_shape=jax.ShapeDtypeStruct((width, width + LANES + columns), bf16),
        compiler_params=pltpu.CompilerParams(vmem_limit_bytes=VMEM_BYTES),
        cost_estimate=cost(7),
        name="run_dense_grads",
    )(mixed, d_attn, grad_router, grad_gain, normed, parts)


def widen_kernel(sums_ref, in_ref, out_ref):
    in_ref[...] = sums_ref[0, 0].astype(f32).T
    out_ref[...] = sums_ref[0, 1].astype(f32)


def widen(sums):
    block, width = sums.shape[2:]
    step = ROWS if block % ROWS == 0 else LANES
    return pl.pallas_call(
        widen_kernel,
        grid=(block // step,),
        in_specs=[pl.BlockSpec((1, 2, step, width), lambda i: (0, 0, i, 0))],
        out_specs=[pl.BlockSpec((width, step), lambda i: (0, i)), pl.BlockSpec((step, width), lambda i: (i, 0))],
        out_shape=[jax.ShapeDtypeStruct((width, block), f32), jax.ShapeDtypeStruct((block, width), f32)],
        cost_estimate=cost(2),
        name="widen",
    )(sums)


def place_kernel(me_ref, *refs):
    out_ref = refs[-1]
    for r, piece in enumerate(refs[:-1]):
        out_ref[pl.ds(lax.bitwise_xor(me_ref[0], r), 1)] = piece[...][None]


def place_pieces(me, pieces):
    return pl.pallas_call(
        place_kernel,
        in_specs=[pl.BlockSpec(memory_space=pltpu.SMEM)] + [pl.BlockSpec(memory_space=pltpu.VMEM)] * len(pieces),
        out_shape=jax.ShapeDtypeStruct((len(pieces), *pieces[0].shape), pieces[0].dtype),
        compiler_params=pltpu.CompilerParams(vmem_limit_bytes=16 * 2**20),
        cost_estimate=cost(2),
        name="place_pieces",
    )(me.reshape(1), *pieces)


HIGHEST = lax.Precision.HIGHEST
SEGMENT_LIMIT = 512
REACH = (SEGMENT_LIMIT + ROWS - LANES) // LANES


def norm_factor(values):
    return lax.rsqrt(jnp.mean(values * values, axis=-1, keepdims=True) + EPSILON)


def distances(axis):
    return [1 << i for i in reversed(range(lax.axis_size(axis).bit_length() - 1))]


def exchange(rows, axis, distance):
    return lax.ppermute(rows, axis, [(i, i ^ distance) for i in range(lax.axis_size(axis))])


def is_high(axis, distance):
    return (lax.axis_index(axis) & distance) != 0


def swap_blocks(blocks):
    return lax.all_to_all(blocks, "expert", split_axis=0, concat_axis=0, tiled=True)


def after(value, *earlier):
    return lax.optimization_barrier((value, *earlier))[0]


def start_gather(near):
    return [near] + [exchange(near, "dp", distance) for distance in distances("dp")]


def finish_gather(terms):
    near = terms[0]
    pieces = dict(zip([0] + distances("dp"), terms))
    for r in range(lax.axis_size("dp")):
        if r not in pieces:
            lowest = r & -r
            pieces[r] = exchange(pieces[r ^ lowest], "dp", lowest)
    block = place_pieces(lax.axis_index("dp"), [pieces[r] for r in range(len(pieces))])
    return block.reshape(-1, near.shape[-1])


def scatter_dp(rows):
    width = rows.shape[1]
    block = rows.reshape(lax.axis_size("dp"), -1, width)
    order = distances("dp")[::-1]
    for distance in order:
        halves = block.reshape(block.shape[0] // 2, 2, -1, width)
        high = is_high("dp", distance).astype(jnp.int32)
        keep = lax.dynamic_index_in_dim(halves, high, 1, keepdims=False)
        send = lax.dynamic_index_in_dim(halves, 1 - high, 1, keepdims=False)
        received = exchange(send.astype(bf16), "dp", distance)
        if distance != order[-1]:
            block = keep.astype(f32) + received.astype(f32)
    return keep, received


def finish_dp(terms):
    keep, received = terms
    return (keep.astype(f32) + received.astype(f32))[0].astype(bf16)


def join(parts):
    return parts[0] if len(parts) == 1 else jnp.concatenate(parts, axis=0)


def near_parts(rows):
    return swap_blocks(rows.reshape(lax.axis_size("expert"), -1, rows.shape[1]))


def gelu_and_slope(values):
    root = 0.7978845608028654
    square = values * values
    share = 0.5 + 0.5 * jnp.tanh(values * (root + root * 0.044715 * square))
    unit = values * share
    slope = share + 2.0 * unit * (1.0 - share) * (root + 3.0 * root * 0.044715 * square)
    return unit, slope


def body(
    inputs,
    cotangent,
    attn_gain,
    qkv_weight,
    out_weight,
    ffn_gain,
    router_weight,
    rel_bias,
    expert_in,
    expert_out,
    routes,
    positions,
    dropped,
    segment_ids,
    valid_mask,
    buckets,
):
    seq_count, seq_length, model_width = inputs.shape
    tokens = seq_count * seq_length
    bucket_count, head_count = rel_bias.shape
    head_dim = model_width // head_count
    experts = router_weight.shape[1]
    capacity = 5 * tokens // (4 * experts)
    slots = experts * capacity
    me = lax.axis_index("expert")

    width = STEP_HEADS * head_dim
    steps = head_count // STEP_HEADS
    groups = [(0, steps - 1), (steps - 1, 1)]
    small_at = 3 * (steps - 1) * width // LANES
    out_at = 3 * width // model_width

    bucket_windows = offset_windows(buckets, REACH)
    one_hot_windows = (bucket_windows[..., None] == jnp.arange(bucket_count, dtype=jnp.int32)).astype(f32)
    windows = jnp.einsum("gpb,bh->hgp", one_hot_windows, rel_bias, precision=HIGHEST)
    tiles = toeplitz_tiles(windows)
    all_masks = [mask_columns(segment_ids[seq], valid_mask[seq]) for seq in range(seq_count)]
    slot_index = jnp.where(
        dropped.reshape(tokens) == 1, slots, routes.reshape(tokens) * capacity + positions.reshape(tokens)
    )
    slot_row, live = slot_index.reshape(1, tokens), valid_mask.reshape(1, tokens)
    rows_in = inputs.reshape(tokens, model_width)
    top = cotangent.reshape(tokens, model_width)

    def send_slots(rows):
        return swap_blocks(rows.reshape(experts, capacity, model_width)).reshape(slots, model_width)

    near, rest = spread_shard(
        qkv_weight, out_weight, attn_gain, ffn_gain, router_weight, width, steps - 1, lax.axis_size("expert")
    )
    near = swap_blocks(near)
    bounds = [tile_bounds(segment_ids[seq]) for seq in range(seq_count)]
    near, rest, tiles = lax.optimization_barrier((near, rest, tiles))
    rest = swap_blocks(rest)
    filled_cotangent = fill_slots(slot_row, top, slots)
    terms = start_gather(near)
    terms, filled_cotangent, rest, all_masks, bounds = lax.optimization_barrier(
        (terms, filled_cotangent, rest, all_masks, bounds)
    )
    weights = [finish_gather(terms)]

    packs, lses, normeds = [], [], None
    mixes = [None] * seq_count
    for g, (first, many) in enumerate(groups):
        if g == 0:
            terms = start_gather(rest)
            weights[0], filled_cotangent = lax.optimization_barrier((weights[0], filled_cotangent))
            d_final_rows = send_slots(filled_cotangent)
        done = [
            attend_forward(
                normeds[seq] if g else rows_in[seq * seq_length : (seq + 1) * seq_length],
                weights[0],
                small_at,
                weights[g],
                *all_masks[seq],
                bounds[seq],
                tiles,
                mixes[seq],
                first,
                many,
                head_dim,
            )
            for seq in range(seq_count)
        ]
        packs.append([results[0] for results in done])
        mixes = [results[1] for results in done]
        lses.append([results[2] for results in done])
        if g == 0:
            normeds = [results[3] for results in done]
            terms, mixes, lses, packs, normeds = lax.optimization_barrier((terms, mixes, lses, packs, normeds))
            weights.append(finish_gather(terms))
    mixed = join(mixes)
    mixed, d_final_rows = lax.optimization_barrier((mixed, d_final_rows))
    mid_rows, filled = run_middle(mixed, weights[1], out_at, rows_in, weights[0], small_at, slot_row, slots)
    slot_rows = send_slots(filled)

    w_in, w_back = expert_in[0], expert_out[0]
    d_hidden = dot(after(d_final_rows, filled), w_back, NT).astype(bf16)
    held_packs = lax.optimization_barrier((packs, filled))[0]
    probs = [
        [
            attend_probs(
                held_packs[g][seq], lses[g][seq], *all_masks[seq], bounds[seq], tiles, first, head_dim
            )
            for seq in range(seq_count)
        ]
        for g, (first, many) in enumerate(groups)
    ]
    slot_rows, d_hidden, probs = lax.optimization_barrier((slot_rows, d_hidden, probs))
    d_rows, d_logits, gate = run_expert(me, slot_rows, w_in, weights[0], small_at, d_hidden, experts)
    d_returned = send_slots(d_rows)

    expert_parts, moe_rows, grad_router = expert_grads(
        gate, slot_rows, w_in, d_hidden, d_final_rows, w_back, d_logits, lax.axis_size("dp")
    )
    d_returned, moe_rows, expert_parts, grad_router = lax.optimization_barrier(
        (d_returned, moe_rows, expert_parts, grad_router)
    )
    expert_sums = lax.psum_scatter(expert_parts, "dp", scatter_dimension=0, tiled=True)
    d_mid, d_mixed, grad_gain_two = run_middle_back(
        d_returned, slot_row, mid_rows, weights[0], small_at, top, weights[1], out_at
    )
    moe_returned = send_slots(moe_rows)

    diagonals, all_parts = [], []
    terms = None
    for g, (first, many) in enumerate(groups):
        parts, diagonal = [], None
        for seq in range(seq_count):
            at = slice(seq * seq_length, (seq + 1) * seq_length)
            part, here = attend_backward(
                packs[g][seq], d_mixed[at], mixed[at], probs[g][seq], bounds[seq], 2 * REACH + 1, first, head_dim
            )
            parts.append(part)
            diagonal = here if diagonal is None else diagonal + here
        parts = join(parts)
        if g == 0:
            grads = run_dense_grads(mixed, d_mid, grad_router, grad_gain_two, join(normeds), parts)
            grads, parts, diagonal, moe_returned = lax.optimization_barrier((grads, parts, diagonal, moe_returned))
            terms = scatter_dp(grads)
        else:
            parts, diagonal, terms = lax.optimization_barrier((parts, diagonal, terms))
            half, parts = lax.optimization_barrier((finish_dp(terms), parts))
            waits = [near_parts(half)]
            terms = scatter_dp(dot(join(normeds), parts, TN).astype(bf16))
        diagonals.append(diagonal)
        all_parts.append(parts)
    held, moe_returned = lax.optimization_barrier((terms[0], moe_returned))
    terms = (held, terms[1])
    output, sums = run_output(moe_returned, slot_row, mid_rows, rows_in, live)
    all_parts, output, sums = lax.optimization_barrier((all_parts, output, sums))
    input_grad = run_first_back(rows_in, small_at, d_mid, all_parts, weights)
    input_grad, terms, waits = lax.optimization_barrier((input_grad, terms, waits))
    near_terms = list(waits)
    grad_expert_in, grad_expert_out = widen(expert_sums)
    grad_rel = jnp.einsum("hgp,gpb->bh", jnp.concatenate(diagonals, axis=0), one_hot_windows, precision=HIGHEST)

    tail = jnp.concatenate([grad_rel.reshape(-1), sums[0, :4]])
    tail_size = tail.shape[0]
    tail = jnp.pad(tail, (0, -tail_size % model_width)).reshape(-1, model_width)
    for distance in distances("dp")[::-1]:
        tail = tail + exchange(tail, "dp", distance)
    pieces = []
    for unused in range(3):
        pieces.append(tail.astype(bf16))
        tail = tail - pieces[-1].astype(f32)
    receivers = lax.axis_size("expert")
    half = finish_dp(terms).reshape(receivers, -1, 3 * width)
    own_rows = half.shape[1]
    half = jnp.concatenate([half] + [jnp.broadcast_to(piece[None], (receivers, *piece.shape)) for piece in pieces], axis=1)
    last_near, grad_expert_in, grad_expert_out = lax.optimization_barrier(
        (swap_blocks(half), grad_expert_in, grad_expert_out)
    )
    near_terms.append(last_near[:, :own_rows])
    tail = jnp.sum(last_near[:, own_rows:].astype(f32), axis=0).reshape(3, -1)
    tail = (tail[0] + tail[1]) + tail[2]
    grad_rel = tail[: bucket_count * head_count].reshape(bucket_count, head_count)
    totals = tail[bucket_count * head_count : tail_size]
    stats = jnp.sqrt(totals[:3] / (totals[3] * model_width))

    dense_out, last_qkv = [jnp.sum(block.astype(f32), axis=0) for block in near_terms]
    dense_qkv = [dense_out[:, model_width + LANES :], last_qkv]
    grad_parts = [total.reshape(-1, many, 3, width) for total, (first, many) in zip(dense_qkv, groups)]
    grad_qkv = jnp.concatenate(grad_parts, axis=1).transpose(0, 2, 1, 3).reshape(-1, 3 * model_width)
    grad_gain_one = jnp.sum(grad_qkv * qkv_weight.astype(f32), axis=1) / attn_gain.astype(f32)
    return (
        output.reshape(inputs.shape),
        input_grad.reshape(inputs.shape),
        grad_gain_one,
        grad_qkv,
        dense_out[:, :model_width],
        dense_out[:, model_width + 1],
        dense_out[:, model_width + SMALL_GAINS : model_width + SMALL_GAINS + experts],
        grad_rel,
        grad_expert_in[None],
        grad_expert_out[None],
        stats,
    )


def solution(mesh):
    in_specs = (
        P(("dp", "expert"), None, None),
        P(("dp", "expert"), None, None),
        P(("dp", "expert")),
        P(("dp", "expert"), None),
        P(("dp", "expert"), None),
        P(("dp", "expert")),
        P(("dp", "expert"), None),
        P(),
        P("expert", None, None),
        P("expert", None, None),
        P(("dp", "expert"), None),
        P(("dp", "expert"), None),
        P(("dp", "expert"), None),
        P(("dp", "expert"), None),
        P(("dp", "expert"), None),
        P(),
    )
    out_specs = (
        P(("dp", "expert"), None, None),
        P(("dp", "expert"), None, None),
        P(("dp", "expert")),
        P(("dp", "expert"), None),
        P(("dp", "expert"), None),
        P(("dp", "expert")),
        P(("dp", "expert"), None),
        P(),
        P("expert", None, "dp"),
        P("expert", "dp", None),
        P(),
    )
    return jax.shard_map(body, mesh=mesh, in_specs=in_specs, out_specs=out_specs, check_vma=False)
```

```python
import functools

import jax
import jax.numpy as jnp
from jax import lax
from jax.experimental import pallas as pl
from jax.experimental.pallas import tpu as pltpu
from jax.sharding import PartitionSpec as P

EPSILON = 1e-06
MASK_STEP = 1e30
ROWS = 256
LANES = 128
STEP_HEADS = 4
VMEM_BYTES = 60 * 2**20
SMALL_GAINS = 2
bf16, f32 = jnp.bfloat16, jnp.float32
NT = (((1,), (1,)), ((), ()))
NN = (((1,), (0,)), ((), ()))
TN = (((0,), (0,)), ((), ()))


def cost(microseconds):
    return pl.CostEstimate(flops=int(microseconds * 1.1e9), bytes_accessed=0, transcendentals=0)


def dot(left, right, dims):
    return lax.dot_general(left, right, dims, preferred_element_type=f32)


def offset_windows(values, reach):
    chunks = (values.shape[0] + 1) // LANES
    turned = jnp.pad(values[::-1], (1, 0)).reshape(chunks, LANES)
    middle = chunks // 2
    return jnp.stack(
        [jnp.concatenate([turned[middle - g], turned[middle - g - 1]]) for g in range(-reach, reach + 1)]
    )


def toeplitz_kernel(reach, window_ref, tile_ref):
    for g in range(2 * reach + 1):
        row = window_ref[0, g : g + 1, :]
        full = jnp.broadcast_to(row, (LANES, 2 * LANES))
        turned = pltpu.roll(full, 0, 1, stride=1, stride_axis=0)
        tile_ref[0, g * LANES : (g + 1) * LANES, :] = turned[:, :LANES]


def toeplitz_tiles(windows):
    heads, groups, width = windows.shape
    return pl.pallas_call(
        functools.partial(toeplitz_kernel, groups // 2),
        grid=(heads,),
        in_specs=[pl.BlockSpec((1, groups, width), lambda n: (n, 0, 0))],
        out_specs=pl.BlockSpec((1, groups * LANES, LANES), lambda n: (n, 0, 0)),
        out_shape=jax.ShapeDtypeStruct((heads, groups * LANES, LANES), f32),
        compiler_params=pltpu.CompilerParams(vmem_limit_bytes=VMEM_BYTES),
        cost_estimate=cost(9),
        name="toeplitz_tiles",
    )(windows)


def head_lanes(rows, head, head_dim):
    lane = lax.broadcasted_iota(jnp.int32, rows.shape, 1)
    return jnp.where((lane >= head * head_dim) & (lane < (head + 1) * head_dim), rows, jnp.zeros_like(rows))


def head_rows(columns, head, head_dim):
    row = lax.broadcasted_iota(jnp.int32, columns.shape, 0)
    return jnp.where((row >= head * head_dim) & (row < (head + 1) * head_dim), columns, jnp.zeros_like(columns))


def bias_tile(bias_ref, head, offset):
    parts = [
        bias_ref[head, pl.ds(pl.multiple_of(offset - LANES * part, LANES), ROWS), :]
        for part in range(ROWS // LANES)
    ]
    return jnp.concatenate(parts, axis=1)


def forward_kernel(head_dim, reach, normalize, low_ref, high_ref, in_ref, small_ref, weight_ref, qx_ref, kx_ref, bias_ref, *refs):
    packed_ref, mix_ref, lse_ref, normed_ref, vt_ref = refs[-5:] if normalize else (*refs[-4:-1], in_ref, refs[-1])
    length, width = mix_ref.shape
    heads = width // head_dim
    scale = head_dim ** (-0.5)
    chunks = [slice(at, at + ROWS) for at in range(0, length, ROWS)]

    if normalize:

        @pl.when(pl.program_id(0) == 0)
        def _():
            gain = gain_row(small_ref, 0)
            for here in chunks:
                rows = in_ref[here].astype(f32)
                normed_ref[here] = (rows * row_factor(rows) * gain).astype(bf16)

    for here in chunks:
        packed_ref[here] = dot(normed_ref[here], weight_ref[...], NN).astype(bf16)
    q_ref, k_ref, v_ref = [packed_ref.at[:, part * width : (part + 1) * width] for part in range(3)]
    for c in range(width // LANES):
        vt_ref[c * LANES : (c + 1) * LANES, :] = v_ref[:, c * LANES : (c + 1) * LANES].T
    per = LANES // head_dim

    def one_block(qb, unused):
        first = pl.multiple_of(qb * ROWS, ROWS)
        qx = qx_ref[:, pl.ds(first, ROWS)]
        queries = []
        for c in range(width // LANES):
            pair = (q_ref[pl.ds(first, ROWS), c * LANES : (c + 1) * LANES] * jnp.asarray(scale, bf16)).T
            queries += [jnp.concatenate([head_rows(pair, h, head_dim), qx], axis=0) for h in range(per)]

        def one_tile(kb, carry):
            keys_at = pl.multiple_of(kb * ROWS, ROWS)
            offset = pl.multiple_of(keys_at - first + LANES * reach, LANES)
            kx = kx_ref[pl.ds(keys_at, ROWS), :]
            out = []
            all_scores = []
            for h in range(heads):
                c = h // per
                keys = jnp.concatenate([k_ref[pl.ds(keys_at, ROWS), c * LANES : (c + 1) * LANES], kx], axis=1)
                all_scores.append(dot(keys, queries[h], NN))
            soft = []
            for h in range(heads):
                peak, total, mixed = carry[h]
                scores = all_scores[h] + bias_tile(bias_ref, h, offset)
                new_peak = jnp.maximum(peak, jnp.max(scores, axis=0, keepdims=True))
                weights = jnp.exp(scores - new_peak)
                shrink = jnp.exp(peak - new_peak)
                total = total * shrink + jnp.sum(weights, axis=0, keepdims=True)
                soft.append((new_peak, total, shrink, weights.astype(bf16)))
            for h in range(heads):
                new_peak, total, shrink, weights = soft[h]
                values = vt_ref[h * head_dim : (h + 1) * head_dim, pl.ds(keys_at, ROWS)]
                mixed = carry[h][2] * shrink + dot(values, weights, NN)
                out.append((new_peak, total, mixed))
            return tuple(out)

        start = tuple(
            (jnp.full((1, ROWS), -3e38, f32), jnp.zeros((1, ROWS), f32), jnp.zeros((head_dim, ROWS), f32))
            for h in range(heads)
        )
        done = lax.fori_loop(low_ref[qb], high_ref[qb], one_tile, start)
        for c in range(width // LANES):
            rows = jnp.concatenate([done[h][2] / done[h][1] for h in range(c * per, (c + 1) * per)], axis=0)
            mix_ref[pl.ds(first, ROWS), c * LANES : (c + 1) * LANES] = rows.T.astype(bf16)
        for h in range(heads):
            lse_ref[0, h : h + 1, pl.ds(first, ROWS)] = done[h][0] + jnp.log(done[h][1])
        return unused

    lax.fori_loop(0, length // ROWS, one_block, 0)


def probs_kernel(head_dim, reach, low_ref, high_ref, q_ref, k_ref, qx_ref, kx_ref, bias_ref, lse_ref, probs_ref):
    length, width = q_ref.shape
    heads = width // head_dim
    scale = head_dim ** (-0.5)
    per = LANES // head_dim

    def one_block(qb, unused):
        first = pl.multiple_of(qb * ROWS, ROWS)
        qx = qx_ref[:, pl.ds(first, ROWS)]
        queries = []
        for c in range(width // LANES):
            pair = (q_ref[pl.ds(first, ROWS), c * LANES : (c + 1) * LANES] * jnp.asarray(scale, bf16)).T
            queries += [jnp.concatenate([head_rows(pair, h, head_dim), qx], axis=0) for h in range(per)]
        lses = [lse_ref[0, h : h + 1, pl.ds(first, ROWS)] for h in range(heads)]

        def one_tile(kb, unused):
            keys_at = pl.multiple_of(kb * ROWS, ROWS)
            offset = pl.multiple_of(keys_at - first + LANES * reach, LANES)
            kx = kx_ref[pl.ds(keys_at, ROWS), :]
            all_scores = []
            for h in range(heads):
                c = h // per
                keys = jnp.concatenate([k_ref[pl.ds(keys_at, ROWS), c * LANES : (c + 1) * LANES], kx], axis=1)
                all_scores.append(dot(keys, queries[h], NN))
            for h in range(heads):
                weights = jnp.exp(all_scores[h] + bias_tile(bias_ref, h, offset) - lses[h])
                probs_ref[h, qb, pl.ds(keys_at, ROWS), :] = weights.astype(bf16)
            return unused

        return lax.fori_loop(low_ref[qb], high_ref[qb], one_tile, unused)

    lax.fori_loop(0, length // ROWS, one_block, 0)


def diagonal_sums(tiles):
    groups = tiles.shape[0]
    step = LANES // 2
    zero = jnp.zeros((groups, step, LANES), f32)
    turned = jnp.concatenate([tiles[:, :step], zero], axis=2) + pltpu.roll(
        jnp.concatenate([tiles[:, step:], zero], axis=2), 2 * LANES - step, 2
    )
    while step > 8:
        step //= 2
        turned = turned[:, :step] + pltpu.roll(turned[:, step:], 2 * LANES - step, 2)
    while step > 1:
        step //= 2
        turned = turned + pltpu.roll(pltpu.roll(turned, 2 * LANES - step, 2), 8 - step, 1)
    return turned[:, 0]


def backward_kernel(head_dim, reach, low_ref, high_ref, q_ref, k_ref, v_ref, dmix_ref, mix_ref, probs_ref,
                    grad_ref, diag_ref, kt_ref, dk_ref, dv_ref, along_ref):
    length, width = q_ref.shape
    heads = width // head_dim
    scale = head_dim ** (-0.5)
    per = LANES // head_dim
    for c in range(width // LANES):
        kt_ref[c * LANES : (c + 1) * LANES, :] = k_ref[:, c * LANES : (c + 1) * LANES].T
    dk_ref[...] = jnp.zeros_like(dk_ref)
    dv_ref[...] = jnp.zeros_like(dv_ref)
    along_ref[...] = jnp.zeros_like(along_ref)

    def one_block(qb, unused):
        first = pl.multiple_of(qb * ROWS, ROWS)
        queries, d_mixes, deltas, d_turned = [], [], [], []
        for c in range(width // LANES):
            lanes = slice(c * LANES, (c + 1) * LANES)
            query = q_ref[pl.ds(first, ROWS), lanes] * jnp.asarray(scale, bf16)
            d_mix = dmix_ref[pl.ds(first, ROWS), lanes]
            product = (d_mix.astype(f32) * mix_ref[pl.ds(first, ROWS), lanes].astype(f32)).T
            d_mix_turned = d_mix.T
            for h in range(per):
                queries.append(head_lanes(query, h, head_dim))
                d_mixes.append(head_lanes(d_mix, h, head_dim))
                d_turned.append(head_rows(d_mix_turned, h, head_dim))
                deltas.append(jnp.sum(product[h * head_dim : (h + 1) * head_dim], axis=0, keepdims=True))

        def one_tile(kb, carry):
            keys_at = pl.multiple_of(kb * ROWS, ROWS)
            offset = pl.multiple_of(keys_at - first + LANES * reach, LANES)
            out = []
            low_weights, low_scores, all_weights = [], [], []
            for h in range(heads):
                lanes = slice(h // per * LANES, (h // per + 1) * LANES)
                all_weights.append(dot(v_ref[pl.ds(keys_at, ROWS), lanes], d_turned[h], NN))
            for h in range(heads):
                weights = probs_ref[h, qb, pl.ds(keys_at, ROWS), :]
                d_scores = weights.astype(f32) * (all_weights[h] - deltas[h])
                for part in range(ROWS // LANES):
                    at = pl.ds(pl.multiple_of(offset - LANES * part, LANES), ROWS)
                    along_ref[h, at, :] += d_scores[:, part * LANES : (part + 1) * LANES]
                low_weights.append(weights)
                low_scores.append(d_scores.astype(bf16))
            for h in range(heads):
                keys_turned = kt_ref[h * head_dim : (h + 1) * head_dim, pl.ds(keys_at, ROWS)]
                out.append(carry[h] + dot(keys_turned, low_scores[h], NN))
            for c in range(width // LANES):
                mine = range(c * per, (c + 1) * per)
                lanes = slice(c * LANES, (c + 1) * LANES)
                dv_ref[pl.ds(keys_at, ROWS), lanes] += dot(
                    jnp.concatenate([low_weights[h] for h in mine], axis=1), jnp.concatenate([d_mixes[h] for h in mine], axis=0), NN)
                dk_ref[pl.ds(keys_at, ROWS), lanes] += dot(
                    jnp.concatenate([low_scores[h] for h in mine], axis=1), jnp.concatenate([queries[h] for h in mine], axis=0), NN)
            return tuple(out)

        start = tuple(jnp.zeros((head_dim, ROWS), f32) for h in range(heads))
        done = lax.fori_loop(low_ref[qb], high_ref[qb], one_tile, start)
        for c in range(width // LANES):
            rows = jnp.concatenate([done[h] for h in range(c * per, (c + 1) * per)], axis=0) * scale
            grad_ref[pl.ds(first, ROWS), c * LANES : (c + 1) * LANES] = rows.T.astype(bf16)
        return unused

    lax.fori_loop(0, length // ROWS, one_block, 0)
    grad_ref[:, width : 2 * width] = dk_ref[...].astype(bf16)
    grad_ref[:, 2 * width :] = dv_ref[...].astype(bf16)
    for h in range(heads):
        diag_ref[h] = diagonal_sums(along_ref[h].reshape(2 * reach + 1, LANES, LANES))


def tile_bounds(segments):
    length = segments.shape[0]
    blocks = segments.reshape(length // ROWS, ROWS)
    starts = jnp.sum((segments[None, :] < blocks[:, :1]).astype(jnp.int32), axis=1)
    ends = jnp.sum((segments[None, :] <= blocks[:, -1:]).astype(jnp.int32), axis=1)
    return starts // ROWS, (ends + ROWS - 1) // ROWS


def mask_columns(segments, validity, segment_count=8):
    length = segments.shape[0]
    short = 1
    while short * (short + 1) < length:
        short += 1
    at = jnp.arange(length, dtype=jnp.int32)
    lane = jnp.arange(LANES, dtype=jnp.int32)[None, :]
    in_first = (lane >= segment_count) & (lane < segment_count + short)
    in_second = (lane >= segment_count + short) & (lane < segment_count + 2 * short + 1)
    mine = (
        (lane == segments[:, None])
        | (in_first & (lane - segment_count == (at % short)[:, None]))
        | (in_second & (lane - segment_count - short == (at % (short + 1))[:, None]))
    )
    used = lane < segment_count + 2 * short + 1
    query_side = jnp.where(used & ~mine, -MASK_STEP, 0.0).astype(bf16).T
    real = (validity == 1)[:, None]
    key_side = jnp.where(mine & jnp.where(real, lane < segment_count, lane >= segment_count), 1.0, 0.0).astype(bf16)
    return query_side, key_side


def attend_forward(rows_in, smalls, small_at, weights, query_side, key_side, bounds, tiles, mixed, first, steps, head_dim):
    length, model_width = rows_in.shape
    width = STEP_HEADS * head_dim
    reach = tiles.shape[1] // LANES // 2
    shared = [] if mixed is None else [mixed]
    whole = lambda *_: (0, 0)
    grid_spec = pltpu.PrefetchScalarGridSpec(
        num_scalar_prefetch=2,
        grid=(steps,),
        in_specs=[
            pl.BlockSpec((length, model_width), whole),
            pl.BlockSpec((model_width, LANES), lambda p, *_: (0, small_at)),
            pl.BlockSpec((model_width, 3 * width), lambda p, *_: (0, p)),
            pl.BlockSpec((LANES, length), whole),
            pl.BlockSpec((length, LANES), whole),
            pl.BlockSpec((STEP_HEADS, tiles.shape[1], LANES), lambda p, *_: (first + p, 0, 0)),
        ]
        + [pl.BlockSpec(memory_space=pl.ANY)] * len(shared),
        out_specs=[
            pl.BlockSpec((length, 3 * width), lambda p, *_: (0, p)),
            pl.BlockSpec((length, width), lambda p, *_: (0, first + p)),
            pl.BlockSpec((1, STEP_HEADS, length), lambda p, *_: (p, 0, 0)),
        ]
        + [pl.BlockSpec((length, model_width), whole)] * (not shared),
        scratch_shapes=[pltpu.VMEM((width, length), bf16)],
    )
    return pl.pallas_call(
        functools.partial(forward_kernel, head_dim, reach, not shared),
        grid_spec=grid_spec,
        out_shape=[
            jax.ShapeDtypeStruct((length, 3 * width * steps), bf16),
            jax.ShapeDtypeStruct((length, tiles.shape[0] * head_dim), bf16),
            jax.ShapeDtypeStruct((steps, STEP_HEADS, length), f32),
        ]
        + [jax.ShapeDtypeStruct((length, model_width), bf16)] * (not shared),
        input_output_aliases={8: 1} if shared else {},
        compiler_params=pltpu.CompilerParams(vmem_limit_bytes=36 * 2**20),
        cost_estimate=cost(1),
        name="attend_forward",
    )(*bounds, rows_in, smalls, weights, query_side, key_side, tiles, *shared)


def attend_probs(packed, lse, query_side, key_side, bounds, tiles, first, head_dim):
    length = packed.shape[0]
    width = STEP_HEADS * head_dim
    steps = packed.shape[1] // 3 // width
    reach = tiles.shape[1] // LANES // 2
    whole = lambda *_: (0, 0)
    blocks = length // ROWS
    grid_spec = pltpu.PrefetchScalarGridSpec(
        num_scalar_prefetch=2,
        grid=(steps,),
        in_specs=[
            pl.BlockSpec((length, width), lambda p, *_: (0, 3 * p)),
            pl.BlockSpec((length, width), lambda p, *_: (0, 3 * p + 1)),
            pl.BlockSpec((LANES, length), whole),
            pl.BlockSpec((length, LANES), whole),
            pl.BlockSpec((STEP_HEADS, tiles.shape[1], LANES), lambda p, *_: (first + p, 0, 0)),
            pl.BlockSpec((1, STEP_HEADS, length), lambda p, *_: (p, 0, 0)),
        ],
        out_specs=pl.BlockSpec((STEP_HEADS, blocks, length, ROWS), lambda p, *_: (p, 0, 0, 0)),
    )
    return pl.pallas_call(
        functools.partial(probs_kernel, head_dim, reach),
        grid_spec=grid_spec,
        out_shape=jax.ShapeDtypeStruct((steps * STEP_HEADS, blocks, length, ROWS), bf16),
        compiler_params=pltpu.CompilerParams(vmem_limit_bytes=56 * 2**20),
        cost_estimate=cost(9 * steps),
        name="attend_probs",
    )(*bounds, packed, packed, query_side, key_side, tiles, lse)


def attend_backward(packed, d_mix, mix, probs, bounds, groups, first, head_dim):
    length = packed.shape[0]
    width = STEP_HEADS * head_dim
    steps = packed.shape[1] // 3 // width
    whole = lambda *_: (0, 0)
    grid_spec = pltpu.PrefetchScalarGridSpec(
        num_scalar_prefetch=2,
        grid=(steps,),
        in_specs=[
            pl.BlockSpec((length, width), lambda p, *_: (0, 3 * p)),
            pl.BlockSpec((length, width), lambda p, *_: (0, 3 * p + 1)),
            pl.BlockSpec((length, width), lambda p, *_: (0, 3 * p + 2)),
            pl.BlockSpec((length, width), lambda p, *_: (0, first + p)),
            pl.BlockSpec((length, width), lambda p, *_: (0, first + p)),
            pl.BlockSpec((STEP_HEADS, *probs.shape[1:]), lambda p, *_: (p, 0, 0, 0)),
        ],
        out_specs=[
            pl.BlockSpec((length, 3 * width), lambda p, *_: (0, p)),
            pl.BlockSpec((STEP_HEADS, groups, 2 * LANES), lambda p, *_: (p, 0, 0)),
        ],
        scratch_shapes=[
            pltpu.VMEM((width, length), bf16),
            pltpu.VMEM((length, width), f32),
            pltpu.VMEM((length, width), f32),
            pltpu.VMEM((STEP_HEADS, groups * LANES, LANES), f32),
        ],
    )
    return pl.pallas_call(
        functools.partial(backward_kernel, head_dim, groups // 2),
        grid_spec=grid_spec,
        out_shape=[
            jax.ShapeDtypeStruct((length, 3 * width * steps), bf16),
            jax.ShapeDtypeStruct((steps * STEP_HEADS, groups, 2 * LANES), f32),
        ],
        compiler_params=pltpu.CompilerParams(vmem_limit_bytes=56 * 2**20),
        cost_estimate=cost(15 * steps),
        name="attend_backward",
    )(*bounds, packed, packed, packed, d_mix, mix, probs)


def spread_kernel(width, near_steps, weight_ref, out_weight_ref, first_ref, second_ref, router_ref, *outs):
    receivers, count = outs[0].shape[:2]
    steps = weight_ref.shape[1] // (3 * width)
    row = lax.broadcasted_iota(jnp.int32, (count, count), 0)
    same = row == lax.broadcasted_iota(jnp.int32, (count, count), 1)
    columns = [
        jnp.sum(jnp.where(same, jnp.broadcast_to(ref[...].astype(f32), same.shape), 0.0), axis=1, keepdims=True)
        for ref in (first_ref, second_ref)
    ]
    columns.append(dot(jnp.where(same, 1.0, 0.0).astype(bf16), router_ref[...], NT))
    used = SMALL_GAINS + router_ref.shape[0]
    columns.append(jnp.zeros((count, -used % LANES), f32))
    pieces = [
        weight_ref[:, (part * steps + p) * width : (part * steps + p + 1) * width] for p in range(steps) for part in range(3)
    ]
    groups = [
        pieces[: 3 * near_steps] + [jnp.concatenate(columns, axis=1).astype(bf16)],
        pieces[3 * near_steps :] + [out_weight_ref[...]],
    ]
    for group, out_ref in zip(groups, outs):
        at = 0
        for piece in group:
            out_ref[:, :, at : at + piece.shape[1]] = jnp.broadcast_to(piece[None], (receivers, *piece.shape))
            at += piece.shape[1]


def spread_shard(weight, out_weight, first_gain, second_gain, router, width, near_steps, receivers):
    rows, columns = weight.shape
    small = SMALL_GAINS + router.shape[1]
    small += -small % LANES
    near = 3 * width * near_steps
    return pl.pallas_call(
        functools.partial(spread_kernel, width, near_steps),
        out_shape=[
            jax.ShapeDtypeStruct((receivers, rows, near + small), bf16),
            jax.ShapeDtypeStruct((receivers, rows, columns - near + out_weight.shape[1]), bf16),
        ],
        compiler_params=pltpu.CompilerParams(vmem_limit_bytes=VMEM_BYTES),
        cost_estimate=cost(2),
        name="spread_shard",
    )(weight, out_weight, first_gain.reshape(1, rows), second_gain.reshape(1, rows), router.T)


def expert_kernel(experts, me_ref, rows_ref, in_ref, small_ref, d_hidden_ref, d_rows_ref, d_logits_ref, gate_ref,
                  probs_ref, total_ref, d_gate_ref):
    step = pl.program_id(0)
    lane = lax.broadcasted_iota(jnp.int32, probs_ref.shape, 1)
    chosen = lane == me_ref[0] + SMALL_GAINS

    @pl.when(step == 0)
    def _():
        logits = dot(rows_ref[...], small_ref[...], NN)
        logits = jnp.where((lane >= SMALL_GAINS) & (lane < SMALL_GAINS + experts), logits, -MASK_STEP)
        raised = jnp.exp(logits - jnp.max(logits, axis=1, keepdims=True))
        probs = raised / jnp.sum(raised, axis=1, keepdims=True)
        probs_ref[...] = probs
        gate_ref[...] = jnp.sum(jnp.where(chosen, probs, 0.0), axis=1, keepdims=True)
        total_ref[...] = jnp.zeros_like(total_ref)
        d_gate_ref[...] = jnp.zeros_like(d_gate_ref)

    count = rows_ref.shape[0]
    chunk = 256 if count % 256 == 0 else count
    weights = in_ref[...]
    pres = [dot(rows_ref[at : at + chunk], weights, NN) for at in range(0, count, chunk)]
    lows = []
    for i, at in enumerate(range(0, count, chunk)):
        here = slice(at, at + chunk)
        unit, slope = gelu_and_slope(pres[i].astype(bf16))
        d_hidden = d_hidden_ref[here]
        d_gate_ref[here] += jnp.sum((unit * d_hidden).astype(f32), axis=1, keepdims=True)
        lows.append(d_hidden * slope)
    for i, at in enumerate(range(0, count, chunk)):
        total_ref[at : at + chunk] += dot(lows[i], weights, NT)

    @pl.when(step == pl.num_programs(0) - 1)
    def _():
        d_logits = (probs_ref[...] * (chosen.astype(f32) - gate_ref[...]) * d_gate_ref[...]).astype(bf16)
        d_logits_ref[...] = d_logits
        d_rows_ref[...] = (gate_ref[...] * total_ref[...] + dot(d_logits, small_ref[...], NT)).astype(bf16)


def run_expert(me, rows, w_in, weights, small_at, d_hidden, experts):
    count, width = rows.shape
    hidden_width = w_in.shape[1]
    block = 768 if hidden_width % 768 == 0 else 512
    whole = lambda f, *_: (0, 0)
    grid_spec = pltpu.PrefetchScalarGridSpec(
        num_scalar_prefetch=1,
        grid=(hidden_width // block,),
        in_specs=[
            pl.BlockSpec((count, width), whole),
            pl.BlockSpec((width, block), lambda f, *_: (0, f)),
            pl.BlockSpec((width, LANES), lambda f, *_: (0, small_at)),
            pl.BlockSpec((count, block), lambda f, *_: (0, f)),
        ],
        out_specs=[
            pl.BlockSpec((count, width), whole),
            pl.BlockSpec((count, LANES), whole),
            pl.BlockSpec((count, 1), whole),
        ],
        scratch_shapes=[pltpu.VMEM((count, LANES), f32), pltpu.VMEM((count, width), f32), pltpu.VMEM((count, 1), f32)],
    )
    return pl.pallas_call(
        functools.partial(expert_kernel, experts),
        grid_spec=grid_spec,
        out_shape=[
            jax.ShapeDtypeStruct((count, width), bf16),
            jax.ShapeDtypeStruct((count, LANES), bf16),
            jax.ShapeDtypeStruct((count, 1), f32),
        ],
        compiler_params=pltpu.CompilerParams(vmem_limit_bytes=VMEM_BYTES),
        cost_estimate=cost(18),
        name="run_expert",
    )(me.reshape(1), rows, w_in, weights, d_hidden)


def expert_grads_kernel(gate_ref, rows_ref, in_ref, d_hidden_ref, d_slots_ref, back_ref, d_logits_ref, parts_ref,
                        moe_ref, router_ref, d_out_ref, total_ref):
    step = pl.program_id(0)

    @pl.when(step == 0)
    def _():
        d_out_ref[...] = (gate_ref[...] * d_slots_ref[...].astype(f32)).astype(bf16)
        total_ref[...] = jnp.zeros_like(total_ref)
        router_ref[...] = dot(rows_ref[...], d_logits_ref[...], TN)

    count = rows_ref.shape[0]
    chunk = 256 if count % 256 == 0 else count
    pres = [dot(rows_ref[at : at + chunk], in_ref[...], NN) for at in range(0, count, chunk)]
    units, lows = [], []
    for i, at in enumerate(range(0, count, chunk)):
        here = slice(at, at + chunk)
        unit, slope = gelu_and_slope(pres[i])
        units.append(unit.astype(bf16))
        lows.append((gate_ref[here] * d_hidden_ref[here].astype(f32) * slope).astype(bf16))
    hidden = jnp.concatenate(units, axis=0)
    parts_ref[0, 0] = dot(jnp.concatenate(lows, axis=0), rows_ref[...], TN).astype(bf16)
    parts_ref[0, 1] = dot(hidden, d_out_ref[...], TN).astype(bf16)
    total_ref[...] += dot(hidden, back_ref[...], NN)

    @pl.when(step == pl.num_programs(0) - 1)
    def _():
        moe_ref[...] = (gate_ref[...] * total_ref[...]).astype(bf16)


def expert_grads(gate, rows, w_in, d_hidden, d_slots, w_back, d_logits, owners):
    count, width = rows.shape
    block = w_in.shape[1] // owners
    whole = lambda f: (0, 0)
    full = pl.BlockSpec((count, width), whole)
    return pl.pallas_call(
        expert_grads_kernel,
        grid=(owners,),
        in_specs=[
            pl.BlockSpec((count, 1), whole),
            full,
            pl.BlockSpec((width, block), lambda f: (0, f)),
            pl.BlockSpec((count, block), lambda f: (0, f)),
            full,
            pl.BlockSpec((block, width), lambda f: (f, 0)),
            pl.BlockSpec((count, LANES), whole),
        ],
        out_specs=[
            pl.BlockSpec((1, 2, block, width), lambda f: (f, 0, 0, 0)),
            full,
            pl.BlockSpec((width, LANES), whole),
        ],
        out_shape=[
            jax.ShapeDtypeStruct((owners, 2, block, width), bf16),
            jax.ShapeDtypeStruct((count, width), bf16),
            jax.ShapeDtypeStruct((width, LANES), f32),
        ],
        scratch_shapes=[pltpu.VMEM((count, width), bf16), pltpu.VMEM((count, width), f32)],
        compiler_params=pltpu.CompilerParams(vmem_limit_bytes=VMEM_BYTES),
        cost_estimate=cost(35),
        name="expert_grads",
    )(gate, rows, w_in, d_hidden, d_slots, w_back, d_logits)


def gain_row(small_ref, lane):
    return small_ref[...].astype(f32).T[lane : lane + 1]


def row_factor(rows):
    return lax.rsqrt(jnp.mean(rows * rows, axis=1, keepdims=True) + EPSILON)


def middle_kernel(row_steps, mixed_ref, weight_ref, in_ref, small_ref, slot_ref, rows_ref, slots_ref, normed_ref):
    step = pl.program_id(0)

    @pl.when(step < row_steps)
    def _():
        count = in_ref.shape[0]
        first = pl.multiple_of(step * count, count)
        chunks = [slice(at, at + ROWS) for at in range(0, count, ROWS)]
        gain = gain_row(small_ref, 1)
        projected = [dot(mixed_ref[here], weight_ref[...], NN) for here in chunks]
        for here, attn in zip(chunks, projected):
            rows = in_ref[here].astype(f32) + attn
            rows_ref[here] = rows
            normed_ref[pl.ds(first + here.start, ROWS)] = (rows * row_factor(rows) * gain).astype(bf16)

    @pl.when(step >= row_steps)
    def _():
        fill_kernel(slot_ref, normed_ref, slots_ref, (step - row_steps) * slots_ref.shape[0])


def fill_kernel(slot_ref, rows_ref, slots_ref, first=0):
    slots, count = slots_ref.shape[0], rows_ref.shape[0]
    chunk = ROWS if slots % ROWS == 0 else slots
    for at in range(0, slots, chunk):
        slot = lax.broadcasted_iota(jnp.int32, (chunk, count), 0) + (first + at)
        place = jnp.where(slot == slot_ref[...], 1.0, 0.0).astype(bf16)
        slots_ref[at : at + chunk] = dot(place, rows_ref[...], NN).astype(bf16)


def across(row):
    return jnp.broadcast_to(row.astype(f32), (LANES, row.shape[1])).T


def row_chunks(ref):
    return [slice(at, at + ROWS) for at in range(0, ref.shape[0], ROWS)]


def row_block(count):
    return 2 * ROWS if count % (2 * ROWS) == 0 else ROWS


def read_slots(slot_row, blocks_ref):
    slots = blocks_ref.shape[0]
    mine = jnp.concatenate([across(slot_row)] * pl.cdiv(slots, LANES), axis=1)[:, :slots]
    slot = lax.broadcasted_iota(jnp.int32, mine.shape, 1).astype(f32)
    return dot(jnp.where(slot == mine, 1.0, 0.0).astype(bf16), blocks_ref[...], NN)


def fill_slots(slot_row, rows, slots):
    return pl.pallas_call(
        fill_kernel,
        out_shape=jax.ShapeDtypeStruct((slots, rows.shape[1]), bf16),
        compiler_params=pltpu.CompilerParams(vmem_limit_bytes=VMEM_BYTES),
        cost_estimate=cost(3.5),
        name="fill_slots",
    )(slot_row, rows)


def run_middle(mixed, weights, at, rows_in, smalls, small_at, slot_row, slots):
    count, width = rows_in.shape
    whole = lambda i: (0, 0)
    row_steps = 2 if count % (2 * ROWS) == 0 else 1
    slot_steps = 2 if slots % 32 == 0 else 1
    part = pl.BlockSpec((count // row_steps, width), lambda i: (jnp.minimum(i, row_steps - 1), 0))
    return pl.pallas_call(
        functools.partial(middle_kernel, row_steps),
        grid=(row_steps + slot_steps,),
        in_specs=[
            part,
            pl.BlockSpec((width, width), lambda i: (0, at)),
            part,
            pl.BlockSpec((width, LANES), lambda i: (0, small_at)),
            pl.BlockSpec((1, count), whole),
        ],
        out_specs=[part, pl.BlockSpec((slots // slot_steps, width), lambda i: (jnp.maximum(i - row_steps, 0), 0))],
        out_shape=[jax.ShapeDtypeStruct((count, width), f32), jax.ShapeDtypeStruct((slots, width), bf16)],
        scratch_shapes=[pltpu.VMEM((count, width), bf16)],
        compiler_params=pltpu.CompilerParams(vmem_limit_bytes=VMEM_BYTES),
        cost_estimate=cost(5),
        name="run_middle",
    )(mixed, weights, rows_in, smalls, slot_row)


def middle_back_kernel(blocks_ref, slot_ref, rows_ref, small_ref, top_ref, weight_ref, d_mid_ref, d_mixed_ref, d_gain_ref):
    @pl.when(pl.program_id(0) == 0)
    def _():
        d_gain_ref[...] = jnp.zeros_like(d_gain_ref)

    gain = gain_row(small_ref, 1)
    chunks = row_chunks(rows_ref)
    picked = [read_slots(slot_ref[:, here], blocks_ref) for here in chunks]
    lows = []
    for here, d_normed in zip(chunks, picked):
        rows = rows_ref[here]
        factor = row_factor(rows)
        normed = rows * factor
        weighted = d_normed * gain
        product = d_normed * normed
        d_mid = top_ref[here].astype(f32) + factor * (weighted - normed * jnp.mean(product * gain, axis=1, keepdims=True))
        lows.append(d_mid.astype(bf16))
        d_mid_ref[here] = lows[-1]
        d_gain_ref[...] += jnp.sum(product, axis=0, keepdims=True)
    for here, low in zip(chunks, lows):
        d_mixed_ref[here] = dot(low, weight_ref[...], NT).astype(bf16)


def run_middle_back(blocks, slot_row, rows, smalls, small_at, top, weights, at):
    count, width = rows.shape
    whole = lambda *_: (0, 0)
    part = pl.BlockSpec((row_block(count), width), lambda i: (i, 0))
    return pl.pallas_call(
        middle_back_kernel,
        grid=(count // row_block(count),),
        in_specs=[
            pl.BlockSpec(blocks.shape, whole),
            pl.BlockSpec((1, row_block(count)), lambda i: (0, i)),
            part,
            pl.BlockSpec((width, LANES), lambda i: (0, small_at)),
            part,
            pl.BlockSpec((width, width), lambda i: (0, at)),
        ],
        out_specs=[part, part, pl.BlockSpec((1, width), whole)],
        out_shape=[
            jax.ShapeDtypeStruct((count, width), bf16),
            jax.ShapeDtypeStruct((count, width), bf16),
            jax.ShapeDtypeStruct((1, width), f32),
        ],
        compiler_params=pltpu.CompilerParams(vmem_limit_bytes=VMEM_BYTES),
        cost_estimate=cost(7),
        name="run_middle_back",
    )(blocks, slot_row, rows, smalls, top, weights)


def first_back_kernel(count, small_at, in_ref, d_mid_ref, *refs):
    d_in_ref = refs[2 * count]
    gain = gain_row(refs[count].at[:, small_at * LANES : (small_at + 1) * LANES], 0)
    chunks = row_chunks(in_ref)
    sums = []
    for here in chunks:
        total = 0.0
        for part_ref, weight_ref in zip(refs[:count], refs[count:]):
            total = total + dot(part_ref[here], weight_ref[:, : part_ref.shape[1]], NT)
        sums.append(total)
    for here, total in zip(chunks, sums):
        rows = in_ref[here].astype(f32)
        factor = row_factor(rows)
        normed = rows * factor
        weighted = total * gain
        d_in_ref[here] = d_mid_ref[here].astype(f32) + factor * (
            weighted - normed * jnp.mean(weighted * normed, axis=1, keepdims=True)
        )


def run_first_back(rows_in, small_at, d_mid, parts, weights):
    count, width = rows_in.shape
    whole = lambda *_: (0, 0)
    part = pl.BlockSpec((row_block(count), width), lambda i: (i, 0))
    return pl.pallas_call(
        functools.partial(first_back_kernel, len(parts), small_at),
        grid=(count // row_block(count),),
        in_specs=[part, part]
        + [pl.BlockSpec((row_block(count), columns.shape[1]), lambda i: (i, 0)) for columns in parts]
        + [pl.BlockSpec(weight.shape, whole) for weight in weights],
        out_specs=part,
        out_shape=jax.ShapeDtypeStruct(rows_in.shape, f32),
        compiler_params=pltpu.CompilerParams(vmem_limit_bytes=VMEM_BYTES),
        cost_estimate=cost(8),
        name="run_first_back",
    )(rows_in, d_mid, *parts, *weights)


def output_kernel(blocks_ref, slot_ref, rows_ref, in_ref, live_ref, out_ref, sums_ref):
    chunks = row_chunks(rows_ref)
    picked = [read_slots(slot_ref[:, here], blocks_ref) for here in chunks]
    lane = lax.broadcasted_iota(jnp.int32, (1, LANES), 1)
    total = jnp.zeros((1, LANES), f32)
    for here, moe in zip(chunks, picked):
        rows = rows_ref[here]
        final = rows + moe
        out_ref[here] = final.astype(bf16)
        live = across(live_ref[:, here])[:, :1]
        sums = jnp.where(lane == 3, jnp.sum(live, axis=0, keepdims=True), 0.0)
        for i, part in enumerate((in_ref[here].astype(f32), rows, final)):
            per_row = live * jnp.sum(part * part, axis=1, keepdims=True)
            sums = jnp.where(lane == i, jnp.sum(per_row, axis=0, keepdims=True), sums)
        total += sums

    @pl.when(pl.program_id(0) == 0)
    def _():
        sums_ref[...] = jnp.zeros_like(sums_ref)

    sums_ref[...] += total


def run_output(blocks, slot_row, rows, rows_in, live):
    count, width = rows.shape
    whole = lambda *_: (0, 0)
    part = pl.BlockSpec((row_block(count), width), lambda i: (i, 0))
    column = pl.BlockSpec((1, row_block(count)), lambda i: (0, i))
    return pl.pallas_call(
        output_kernel,
        grid=(count // row_block(count),),
        in_specs=[pl.BlockSpec(blocks.shape, whole), column, part, part, column],
        out_specs=[part, pl.BlockSpec((1, LANES), whole)],
        out_shape=[jax.ShapeDtypeStruct((count, width), bf16), jax.ShapeDtypeStruct((1, LANES), f32)],
        compiler_params=pltpu.CompilerParams(vmem_limit_bytes=VMEM_BYTES),
        cost_estimate=cost(4),
        name="run_output",
    )(blocks, slot_row, rows, rows_in, live)


def dense_grads_kernel(mixed_ref, d_attn_ref, router_ref, gain_ref, normed_ref, parts_ref, grad_ref):
    width = d_attn_ref.shape[1]
    grad_ref[:, :width] = dot(mixed_ref[...], d_attn_ref[...], TN).astype(bf16)
    lane = lax.broadcasted_iota(jnp.int32, router_ref.shape, 1)
    grad_ref[:, width : width + LANES] = jnp.where(lane == 1, across(gain_ref[...]), router_ref[...]).astype(bf16)
    grad_ref[:, width + LANES :] = dot(normed_ref[...], parts_ref[...], TN).astype(bf16)


def run_dense_grads(mixed, d_attn, grad_router, grad_gain, normed, parts):
    count, width = mixed.shape
    columns = parts.shape[1]
    block = ROWS if width % ROWS == 0 else width
    whole = lambda i: (0, 0)
    part = pl.BlockSpec((count, block), lambda i: (0, i))
    return pl.pallas_call(
        dense_grads_kernel,
        grid=(width // block,),
        in_specs=[
            part,
            pl.BlockSpec((count, width), whole),
            pl.BlockSpec((block, LANES), lambda i: (i, 0)),
            pl.BlockSpec((1, block), lambda i: (0, i)),
            part,
            pl.BlockSpec((count, columns), whole),
        ],
        out_specs=pl.BlockSpec((block, width + LANES + columns), lambda i: (i, 0)),
        out_shape=jax.ShapeDtypeStruct((width, width + LANES + columns), bf16),
        compiler_params=pltpu.CompilerParams(vmem_limit_bytes=VMEM_BYTES),
        cost_estimate=cost(7),
        name="run_dense_grads",
    )(mixed, d_attn, grad_router, grad_gain, normed, parts)


def widen_kernel(sums_ref, in_ref, out_ref):
    in_ref[...] = sums_ref[0, 0].astype(f32).T
    out_ref[...] = sums_ref[0, 1].astype(f32)


def widen(sums):
    block, width = sums.shape[2:]
    step = ROWS if block % ROWS == 0 else LANES
    return pl.pallas_call(
        widen_kernel,
        grid=(block // step,),
        in_specs=[pl.BlockSpec((1, 2, step, width), lambda i: (0, 0, i, 0))],
        out_specs=[pl.BlockSpec((width, step), lambda i: (0, i)), pl.BlockSpec((step, width), lambda i: (i, 0))],
        out_shape=[jax.ShapeDtypeStruct((width, block), f32), jax.ShapeDtypeStruct((block, width), f32)],
        cost_estimate=cost(2),
        name="widen",
    )(sums)


def place_kernel(me_ref, *refs):
    out_ref = refs[-1]
    for r, piece in enumerate(refs[:-1]):
        out_ref[pl.ds(lax.bitwise_xor(me_ref[0], r), 1)] = piece[...][None]


def place_pieces(me, pieces):
    return pl.pallas_call(
        place_kernel,
        in_specs=[pl.BlockSpec(memory_space=pltpu.SMEM)] + [pl.BlockSpec(memory_space=pltpu.VMEM)] * len(pieces),
        out_shape=jax.ShapeDtypeStruct((len(pieces), *pieces[0].shape), pieces[0].dtype),
        compiler_params=pltpu.CompilerParams(vmem_limit_bytes=16 * 2**20),
        cost_estimate=cost(2),
        name="place_pieces",
    )(me.reshape(1), *pieces)


HIGHEST = lax.Precision.HIGHEST
SEGMENT_LIMIT = 512
REACH = (SEGMENT_LIMIT + ROWS - LANES) // LANES


def norm_factor(values):
    return lax.rsqrt(jnp.mean(values * values, axis=-1, keepdims=True) + EPSILON)


def distances(axis):
    return [1 << i for i in reversed(range(lax.axis_size(axis).bit_length() - 1))]


def exchange(rows, axis, distance):
    return lax.ppermute(rows, axis, [(i, i ^ distance) for i in range(lax.axis_size(axis))])


def is_high(axis, distance):
    return (lax.axis_index(axis) & distance) != 0


def swap_blocks(blocks):
    return lax.all_to_all(blocks, "expert", split_axis=0, concat_axis=0, tiled=True)


def after(value, *earlier):
    return lax.optimization_barrier((value, *earlier))[0]


def start_gather(near):
    return [near] + [exchange(near, "dp", distance) for distance in distances("dp")]


def finish_gather(terms):
    near = terms[0]
    pieces = dict(zip([0] + distances("dp"), terms))
    for r in range(lax.axis_size("dp")):
        if r not in pieces:
            lowest = r & -r
            pieces[r] = exchange(pieces[r ^ lowest], "dp", lowest)
    block = place_pieces(lax.axis_index("dp"), [pieces[r] for r in range(len(pieces))])
    return block.reshape(-1, near.shape[-1])


def scatter_dp(rows):
    width = rows.shape[1]
    block = rows.reshape(lax.axis_size("dp"), -1, width)
    order = distances("dp")[::-1]
    for distance in order:
        halves = block.reshape(block.shape[0] // 2, 2, -1, width)
        high = is_high("dp", distance).astype(jnp.int32)
        keep = lax.dynamic_index_in_dim(halves, high, 1, keepdims=False)
        send = lax.dynamic_index_in_dim(halves, 1 - high, 1, keepdims=False)
        received = exchange(send.astype(bf16), "dp", distance)
        if distance != order[-1]:
            block = keep.astype(f32) + received.astype(f32)
    return keep, received


def finish_dp(terms):
    keep, received = terms
    return (keep.astype(f32) + received.astype(f32))[0].astype(bf16)


def join(parts):
    return parts[0] if len(parts) == 1 else jnp.concatenate(parts, axis=0)


def near_parts(rows):
    return swap_blocks(rows.reshape(lax.axis_size("expert"), -1, rows.shape[1]))


def gelu_and_slope(values):
    root = 0.7978845608028654
    square = values * values
    share = 0.5 + 0.5 * jnp.tanh(values * (root + root * 0.044715 * square))
    unit = values * share
    slope = share + 2.0 * unit * (1.0 - share) * (root + 3.0 * root * 0.044715 * square)
    return unit, slope


def body(
    inputs,
    cotangent,
    attn_gain,
    qkv_weight,
    out_weight,
    ffn_gain,
    router_weight,
    rel_bias,
    expert_in,
    expert_out,
    routes,
    positions,
    dropped,
    segment_ids,
    valid_mask,
    buckets,
):
    seq_count, seq_length, model_width = inputs.shape
    tokens = seq_count * seq_length
    bucket_count, head_count = rel_bias.shape
    head_dim = model_width // head_count
    experts = router_weight.shape[1]
    capacity = 5 * tokens // (4 * experts)
    slots = experts * capacity
    me = lax.axis_index("expert")

    width = STEP_HEADS * head_dim
    steps = head_count // STEP_HEADS
    groups = [(0, steps - 1), (steps - 1, 1)]
    small_at = 3 * (steps - 1) * width // LANES
    out_at = 3 * width // model_width

    bucket_windows = offset_windows(buckets, REACH)
    one_hot_windows = (bucket_windows[..., None] == jnp.arange(bucket_count, dtype=jnp.int32)).astype(f32)
    windows = jnp.einsum("gpb,bh->hgp", one_hot_windows, rel_bias, precision=HIGHEST)
    tiles = toeplitz_tiles(windows)
    all_masks = [mask_columns(segment_ids[seq], valid_mask[seq]) for seq in range(seq_count)]
    slot_index = jnp.where(
        dropped.reshape(tokens) == 1, slots, routes.reshape(tokens) * capacity + positions.reshape(tokens)
    )
    slot_row, live = slot_index.reshape(1, tokens), valid_mask.reshape(1, tokens)
    rows_in = inputs.reshape(tokens, model_width)
    top = cotangent.reshape(tokens, model_width)

    def send_slots(rows):
        return swap_blocks(rows.reshape(experts, capacity, model_width)).reshape(slots, model_width)

    near, rest = spread_shard(
        qkv_weight, out_weight, attn_gain, ffn_gain, router_weight, width, steps - 1, lax.axis_size("expert")
    )
    near = swap_blocks(near)
    bounds = [tile_bounds(segment_ids[seq]) for seq in range(seq_count)]
    near, rest, tiles = lax.optimization_barrier((near, rest, tiles))
    rest = swap_blocks(rest)
    filled_cotangent = fill_slots(slot_row, top, slots)
    terms = start_gather(near)
    terms, filled_cotangent, rest, all_masks, bounds = lax.optimization_barrier(
        (terms, filled_cotangent, rest, all_masks, bounds)
    )
    weights = [finish_gather(terms)]

    packs, lses, normeds = [], [], None
    mixes = [None] * seq_count
    for g, (first, many) in enumerate(groups):
        if g == 0:
            terms = start_gather(rest)
            weights[0], filled_cotangent = lax.optimization_barrier((weights[0], filled_cotangent))
            d_final_rows = send_slots(filled_cotangent)
        done = [
            attend_forward(
                normeds[seq] if g else rows_in[seq * seq_length : (seq + 1) * seq_length],
                weights[0],
                small_at,
                weights[g],
                *all_masks[seq],
                bounds[seq],
                tiles,
                mixes[seq],
                first,
                many,
                head_dim,
            )
            for seq in range(seq_count)
        ]
        packs.append([results[0] for results in done])
        mixes = [results[1] for results in done]
        lses.append([results[2] for results in done])
        if g == 0:
            normeds = [results[3] for results in done]
            terms, mixes, lses, packs, normeds = lax.optimization_barrier((terms, mixes, lses, packs, normeds))
            weights.append(finish_gather(terms))
    mixed = join(mixes)
    mixed, d_final_rows = lax.optimization_barrier((mixed, d_final_rows))
    mid_rows, filled = run_middle(mixed, weights[1], out_at, rows_in, weights[0], small_at, slot_row, slots)
    slot_rows = send_slots(filled)

    w_in, w_back = expert_in[0], expert_out[0]
    d_hidden = dot(after(d_final_rows, filled), w_back, NT).astype(bf16)
    held_packs = lax.optimization_barrier((packs, filled))[0]
    probs = [
        [
            attend_probs(
                held_packs[g][seq], lses[g][seq], *all_masks[seq], bounds[seq], tiles, first, head_dim
            )
            for seq in range(seq_count)
        ]
        for g, (first, many) in enumerate(groups)
    ]
    slot_rows, d_hidden, probs = lax.optimization_barrier((slot_rows, d_hidden, probs))
    d_rows, d_logits, gate = run_expert(me, slot_rows, w_in, weights[0], small_at, d_hidden, experts)
    d_returned = send_slots(d_rows)

    expert_parts, moe_rows, grad_router = expert_grads(
        gate, slot_rows, w_in, d_hidden, d_final_rows, w_back, d_logits, lax.axis_size("dp")
    )
    d_returned, moe_rows, expert_parts, grad_router = lax.optimization_barrier(
        (d_returned, moe_rows, expert_parts, grad_router)
    )
    expert_sums = lax.psum_scatter(expert_parts, "dp", scatter_dimension=0, tiled=True)
    d_mid, d_mixed, grad_gain_two = run_middle_back(
        d_returned, slot_row, mid_rows, weights[0], small_at, top, weights[1], out_at
    )
    moe_returned = send_slots(moe_rows)

    diagonals, all_parts = [], []
    terms = None
    for g, (first, many) in enumerate(groups):
        parts, diagonal = [], None
        for seq in range(seq_count):
            at = slice(seq * seq_length, (seq + 1) * seq_length)
            part, here = attend_backward(
                packs[g][seq], d_mixed[at], mixed[at], probs[g][seq], bounds[seq], 2 * REACH + 1, first, head_dim
            )
            parts.append(part)
            diagonal = here if diagonal is None else diagonal + here
        parts = join(parts)
        if g == 0:
            grads = run_dense_grads(mixed, d_mid, grad_router, grad_gain_two, join(normeds), parts)
            grads, parts, diagonal, moe_returned = lax.optimization_barrier((grads, parts, diagonal, moe_returned))
            terms = scatter_dp(grads)
        else:
            parts, diagonal, terms = lax.optimization_barrier((parts, diagonal, terms))
            half, parts = lax.optimization_barrier((finish_dp(terms), parts))
            waits = [near_parts(half)]
            terms = scatter_dp(dot(join(normeds), parts, TN).astype(bf16))
        diagonals.append(diagonal)
        all_parts.append(parts)
    held, moe_returned = lax.optimization_barrier((terms[0], moe_returned))
    terms = (held, terms[1])
    output, sums = run_output(moe_returned, slot_row, mid_rows, rows_in, live)
    all_parts, output, sums = lax.optimization_barrier((all_parts, output, sums))
    input_grad = run_first_back(rows_in, small_at, d_mid, all_parts, weights)
    input_grad, terms, waits = lax.optimization_barrier((input_grad, terms, waits))
    near_terms = list(waits)
    grad_expert_in, grad_expert_out = widen(expert_sums)
    grad_rel = jnp.einsum("hgp,gpb->bh", jnp.concatenate(diagonals, axis=0), one_hot_windows, precision=HIGHEST)

    tail = jnp.concatenate([grad_rel.reshape(-1), sums[0, :4]])
    tail_size = tail.shape[0]
    tail = jnp.pad(tail, (0, -tail_size % model_width)).reshape(-1, model_width)
    for distance in distances("dp")[::-1]:
        tail = tail + exchange(tail, "dp", distance)
    pieces = []
    for unused in range(3):
        pieces.append(tail.astype(bf16))
        tail = tail - pieces[-1].astype(f32)
    receivers = lax.axis_size("expert")
    half = finish_dp(terms).reshape(receivers, -1, 3 * width)
    own_rows = half.shape[1]
    half = jnp.concatenate([half] + [jnp.broadcast_to(piece[None], (receivers, *piece.shape)) for piece in pieces], axis=1)
    last_near, grad_expert_in, grad_expert_out = lax.optimization_barrier(
        (swap_blocks(half), grad_expert_in, grad_expert_out)
    )
    near_terms.append(last_near[:, :own_rows])
    tail = jnp.sum(last_near[:, own_rows:].astype(f32), axis=0).reshape(3, -1)
    tail = (tail[0] + tail[1]) + tail[2]
    grad_rel = tail[: bucket_count * head_count].reshape(bucket_count, head_count)
    totals = tail[bucket_count * head_count : tail_size]
    stats = jnp.sqrt(totals[:3] / (totals[3] * model_width))

    dense_out, last_qkv = [jnp.sum(block.astype(f32), axis=0) for block in near_terms]
    dense_qkv = [dense_out[:, model_width + LANES :], last_qkv]
    grad_parts = [total.reshape(-1, many, 3, width) for total, (first, many) in zip(dense_qkv, groups)]
    grad_qkv = jnp.concatenate(grad_parts, axis=1).transpose(0, 2, 1, 3).reshape(-1, 3 * model_width)
    grad_gain_one = jnp.sum(grad_qkv * qkv_weight.astype(f32), axis=1) / attn_gain.astype(f32)
    return (
        output.reshape(inputs.shape),
        input_grad.reshape(inputs.shape),
        grad_gain_one,
        grad_qkv,
        dense_out[:, :model_width],
        dense_out[:, model_width + 1],
        dense_out[:, model_width + SMALL_GAINS : model_width + SMALL_GAINS + experts],
        grad_rel,
        grad_expert_in[None],
        grad_expert_out[None],
        stats,
    )


def solution(mesh):
    in_specs = (
        P(("dp", "expert"), None, None),
        P(("dp", "expert"), None, None),
        P(("dp", "expert")),
        P(("dp", "expert"), None),
        P(("dp", "expert"), None),
        P(("dp", "expert")),
        P(("dp", "expert"), None),
        P(),
        P("expert", None, None),
        P("expert", None, None),
        P(("dp", "expert"), None),
        P(("dp", "expert"), None),
        P(("dp", "expert"), None),
        P(("dp", "expert"), None),
        P(("dp", "expert"), None),
        P(),
    )
    out_specs = (
        P(("dp", "expert"), None, None),
        P(("dp", "expert"), None, None),
        P(("dp", "expert")),
        P(("dp", "expert"), None),
        P(("dp", "expert"), None),
        P(("dp", "expert")),
        P(("dp", "expert"), None),
        P(),
        P("expert", None, "dp"),
        P("expert", "dp", None),
        P(),
    )
    return jax.shard_map(body, mesh=mesh, in_specs=in_specs, out_specs=out_specs, check_vma=False)
```
